32 devices in a mesh: cells: 16 (over z, y, core), genes: 2 (over x).
Axes of the slice: x: 2, y: 2, z: 4, core: 2. Of those that a mesh axis runs over, the one named last changes fastest.
Arguments:
- data: bfloat16 [16384, 2000], P('cells', 'genes'), may hold values from -6 to 6
- start: float32 [2000, 64], P('genes'), may hold values from -6 to 6
- link_dev: int32 [64, 8], P('cells'), may hold values from 0 to 15, all different within a row; in each aligned block of 4 rows (0 to 3, 4 to 7, ...) at most 4 rows name the same one
- link_slot: int32 [64, 8], P('cells'), may hold values from 0 to 3
- link_weight: int32 [64, 8], P('cells'), may hold values from 1 to 8
Outputs:
- loadings: float32 [2000, 64], P('genes')
- smoothed: bfloat16 [64, 16384], P('genes', 'cells')
The draws below stay inside these ranges and needn't reach their ends.
Inputs may be any that keep to these rules, and one draw needn't show every extreme that they name: `link_dev`: each row names 8 different devices; the tiles of one device name any one device in at most 4 links, and some device in exactly 4.
All inputs are finite; a program needn't handle non-finite values.
Results may differ from the reference program's by a relative error of at most 0.017.
Values may be sent and summed in bfloat16 or wider, within the bound.
No kernel may reach another device: no remote copies, remote signals or barrier semaphores. Data moves between devices by JAX's collectives and lax.ppermute only.
A program may use at most 64 MiB of HBM per device.

```python
import math
import jax
import jax.numpy as jnp
import numpy as np
from jax import lax

G = 2000
K = 64
NB = 8
TILES_DEV = 4
ITERS = 3
NT = 64
CELLS = 16384
CAP = 4
N_CELLS = 16


def touch_ends(result, own_key, smallest, largest):
    extent = result.shape
    place = [jax.random.randint(jax.random.fold_in(own_key, axis), (), 0, extent[axis]) for axis in range(len(extent))]
    result = result.at[tuple(place)].set(smallest)
    longest = extent.index(max(extent))
    place[longest] = (place[longest] + 1) % extent[longest]
    return result.at[tuple(place)].set(largest)


def block_scale(rng, shape, split, least, high):
    level, own = 1.0, jax.random.fold_in(rng, 6)
    for axis_at, shards_of in split:
        heights = jnp.exp(jax.random.uniform(jax.random.fold_in(own, axis_at), (shards_of,), jnp.float32, least / len(split), high / len(split)))
        level = level * jnp.repeat(heights, shape[axis_at] // shards_of).reshape([-1 if axis == axis_at else 1 for axis in range(len(shape))])
    return level


def routed_block(stream_key, own, number, rows, amount, top, limit, skew):
    order = jax.random.permutation(stream_key, amount)
    packed, common = load_shares(amount, rows * top, limit, skew, True), load_shares(amount, rows * top, limit, skew, False)
    places = jnp.arange(amount)

    def named(sizes, turn):
        used = int((sizes > 0).sum())
        fixed = max(1, used // 4)
        moved = fixed + (places - fixed + turn * (used - fixed)) % max(1, amount - fixed)
        return jnp.zeros((amount,), jnp.int32).at[order[jnp.where(places < fixed, places, moved)]].set(jnp.asarray(sizes, jnp.int32))

    sizes = jnp.where(number % 4 == 0, named(packed, number // 4), named(common, number - number // 4 - 1))
    mixed = jax.random.permutation(jax.random.fold_in(own, 3), amount)
    donor, sink = mixed[0:amount // 2 * 2:2], mixed[1:amount // 2 * 2:2]
    slack = jnp.minimum(sizes[donor] - 1, limit - sizes[sink]) // 2
    slack = jnp.where((donor == order[0]) | (sink == order[0]) | (sizes[sink] == 0), 0, jnp.maximum(slack, 0))
    moved = jax.random.randint(jax.random.fold_in(own, 4), (amount // 2,), 0, 1 << 20) % (slack + 1)
    sizes = sizes.at[donor].add(-moved).at[sink].add(moved)
    labels = jnp.searchsorted(jnp.cumsum(sizes), jnp.arange(rows * top), side="right").astype(jnp.int32)
    listing = labels.reshape(top, rows).T
    listing = listing[jax.random.permutation(jax.random.fold_in(own, 1), rows)]
    turn = jax.random.randint(jax.random.fold_in(own, 2), (rows, 1), 0, top)
    return jnp.take_along_axis(listing, (jnp.arange(top)[None, :] + turn) % top, axis=1)


def load_shares(number_of, total, reach, lean, full):
    weights = [(1 << 20) // math.isqrt(rank ** lean) + 1 for rank in range(1, number_of + 1)]
    largest = reach if full else min(reach, max(-(-total // number_of), total * weights[0] // sum(weights)))
    least = 1 if total - largest >= number_of - 1 else 0
    given, rest = [largest] + [least] * (number_of - 1), total - largest - least * (number_of - 1)
    while rest > 0:
        candidates = [i for i in range(1, number_of) if given[i] < largest] or [i for i in range(1, number_of) if given[i] < reach]
        pool, budget = sum([weights[i] for i in candidates]), rest
        for i in candidates:
            extra = min(reach - given[i], max(1, budget * weights[i] // pool), rest)
            given[i] = given[i] + extra
            rest = rest - extra
    return np.array(given)


def bell_draw(rng, shape, scale, most, cuts=(), held_as=jnp.bfloat16):
    drawn = scale * jax.random.normal(rng, shape, jnp.float32)
    if cuts:
        drawn = drawn * block_scale(rng, shape, cuts, -0.22, 0.18)
    return jnp.clip(drawn, -most, most).astype(held_as)


def setup_inputs(seed: int = 0) -> dict:
    splits = jax.random.split(jax.random.key(seed), 6)
    data = bell_draw(splits[0], (CELLS, G), 1.0, 6.0, ((0, 16), (1, 2)))
    start = bell_draw(splits[1], (G, K), 1.0, 6.0, ((0, 2),), jnp.float32)
    link_dev_keys = jax.random.split(jax.random.fold_in(splits[2], 1), NT // TILES_DEV)
    link_dev_turns = jax.random.permutation(jax.random.fold_in(splits[2], 3), NT // TILES_DEV)
    link_dev = jax.vmap(lambda own, number: routed_block(jax.random.fold_in(splits[2], 2), own, number, TILES_DEV, N_CELLS, NB, CAP, 2))(link_dev_keys, link_dev_turns).reshape((NT, NB))
    link_slot = touch_ends(jax.random.randint(splits[3], (NT, NB), 0, TILES_DEV), jax.random.fold_in(splits[3], 1), 0, TILES_DEV - 1).astype(jnp.int32)
    link_weight = touch_ends(jax.random.randint(splits[4], (NT, NB), 1, 9), jax.random.fold_in(splits[4], 1), 1, 8).astype(jnp.int32)
    return dict(data=data, start=start, link_dev=link_dev, link_slot=link_slot, link_weight=link_weight)


self_weight = 8.0

def reference(data, start, link_dev, link_slot, link_weight):
    tiles_total = link_dev.shape[0]
    tile_cells = data.shape[0] // tiles_total
    width = start.shape[1]
    genes_total = data.shape[1]
    target = (link_dev * TILES_DEV + link_slot).astype(jnp.int32)
    weight = link_weight.astype(jnp.float32)
    degree = self_weight + lax.optimization_barrier(jnp.sum(weight, axis=1))
    scale = degree[:, None, None]
    loadings = start
    second = jnp.zeros((data.shape[0], width), jnp.bfloat16)
    for step in range(ITERS):
        narrow = loadings.astype(jnp.bfloat16)
        scores = (jnp.dot(data.astype(jnp.float32), narrow.astype(jnp.float32), preferred_element_type=jnp.float32) / math.sqrt(genes_total)).astype(jnp.bfloat16)
        blocks = scores.reshape(tiles_total, tile_cells, width).astype(jnp.float32)
        total = self_weight * blocks
        for slot in range(NB):
            total = total + weight[:, slot][:, None, None] * blocks[target[:, slot]]
        first = lax.optimization_barrier((total / scale).astype(jnp.bfloat16)).astype(jnp.float32)
        spread = lax.optimization_barrier((self_weight * first / scale).astype(jnp.bfloat16)).astype(jnp.float32)
        pushed = self_weight * spread
        for slot in range(NB):
            pushed = pushed.at[target[:, slot]].add(weight[:, slot][:, None, None] * spread)
        second = pushed.astype(jnp.bfloat16).reshape(tiles_total * tile_cells, width)
        update = lax.dot_general(data.astype(jnp.float32), second.astype(jnp.float32), (((0,), (0,)), ((), ())), preferred_element_type=jnp.float32)
        gram = jnp.dot(update.T.astype(jnp.float32), update.astype(jnp.float32), precision=lax.Precision.HIGHEST, preferred_element_type=jnp.float32) / genes_total
        factor = jnp.linalg.cholesky(gram)
        loadings = lax.linalg.triangular_solve(factor, update, left_side=False, lower=True, transpose_a=True)
    return (loadings, second.T)
```

```python
import functools
import math

import jax
import jax.numpy as jnp
from jax import lax
from jax.experimental import pallas as pl
from jax.experimental.pallas import tpu as pltpu
from jax.sharding import PartitionSpec as P

ITERS = 3
LANES = 128

self_weight = 8.0
HIGHEST = lax.Precision.HIGHEST


def inverse_factor(gram):
    width = gram.shape[0]
    rows = lax.broadcasted_iota(jnp.int32, (width, width), 0)
    cols = lax.broadcasted_iota(jnp.int32, (width, width), 1)
    eye = (rows == cols).astype(jnp.float32)
    state = jnp.concatenate([eye, gram], axis=1)
    strips = [state[at : at + 8] for at in range(0, width, 8)]
    place = lax.broadcasted_iota(jnp.int32, (8, 2 * width), 0)
    for k in range(width - 1):
        own, within = divmod(k, 8)
        row = strips[own][within : within + 1]
        scaled = row / row[:, width + k : width + k + 1]
        for strip in range(own, width // 8):
            factor = strips[strip][:, width + k : width + k + 1]
            if strip == own:
                factor = jnp.where(place > within, factor, 0.0)
            strips[strip] = strips[strip] - factor * scaled
    state = jnp.concatenate(strips, axis=0)
    pivots = jnp.sum(eye * state[:, width:], axis=1, keepdims=True)
    return state[:, :width] * lax.rsqrt(pivots)


def link_matrix(packed, tiles, neighbours, slots, rows_of):
    own_dev, own_slot, own_weight = packed[:, 0:1], packed[:, 1:2], packed[:, 2:3]
    target = own_dev * slots + own_slot
    lane = lax.broadcasted_iota(jnp.int32, (tiles * neighbours, tiles), 1).astype(jnp.float32)
    hits = jnp.where(lane == target, own_weight, 0.0)
    weights = jnp.sum(hits.reshape(tiles, neighbours, tiles), axis=1)
    tile_row = lax.broadcasted_iota(jnp.int32, (tiles, tiles), 0)
    tile_col = lax.broadcasted_iota(jnp.int32, (tiles, tiles), 1)
    weights = weights + jnp.where(tile_row == tile_col, self_weight, 0.0)
    cells = tiles * rows_of
    tile_of = lax.broadcasted_iota(jnp.int32, (cells, tiles), 0) // rows_of
    expand = (tile_of == lax.broadcasted_iota(jnp.int32, (cells, tiles), 1)).astype(jnp.bfloat16)
    tall = jnp.dot(expand, weights.astype(jnp.bfloat16), preferred_element_type=jnp.float32)
    full = lax.dot_general(
        tall.astype(jnp.bfloat16),
        expand,
        (((1,), (1,)), ((), ())),
        preferred_element_type=jnp.float32,
    )
    same = (
        lax.broadcasted_iota(jnp.int32, (cells, cells), 0) % rows_of
        == lax.broadcasted_iota(jnp.int32, (cells, cells), 1) % rows_of
    )
    full = jnp.where(same, full, 0.0).astype(jnp.bfloat16)
    ones = jnp.ones((8, cells), jnp.bfloat16)
    degree = lax.dot_general(
        ones, full, (((1,), (1,)), ((), ())), preferred_element_type=jnp.float32
    )
    return full, degree


def diffuse(scores, links, degree):
    scores = scores.astype(jnp.bfloat16)
    total = lax.dot_general(
        scores, links, (((1,), (1,)), ((), ())), preferred_element_type=jnp.float32
    )
    first = (total / degree).astype(jnp.bfloat16).astype(jnp.float32)
    spread = (self_weight * first / degree).astype(jnp.bfloat16)
    return jnp.dot(spread, links, preferred_element_type=jnp.float32).astype(jnp.bfloat16)


def block(data_ref, group):
    part = data_ref[:, group]
    return part.reshape(part.shape[0] * part.shape[1], part.shape[2])


def push_update(genes_here, data_ref, second, out_ref):
    groups, padded = data_ref.shape[1], data_ref.shape[3]
    chunk = out_ref.shape[1]
    halves = second.shape[0] // chunk
    blocks = padded // LANES
    for group in range(groups):
        update = jnp.dot(second, block(data_ref, group), preferred_element_type=jnp.float32)
        lane = lax.broadcasted_iota(jnp.int32, update.shape, 1)
        update = jnp.where(lane < genes_here, update, 0.0).astype(jnp.bfloat16)
        for at in range(blocks):
            for half in range(halves):
                out_ref[(group * blocks + at) * halves + half] = update[
                    half * chunk : (half + 1) * chunk, at * LANES : (at + 1) * LANES
                ]


def pull_update(chunks_ref, update_ref):
    groups, width, padded = update_ref.shape
    chunk = chunks_ref.shape[1]
    halves = width // chunk
    blocks = padded // LANES
    for group in range(groups):
        for at in range(blocks):
            for half in range(halves):
                update_ref[
                    group, half * chunk : (half + 1) * chunk, at * LANES : (at + 1) * LANES
                ] = chunks_ref[(group * blocks + at) * halves + half]


def gram_of(update_ref, genes_total):
    gram = None
    for group in range(update_ref.shape[0]):
        update = update_ref[group]
        part = lax.dot_general(
            update, update, (((1,), (1,)), ((), ())), preferred_element_type=jnp.float32
        )
        gram = part if gram is None else gram + part
    return gram / genes_total


def first_kernel(
    genes_here, slots, neighbours, own_ref, data_ref, start_ref, out_ref, links_ref, degree_ref
):
    devices, groups, rows, padded = data_ref.shape
    tiles = devices * slots
    packed = data_ref[:, 0][:, : slots * neighbours, padded - LANES :].astype(jnp.float32)
    packed = packed.reshape(tiles * neighbours, LANES)
    offset = genes_here - (padded - LANES)
    links, degree = link_matrix(
        packed[:, offset : offset + 3], tiles, neighbours, slots, rows // slots
    )
    links_ref[...] = links
    degree_ref[...] = degree
    scores = None
    for shift in range(groups):
        group = lax.rem(own_ref[0] + groups - shift, groups)
        part = lax.dot_general(
            start_ref[shift],
            block(data_ref, group),
            (((1,), (1,)), ((), ())),
            preferred_element_type=jnp.float32,
        )
        scores = part if scores is None else scores + part
    scores = scores / math.sqrt(genes_here * groups)
    push_update(genes_here, data_ref, diffuse(scores, links, degree[:1]), out_ref)


def next_kernel(
    genes_here, chunks_ref, data_ref, links_ref, degree_ref, out_ref, second_ref, update_ref
):
    groups = data_ref.shape[1]
    genes_total = genes_here * groups
    pull_update(chunks_ref, update_ref)
    inverse = inverse_factor(gram_of(update_ref, genes_total))
    scores = None
    for group in range(groups):
        part = lax.dot_general(
            update_ref[group],
            block(data_ref, group),
            (((1,), (1,)), ((), ())),
            preferred_element_type=jnp.float32,
        )
        scores = part if scores is None else scores + part
    scores = jnp.dot(
        inverse, scores, precision=HIGHEST, preferred_element_type=jnp.float32
    ) / math.sqrt(genes_total)
    second = diffuse(scores, links_ref[...], degree_ref[:1])
    second_ref[...] = second
    push_update(genes_here, data_ref, second, out_ref)


def last_kernel(genes_here, own_ref, chunks_ref, out_ref, update_ref):
    pull_update(chunks_ref, update_ref)
    genes_total = genes_here * update_ref.shape[0]
    inverse = inverse_factor(gram_of(update_ref, genes_total))
    mine = update_ref[own_ref[0]].astype(jnp.float32)
    loadings = jnp.dot(inverse, mine, precision=HIGHEST, preferred_element_type=jnp.float32)
    out_ref[...] = loadings.T[:genes_here]


def sum_kernel(chunks_ref, out_ref):
    total = jnp.sum(chunks_ref[...].astype(jnp.float32), axis=0).astype(jnp.bfloat16)
    out_ref[...] = jnp.broadcast_to(total[None], out_ref.shape)


def call(kernel, out_shape, scratch=(), scalars=0, arrays=0):
    in_specs = [pl.BlockSpec(memory_space=pltpu.SMEM)] * scalars
    in_specs += [pl.BlockSpec(memory_space=pltpu.VMEM)] * arrays
    return pl.pallas_call(
        kernel,
        out_shape=out_shape,
        in_specs=in_specs,
        out_specs=jax.tree.map(lambda _: pl.BlockSpec(memory_space=pltpu.VMEM), out_shape),
        scratch_shapes=list(scratch),
        compiler_params=pltpu.CompilerParams(vmem_limit_bytes=32 * 1024 * 1024),
    )


def by_cell(data, start, link_dev, link_slot, link_weight):
    axes = ("cells", "genes")
    devices, groups = lax.axis_size("cells"), lax.axis_size("genes")
    parts = devices * groups
    slots, neighbours = link_dev.shape
    genes_here, width = data.shape[1], start.shape[1]
    tile_cells = data.shape[0] // slots
    rows_of = tile_cells // parts
    rows = slots * rows_of
    padded = -(-genes_here // LANES) * LANES
    cells = devices * rows
    chunk = groups * width * padded // (parts * LANES)
    own = lax.axis_index("genes").astype(jnp.int32).reshape(1)

    packed = jnp.stack([link_dev, link_slot, link_weight], axis=-1).astype(jnp.bfloat16)
    packed = packed.reshape(slots * neighbours, 3)
    packed = jnp.pad(packed, ((0, rows - slots * neighbours), (0, padded - genes_here - 3)))
    moved = data.reshape(slots, parts, rows_of, genes_here).transpose(1, 0, 2, 3)
    moved = moved.reshape(parts, rows, genes_here)
    moved = jnp.concatenate(
        [moved, jnp.broadcast_to(packed[None], (parts, rows, padded - genes_here))], axis=2
    )
    moved = lax.all_to_all(moved, axes, 0, 0, tiled=True).reshape(devices, groups, rows, padded)
    narrow = jnp.pad(start.astype(jnp.bfloat16).T, ((0, 0), (0, padded - genes_here)))
    starts = [narrow]
    for shift in range(1, groups):
        pairs = [(at, (at + shift) % groups) for at in range(groups)]
        starts.append(lax.ppermute(narrow, "genes", pairs))
    starts = jnp.stack(starts)

    chunks = jax.ShapeDtypeStruct((parts, chunk, LANES), jnp.bfloat16)
    update = pltpu.VMEM((groups, width, padded), jnp.bfloat16)
    links = jax.ShapeDtypeStruct((cells, cells), jnp.bfloat16)
    degree = jax.ShapeDtypeStruct((8, cells), jnp.float32)
    second = jax.ShapeDtypeStruct((width, cells), jnp.bfloat16)

    def everywhere(pushed):
        summed = call(sum_kernel, chunks, arrays=1)(
            lax.all_to_all(pushed, axes, 0, 0, tiled=True)
        )
        return lax.all_to_all(summed, axes, 0, 0, tiled=True)

    pushed, links, degree = call(
        functools.partial(first_kernel, genes_here, slots, neighbours),
        (chunks, links, degree),
        scalars=1,
        arrays=2,
    )(own, moved, starts)
    for step in range(1, ITERS):
        pushed, diffused = call(
            functools.partial(next_kernel, genes_here), (chunks, second), (update,), arrays=4
        )(everywhere(pushed), moved, links, degree)
    loadings = call(
        functools.partial(last_kernel, genes_here),
        jax.ShapeDtypeStruct((genes_here, width), jnp.float32),
        (update,),
        scalars=1,
        arrays=1,
    )(own, everywhere(pushed))

    part_width = width // groups
    smoothed = diffused.reshape(groups, part_width, devices, rows).transpose(2, 0, 1, 3)
    smoothed = lax.all_to_all(
        smoothed.reshape(parts, part_width, rows), axes, 0, 0, tiled=True
    )
    smoothed = smoothed.reshape(parts, part_width, slots, rows_of).transpose(1, 2, 0, 3)
    return loadings, smoothed.reshape(part_width, slots * tile_cells)


def by_tile(data, start, link_dev, link_slot, link_weight):
    devices = lax.axis_size("cells")
    groups = lax.axis_size("genes")
    tiles_here, neighbours = link_dev.shape
    tile_cells = data.shape[0] // tiles_here
    genes_total = data.shape[1] * groups
    width = start.shape[1]
    part_width = width // groups
    capacity = max(2, 2 * tiles_here * neighbours // devices)
    slot_count = devices * capacity
    links = tiles_here * neighbours
    columns = part_width * tile_cells
    flat_dev = link_dev.reshape(links)
    flat_slot = link_slot.reshape(links)
    flat_weight = link_weight.reshape(links)
    dev_hits = (flat_dev[:, None] == jnp.arange(devices, dtype=jnp.int32)[None, :]).astype(
        jnp.int32
    )
    earlier = jnp.cumsum(dev_hits, axis=0) - dev_hits
    ranking = jnp.sum(earlier * dev_hits, axis=1)
    position = flat_dev * capacity + ranking
    placed = (position[:, None] == jnp.arange(slot_count, dtype=jnp.int32)[None, :]).astype(
        jnp.int32
    )
    wanted = jnp.sum(placed * (flat_slot + 1)[:, None], axis=0).reshape(devices, capacity)
    wanted_weight = jnp.sum(placed * flat_weight[:, None], axis=0).reshape(devices, capacity)
    asked_pair = (
        lax.all_to_all(wanted, "cells", split_axis=0, concat_axis=0, tiled=True),
        lax.all_to_all(wanted_weight, "cells", split_axis=0, concat_axis=0, tiled=True),
    )
    asked = asked_pair[0].reshape(slot_count)
    asked_weight = asked_pair[1].reshape(slot_count)
    tile_ids = jnp.arange(tiles_here, dtype=jnp.int32)
    serve_match = ((asked - 1)[:, None] == tile_ids[None, :]).astype(jnp.int32)
    serve = serve_match.astype(jnp.bfloat16)
    collect = (serve_match * asked_weight[:, None]).T.astype(jnp.bfloat16)
    placed_tiles = placed.reshape(tiles_here, neighbours, slot_count)
    link_matrix = jnp.sum(placed_tiles * link_weight[:, :, None], axis=1).astype(jnp.bfloat16)
    sender = jnp.sum(placed_tiles, axis=1).astype(jnp.bfloat16)
    degree = (self_weight + jnp.sum(link_weight, axis=1).astype(jnp.float32))[:, None]
    loadings = start
    smoothed = jnp.zeros((part_width, tiles_here * tile_cells), jnp.bfloat16)
    for step in range(ITERS):
        narrow = loadings.astype(jnp.bfloat16)
        partial_scores = lax.dot_general(
            narrow, data, (((0,), (1,)), ((), ())), preferred_element_type=jnp.float32
        )
        summed = lax.psum(partial_scores.astype(jnp.bfloat16), "genes").astype(jnp.float32)
        mine = lax.dynamic_slice_in_dim(summed, lax.axis_index("genes") * part_width, part_width, 0)
        scores = (mine / math.sqrt(genes_total)).astype(jnp.bfloat16)
        tiles = (
            scores.reshape(part_width, tiles_here, tile_cells)
            .transpose(1, 0, 2)
            .reshape(tiles_here, columns)
        )
        outgoing = jnp.dot(serve, tiles, preferred_element_type=jnp.float32).astype(jnp.bfloat16)
        linked = jnp.dot(
            link_matrix,
            lax.all_to_all(
                outgoing.reshape(devices, capacity, columns),
                "cells",
                split_axis=0,
                concat_axis=0,
                tiled=True,
            ).reshape(slot_count, -1),
            preferred_element_type=jnp.float32,
        )
        first = lax.optimization_barrier(
            ((self_weight * tiles.astype(jnp.float32) + linked) / degree).astype(jnp.bfloat16)
        )
        spread = lax.optimization_barrier(
            (self_weight * first.astype(jnp.float32) / degree).astype(jnp.bfloat16)
        )
        returning = lax.dot_general(
            sender, spread, (((0,), (0,)), ((), ())), preferred_element_type=jnp.float32
        ).astype(jnp.bfloat16)
        pushed = jnp.dot(
            collect,
            lax.all_to_all(
                returning.reshape(devices, capacity, columns),
                "cells",
                split_axis=0,
                concat_axis=0,
                tiled=True,
            ).reshape(slot_count, -1),
            preferred_element_type=jnp.float32,
        )
        second = (self_weight * spread.astype(jnp.float32) + pushed).astype(jnp.bfloat16)
        smoothed = (
            second.reshape(tiles_here, part_width, tile_cells)
            .transpose(1, 0, 2)
            .reshape(part_width, tiles_here * tile_cells)
        )
        update = lax.dot_general(
            data,
            lax.all_gather(smoothed, "genes", axis=0, tiled=True),
            (((0,), (1,)), ((), ())),
            preferred_element_type=jnp.float32,
        )
        update = lax.psum(update, "cells")
        gram_part = jnp.dot(
            update.T, update, precision=lax.Precision.HIGHEST, preferred_element_type=jnp.float32
        )
        gram = lax.psum(gram_part, "genes") / genes_total
        factor = jnp.linalg.cholesky(gram)
        loadings = lax.linalg.triangular_solve(
            factor, update, left_side=False, lower=True, transpose_a=True
        )
    return (loadings, smoothed)


def per_device(data, start, link_dev, link_slot, link_weight):
    parts = lax.axis_size("cells") * lax.axis_size("genes")
    slots, neighbours = link_dev.shape
    tile_cells = data.shape[0] // slots
    genes_here, width = data.shape[1], start.shape[1]
    padded = -(-genes_here // LANES) * LANES
    rows = slots * tile_cells // parts
    fits = (
        tile_cells % (8 * parts) == 0
        and rows % 16 == 0
        and rows >= slots * neighbours
        and slots * neighbours % 16 == 0
        and padded - genes_here >= 3
        and width * padded * lax.axis_size("genes") % (parts * LANES * 16) == 0
    )
    way = by_cell if fits else by_tile
    return way(data, start, link_dev, link_slot, link_weight)


def solution(mesh):
    placed = (
        P("cells", "genes"),
        P("genes", None),
        P("cells", None),
        P("cells", None),
        P("cells", None),
    )
    return jax.shard_map(
        per_device,
        mesh=mesh,
        in_specs=placed,
        out_specs=(P("genes", None), P("genes", "cells")),
        check_vma=False,
    )
```

```python
import functools
import math

import jax
import jax.numpy as jnp
from jax import lax
from jax.experimental import pallas as pl
from jax.experimental.pallas import tpu as pltpu
from jax.sharding import PartitionSpec as P

ITERS = 3
LANES = 128

self_weight = 8.0
HIGHEST = lax.Precision.HIGHEST


def inverse_factor(gram):
    width = gram.shape[0]
    rows = lax.broadcasted_iota(jnp.int32, (width, width), 0)
    cols = lax.broadcasted_iota(jnp.int32, (width, width), 1)
    eye = (rows == cols).astype(jnp.float32)
    state = jnp.concatenate([eye, gram], axis=1)
    strips = [state[at : at + 8] for at in range(0, width, 8)]
    place = lax.broadcasted_iota(jnp.int32, (8, 2 * width), 0)
    for k in range(width - 1):
        own, within = divmod(k, 8)
        row = strips[own][within : within + 1]
        scaled = row / row[:, width + k : width + k + 1]
        for strip in range(own, width // 8):
            factor = strips[strip][:, width + k : width + k + 1]
            if strip == own:
                factor = jnp.where(place > within, factor, 0.0)
            strips[strip] = strips[strip] - factor * scaled
    state = jnp.concatenate(strips, axis=0)
    pivots = jnp.sum(eye * state[:, width:], axis=1, keepdims=True)
    return state[:, :width] * lax.rsqrt(pivots)


def link_matrix(packed, tiles, neighbours, slots, rows_of):
    own_dev, own_slot, own_weight = packed[:, 0:1], packed[:, 1:2], packed[:, 2:3]
    target = own_dev * slots + own_slot
    lane = lax.broadcasted_iota(jnp.int32, (tiles * neighbours, tiles), 1).astype(jnp.float32)
    hits = jnp.where(lane == target, own_weight, 0.0)
    weights = jnp.sum(hits.reshape(tiles, neighbours, tiles), axis=1)
    tile_row = lax.broadcasted_iota(jnp.int32, (tiles, tiles), 0)
    tile_col = lax.broadcasted_iota(jnp.int32, (tiles, tiles), 1)
    weights = weights + jnp.where(tile_row == tile_col, self_weight, 0.0)
    cells = tiles * rows_of
    tile_of = lax.broadcasted_iota(jnp.int32, (cells, tiles), 0) // rows_of
    expand = (tile_of == lax.broadcasted_iota(jnp.int32, (cells, tiles), 1)).astype(jnp.bfloat16)
    tall = jnp.dot(expand, weights.astype(jnp.bfloat16), preferred_element_type=jnp.float32)
    full = lax.dot_general(
        tall.astype(jnp.bfloat16),
        expand,
        (((1,), (1,)), ((), ())),
        preferred_element_type=jnp.float32,
    )
    same = (
        lax.broadcasted_iota(jnp.int32, (cells, cells), 0) % rows_of
        == lax.broadcasted_iota(jnp.int32, (cells, cells), 1) % rows_of
    )
    full = jnp.where(same, full, 0.0).astype(jnp.bfloat16)
    ones = jnp.ones((8, cells), jnp.bfloat16)
    degree = lax.dot_general(
        ones, full, (((1,), (1,)), ((), ())), preferred_element_type=jnp.float32
    )
    return full, degree


def diffuse(scores, links, degree):
    scores = scores.astype(jnp.bfloat16)
    total = lax.dot_general(
        scores, links, (((1,), (1,)), ((), ())), preferred_element_type=jnp.float32
    )
    first = (total / degree).astype(jnp.bfloat16).astype(jnp.float32)
    spread = (self_weight * first / degree).astype(jnp.bfloat16)
    return jnp.dot(spread, links, preferred_element_type=jnp.float32).astype(jnp.bfloat16)


def block(data_ref, group):
    part = data_ref[:, group]
    return part.reshape(part.shape[0] * part.shape[1], part.shape[2])


def push_update(genes_here, data_ref, second, out_ref, chunk):
    groups, padded = data_ref.shape[1], data_ref.shape[3]
    halves = second.shape[0] // chunk
    blocks = padded // LANES
    for group in range(groups):
        update = jnp.dot(second, block(data_ref, group), preferred_element_type=jnp.float32)
        lane = lax.broadcasted_iota(jnp.int32, update.shape, 1)
        update = jnp.where(lane < genes_here, update, 0.0).astype(jnp.bfloat16)
        for at in range(blocks):
            for half in range(halves):
                out_ref[(group * blocks + at) * halves + half, :chunk] = update[
                    half * chunk : (half + 1) * chunk, at * LANES : (at + 1) * LANES
                ]


def pull_update(chunks_ref, update_ref):
    groups, width, padded = update_ref.shape
    chunk = chunks_ref.shape[1]
    halves = width // chunk
    blocks = padded // LANES
    for group in range(groups):
        for at in range(blocks):
            for half in range(halves):
                update_ref[
                    group, half * chunk : (half + 1) * chunk, at * LANES : (at + 1) * LANES
                ] = chunks_ref[(group * blocks + at) * halves + half]


def gram_of(update_ref, genes_total):
    gram = None
    for group in range(update_ref.shape[0]):
        update = update_ref[group]
        part = lax.dot_general(
            update, update, (((1,), (1,)), ((), ())), preferred_element_type=jnp.float32
        )
        gram = part if gram is None else gram + part
    return gram / genes_total


def regroup_kernel(rows_of, data_ref, links_ref, out_ref):
    genes_here = data_ref.shape[0]
    parts, rows, padded = out_ref.shape
    tile_cells = parts * rows_of
    joined = max(1, 16 // rows_of)
    span, share = joined * tile_cells, joined * rows_of
    to = lax.broadcasted_iota(jnp.int32, (span, span), 0)
    at = lax.broadcasted_iota(jnp.int32, (span, span), 1)
    source = (to % share // rows_of) * tile_cells + to // share * rows_of + to % rows_of
    order = (source == at).astype(jnp.bfloat16)
    whole = padded - LANES

    def moved(part):
        taken = lax.dot_general(
            order, part, (((1,), (1,)), ((), ())), preferred_element_type=jnp.float32
        )
        return taken.astype(jnp.bfloat16).reshape(parts, share, part.shape[0])

    for turn in range(rows // share):
        cells = slice(turn * span, (turn + 1) * span)
        keep = slice(turn * share, (turn + 1) * share)
        out_ref[:, keep, :whole] = moved(data_ref[:whole, cells])
        rest = data_ref[whole:genes_here, cells].astype(jnp.float32)
        rest = jnp.concatenate([rest, links_ref[:, cells]], axis=0)
        out_ref[:, keep, whole:] = moved(rest.astype(jnp.bfloat16))


def share_second(second, out_ref, chunk, groups):
    width, cells = second.shape
    rows = cells * groups // out_ref.shape[0]
    tall = out_ref.shape[1] - chunk
    slabs = width // groups // tall
    lane = lax.broadcasted_iota(jnp.int32, (tall, LANES), 1)
    for at in range(cells // LANES):
        wide = second[:, at * LANES : (at + 1) * LANES].astype(jnp.float32)
        for group in range(groups):
            for device in range(LANES // rows):
                share = jnp.zeros((tall, LANES), jnp.float32)
                for slab in range(slabs):
                    first_row = (group * slabs + slab) * tall
                    turned = pltpu.roll(
                        wide[first_row : first_row + tall],
                        (slab - device) * rows % LANES,
                        1,
                    )
                    share = jnp.where(lane // rows == slab, turned, share)
                to = (at * (LANES // rows) + device) * groups + group
                out_ref[to, chunk:] = share.astype(jnp.bfloat16)


def first_kernel(
    genes_here, slots, own_ref, data_ref, start_ref, out_ref, links_ref, degree_ref
):
    devices, groups, rows, padded = data_ref.shape
    tiles = devices * slots
    packed = block(data_ref, 0)[:, padded - LANES :].astype(jnp.float32)
    offset = genes_here - (padded - LANES)
    links, degree = link_matrix(
        packed[:, offset : offset + 3], tiles, rows // slots, slots, rows // slots
    )
    links_ref[...] = links
    degree_ref[...] = degree
    scores = None
    for shift in range(groups):
        group = lax.rem(own_ref[0] + groups - shift, groups)
        part = lax.dot_general(
            start_ref[shift],
            block(data_ref, group),
            (((1,), (1,)), ((), ())),
            preferred_element_type=jnp.float32,
        )
        scores = part if scores is None else scores + part
    scores = scores / math.sqrt(genes_here * groups)
    second = diffuse(scores, links, degree[:1])
    push_update(genes_here, data_ref, second, out_ref, out_ref.shape[1])


def next_kernel(genes_here, chunks_ref, data_ref, links_ref, degree_ref, out_ref, update_ref):
    chunk = chunks_ref.shape[1]
    groups = data_ref.shape[1]
    genes_total = genes_here * groups
    pull_update(chunks_ref, update_ref)
    inverse = inverse_factor(gram_of(update_ref, genes_total))
    scores = None
    for group in range(groups):
        part = lax.dot_general(
            update_ref[group],
            block(data_ref, group),
            (((1,), (1,)), ((), ())),
            preferred_element_type=jnp.float32,
        )
        scores = part if scores is None else scores + part
    scores = jnp.dot(
        inverse, scores, precision=HIGHEST, preferred_element_type=jnp.float32
    ) / math.sqrt(genes_total)
    second = diffuse(scores, links_ref[...], degree_ref[:1])
    push_update(genes_here, data_ref, second, out_ref, chunk)
    if out_ref.shape[1] > chunk:
        share_second(second, out_ref, chunk, groups)


def last_kernel(genes_here, own_ref, chunks_ref, out_ref, update_ref):
    pull_update(chunks_ref, update_ref)
    genes_total = genes_here * update_ref.shape[0]
    inverse = inverse_factor(gram_of(update_ref, genes_total))
    mine = update_ref[own_ref[0]].astype(jnp.float32)
    loadings = jnp.dot(inverse, mine, precision=HIGHEST, preferred_element_type=jnp.float32)
    out_ref[...] = loadings[:, :genes_here]


def sum_kernel(chunks_ref, out_ref):
    parts = chunks_ref[:, : out_ref.shape[1]].astype(jnp.float32)
    total = jnp.sum(parts, axis=0).astype(jnp.bfloat16)
    out_ref[...] = jnp.broadcast_to(total[None], out_ref.shape)


def call(kernel, out_shape, scratch=(), scalars=0, arrays=0):
    in_specs = [pl.BlockSpec(memory_space=pltpu.SMEM)] * scalars
    in_specs += [pl.BlockSpec(memory_space=pltpu.VMEM)] * arrays
    return pl.pallas_call(
        kernel,
        out_shape=out_shape,
        in_specs=in_specs,
        out_specs=jax.tree.map(lambda _: pl.BlockSpec(memory_space=pltpu.VMEM), out_shape),
        scratch_shapes=list(scratch),
        compiler_params=pltpu.CompilerParams(vmem_limit_bytes=32 * 1024 * 1024),
    )


def by_cell(data, start, link_dev, link_slot, link_weight):
    axes = ("cells", "genes")
    devices, groups = lax.axis_size("cells"), lax.axis_size("genes")
    parts = devices * groups
    slots, neighbours = link_dev.shape
    genes_here, width = data.shape[1], start.shape[1]
    tile_cells = data.shape[0] // slots
    rows_of = tile_cells // parts
    rows = slots * rows_of
    padded = -(-genes_here // LANES) * LANES
    cells = devices * rows
    chunk = groups * width * padded // (parts * LANES)
    own = lax.axis_index("genes").astype(jnp.int32).reshape(1)

    links = jnp.stack([link_dev, link_slot, link_weight]).astype(jnp.float32)
    links = jnp.pad(links, ((0, padded - genes_here - 3), (0, 0), (0, rows_of - neighbours)))
    links = jnp.broadcast_to(links[:, :, None], (links.shape[0], slots, parts, rows_of))
    links = links.reshape(links.shape[0], slots * tile_cells)
    moved = call(
        functools.partial(regroup_kernel, rows_of),
        jax.ShapeDtypeStruct((parts, rows, padded), jnp.bfloat16),
        arrays=2,
    )(data.T, links)
    moved = lax.all_to_all(moved, axes, 0, 0, tiled=True).reshape(devices, groups, rows, padded)
    narrow = jnp.pad(start.astype(jnp.bfloat16).T, ((0, 0), (0, padded - genes_here)))
    starts = [narrow]
    for shift in range(1, groups):
        pairs = [(at, (at + shift) % groups) for at in range(groups)]
        starts.append(lax.ppermute(narrow, "genes", pairs))
    starts = jnp.stack(starts)

    chunks = jax.ShapeDtypeStruct((parts, chunk, LANES), jnp.bfloat16)
    update = pltpu.VMEM((groups, width, padded), jnp.bfloat16)
    links = jax.ShapeDtypeStruct((cells, cells), jnp.bfloat16)
    degree = jax.ShapeDtypeStruct((8, cells), jnp.float32)
    extra = jax.ShapeDtypeStruct((parts, chunk + 16, LANES), jnp.bfloat16)

    def gather(arrived):
        summed = call(sum_kernel, chunks, arrays=1)(arrived)
        return lax.all_to_all(summed, axes, 0, 0, tiled=True)

    pushed, links, degree = call(
        functools.partial(first_kernel, genes_here, slots),
        (chunks, links, degree),
        scalars=1,
        arrays=2,
    )(own, moved, starts)
    arrived = lax.all_to_all(pushed, axes, 0, 0, tiled=True)
    for step in range(1, ITERS):
        pushed = call(
            functools.partial(next_kernel, genes_here),
            extra if step == ITERS - 1 else chunks,
            (update,),
            arrays=4,
        )(gather(arrived), moved, links, degree)
        arrived = lax.all_to_all(pushed, axes, 0, 0, tiled=True)
    loadings = call(
        functools.partial(last_kernel, genes_here),
        jax.ShapeDtypeStruct((width, genes_here), jnp.float32),
        (update,),
        scalars=1,
        arrays=1,
    )(own, gather(arrived))

    part_width = width // groups
    slabs = part_width // 16
    smoothed = arrived[:, chunk:, : slabs * rows].reshape(parts, 16, slabs, slots, rows_of)
    smoothed = smoothed.transpose(2, 1, 3, 0, 4)
    return loadings.T, smoothed.reshape(part_width, slots * tile_cells)


def by_tile(data, start, link_dev, link_slot, link_weight):
    devices = lax.axis_size("cells")
    groups = lax.axis_size("genes")
    tiles_here, neighbours = link_dev.shape
    tile_cells = data.shape[0] // tiles_here
    genes_total = data.shape[1] * groups
    width = start.shape[1]
    part_width = width // groups
    capacity = max(2, 2 * tiles_here * neighbours // devices)
    slot_count = devices * capacity
    links = tiles_here * neighbours
    columns = part_width * tile_cells
    flat_dev = link_dev.reshape(links)
    flat_slot = link_slot.reshape(links)
    flat_weight = link_weight.reshape(links)
    dev_hits = (flat_dev[:, None] == jnp.arange(devices, dtype=jnp.int32)[None, :]).astype(
        jnp.int32
    )
    earlier = jnp.cumsum(dev_hits, axis=0) - dev_hits
    ranking = jnp.sum(earlier * dev_hits, axis=1)
    position = flat_dev * capacity + ranking
    placed = (position[:, None] == jnp.arange(slot_count, dtype=jnp.int32)[None, :]).astype(
        jnp.int32
    )
    wanted = jnp.sum(placed * (flat_slot + 1)[:, None], axis=0).reshape(devices, capacity)
    wanted_weight = jnp.sum(placed * flat_weight[:, None], axis=0).reshape(devices, capacity)
    asked_pair = (
        lax.all_to_all(wanted, "cells", split_axis=0, concat_axis=0, tiled=True),
        lax.all_to_all(wanted_weight, "cells", split_axis=0, concat_axis=0, tiled=True),
    )
    asked = asked_pair[0].reshape(slot_count)
    asked_weight = asked_pair[1].reshape(slot_count)
    tile_ids = jnp.arange(tiles_here, dtype=jnp.int32)
    serve_match = ((asked - 1)[:, None] == tile_ids[None, :]).astype(jnp.int32)
    serve = serve_match.astype(jnp.bfloat16)
    collect = (serve_match * asked_weight[:, None]).T.astype(jnp.bfloat16)
    placed_tiles = placed.reshape(tiles_here, neighbours, slot_count)
    link_matrix = jnp.sum(placed_tiles * link_weight[:, :, None], axis=1).astype(jnp.bfloat16)
    sender = jnp.sum(placed_tiles, axis=1).astype(jnp.bfloat16)
    degree = (self_weight + jnp.sum(link_weight, axis=1).astype(jnp.float32))[:, None]
    loadings = start
    smoothed = jnp.zeros((part_width, tiles_here * tile_cells), jnp.bfloat16)
    for step in range(ITERS):
        narrow = loadings.astype(jnp.bfloat16)
        partial_scores = lax.dot_general(
            narrow, data, (((0,), (1,)), ((), ())), preferred_element_type=jnp.float32
        )
        summed = lax.psum(partial_scores.astype(jnp.bfloat16), "genes").astype(jnp.float32)
        mine = lax.dynamic_slice_in_dim(summed, lax.axis_index("genes") * part_width, part_width, 0)
        scores = (mine / math.sqrt(genes_total)).astype(jnp.bfloat16)
        tiles = (
            scores.reshape(part_width, tiles_here, tile_cells)
            .transpose(1, 0, 2)
            .reshape(tiles_here, columns)
        )
        outgoing = jnp.dot(serve, tiles, preferred_element_type=jnp.float32).astype(jnp.bfloat16)
        linked = jnp.dot(
            link_matrix,
            lax.all_to_all(
                outgoing.reshape(devices, capacity, columns),
                "cells",
                split_axis=0,
                concat_axis=0,
                tiled=True,
            ).reshape(slot_count, -1),
            preferred_element_type=jnp.float32,
        )
        first = lax.optimization_barrier(
            ((self_weight * tiles.astype(jnp.float32) + linked) / degree).astype(jnp.bfloat16)
        )
        spread = lax.optimization_barrier(
            (self_weight * first.astype(jnp.float32) / degree).astype(jnp.bfloat16)
        )
        returning = lax.dot_general(
            sender, spread, (((0,), (0,)), ((), ())), preferred_element_type=jnp.float32
        ).astype(jnp.bfloat16)
        pushed = jnp.dot(
            collect,
            lax.all_to_all(
                returning.reshape(devices, capacity, columns),
                "cells",
                split_axis=0,
                concat_axis=0,
                tiled=True,
            ).reshape(slot_count, -1),
            preferred_element_type=jnp.float32,
        )
        second = (self_weight * spread.astype(jnp.float32) + pushed).astype(jnp.bfloat16)
        smoothed = (
            second.reshape(tiles_here, part_width, tile_cells)
            .transpose(1, 0, 2)
            .reshape(part_width, tiles_here * tile_cells)
        )
        update = lax.dot_general(
            data,
            lax.all_gather(smoothed, "genes", axis=0, tiled=True),
            (((0,), (1,)), ((), ())),
            preferred_element_type=jnp.float32,
        )
        update = lax.psum(update, "cells")
        gram_part = jnp.dot(
            update.T, update, precision=lax.Precision.HIGHEST, preferred_element_type=jnp.float32
        )
        gram = lax.psum(gram_part, "genes") / genes_total
        factor = jnp.linalg.cholesky(gram)
        loadings = lax.linalg.triangular_solve(
            factor, update, left_side=False, lower=True, transpose_a=True
        )
    return (loadings, smoothed)


def per_device(data, start, link_dev, link_slot, link_weight):
    groups = lax.axis_size("genes")
    parts = lax.axis_size("cells") * groups
    slots, neighbours = link_dev.shape
    tile_cells = data.shape[0] // slots
    genes_here, width = data.shape[1], start.shape[1]
    padded = -(-genes_here // LANES) * LANES
    rows = slots * tile_cells // parts
    fits = (
        tile_cells % (8 * parts) == 0
        and neighbours <= tile_cells // parts
        and rows % 16 == 0
        and LANES % rows == 0
        and (genes_here - padded + LANES) % 8 == 0
        and padded - genes_here >= 3
        and width % (16 * groups) == 0
        and width // groups // 16 * rows <= LANES
        and width * padded * groups % (parts * LANES * 16) == 0
    )
    way = by_cell if fits else by_tile
    return way(data, start, link_dev, link_slot, link_weight)


def solution(mesh):
    placed = (
        P("cells", "genes"),
        P("genes", None),
        P("cells", None),
        P("cells", None),
        P("cells", None),
    )
    return jax.shard_map(
        per_device,
        mesh=mesh,
        in_specs=placed,
        out_specs=(P("genes", None), P("genes", "cells")),
        check_vma=False,
    )
```

```python
import functools
import math

import jax
import jax.numpy as jnp
from jax import lax
from jax.experimental import pallas as pl
from jax.experimental.pallas import tpu as pltpu
from jax.sharding import PartitionSpec as P

ITERS = 3
LANES = 128

self_weight = 8.0
HIGHEST = lax.Precision.HIGHEST


def inverse_factor(gram):
    width = gram.shape[0]
    rows = lax.broadcasted_iota(jnp.int32, (width, width), 0)
    cols = lax.broadcasted_iota(jnp.int32, (width, width), 1)
    diagonal = jnp.where(rows == cols, gram, 0.0)
    down = lax.rsqrt(jnp.sum(diagonal, axis=1, keepdims=True))
    along = lax.rsqrt(jnp.sum(diagonal, axis=0, keepdims=True))
    scaled = gram * down * along
    state = jnp.concatenate([jnp.where(rows == cols, along, 0.0), scaled], axis=1)
    strips = [state[at : at + 8] for at in range(0, width, 8)]
    shape = strips[0].shape
    place = lax.broadcasted_iota(jnp.int32, shape, 0)
    done = []
    for panel, strip in enumerate(strips):
        base = width + 8 * panel

        def column(of, j):
            return jnp.broadcast_to(of[:, base + j : base + j + 1], shape)

        columns = [column(strip, j) for j in range(8)]
        core = {
            (i, j): jnp.broadcast_to(columns[j][i : i + 1], shape)
            for j in range(8)
            for i in range(j, 8)
        }
        lines = [jnp.broadcast_to(strip[j : j + 1], shape) for j in range(8)]
        factor, solved = {}, [None] * 8
        for j in range(0, 8, 2):
            a, b, c = core[j, j], core[j + 1, j], core[j + 1, j + 1]
            inverse = 1.0 / (a * c - b * b)
            step = b * (1.0 / a)
            ia, ib, ic = c * inverse, b * inverse, a * inverse
            for i in range(j + 2, 8):
                factor[i, j] = core[i, j] * ia - core[i, j + 1] * ib
                factor[i, j + 1] = core[i, j + 1] * ic - core[i, j] * ib
            for i in range(j + 2, 8):
                for m in range(j + 2, i + 1):
                    core[i, m] -= factor[i, j] * core[m, j] + factor[i, j + 1] * core[m, j + 1]
                lines[i] -= factor[i, j] * lines[j] + factor[i, j + 1] * lines[j + 1]
            solved[j] = ia * lines[j] - ib * lines[j + 1]
            solved[j + 1] = ic * lines[j + 1] - ib * lines[j]
            lines[j + 1] -= step * lines[j]
            core[j + 1, j + 1] = c - step * b
        for j in reversed(range(0, 8, 2)):
            for i in range(j + 2, 8):
                solved[j] -= factor[i, j] * solved[i]
                solved[j + 1] -= factor[i, j + 1] * solved[i]
        for later in range(panel + 1, len(strips)):
            terms = [column(strips[later], j) * solved[j] for j in range(8)]
            while len(terms) > 1:
                terms = [terms[at] + terms[at + 1] for at in range(0, len(terms), 2)]
            strips[later] = strips[later] - terms[0]
        final = lines[0] * lax.rsqrt(core[0, 0])
        for j in range(1, 8):
            final = jnp.where(place == j, lines[j] * lax.rsqrt(core[j, j]), final)
        done.append(final)
    return jnp.concatenate(done, axis=0)[:, :width]


def link_matrix(packed, tiles, neighbours, slots, rows_of):
    own_dev, own_slot, own_weight = packed[:, 0:1], packed[:, 1:2], packed[:, 2:3]
    target = own_dev * slots + own_slot
    lane = lax.broadcasted_iota(jnp.int32, (tiles * neighbours, tiles), 1).astype(jnp.float32)
    hits = jnp.where(lane == target, own_weight, 0.0)
    weights = jnp.sum(hits.reshape(tiles, neighbours, tiles), axis=1)
    tile_row = lax.broadcasted_iota(jnp.int32, (tiles, tiles), 0)
    tile_col = lax.broadcasted_iota(jnp.int32, (tiles, tiles), 1)
    weights = weights + jnp.where(tile_row == tile_col, self_weight, 0.0)
    cells = tiles * rows_of
    tile_of = lax.broadcasted_iota(jnp.int32, (cells, tiles), 0) // rows_of
    expand = (tile_of == lax.broadcasted_iota(jnp.int32, (cells, tiles), 1)).astype(jnp.bfloat16)
    tall = jnp.dot(expand, weights.astype(jnp.bfloat16), preferred_element_type=jnp.float32)
    full = lax.dot_general(
        tall.astype(jnp.bfloat16),
        expand,
        (((1,), (1,)), ((), ())),
        preferred_element_type=jnp.float32,
    )
    same = (
        lax.broadcasted_iota(jnp.int32, (cells, cells), 0) % rows_of
        == lax.broadcasted_iota(jnp.int32, (cells, cells), 1) % rows_of
    )
    full = jnp.where(same, full, 0.0).astype(jnp.bfloat16)
    ones = jnp.ones((8, cells), jnp.bfloat16)
    degree = lax.dot_general(
        ones, full, (((1,), (1,)), ((), ())), preferred_element_type=jnp.float32
    )
    return full, degree


def diffuse(scores, links, degree):
    scores = scores.astype(jnp.bfloat16)
    total = lax.dot_general(
        scores, links, (((1,), (1,)), ((), ())), preferred_element_type=jnp.float32
    )
    first = (total / degree).astype(jnp.bfloat16).astype(jnp.float32)
    spread = (self_weight * first / degree).astype(jnp.bfloat16)
    return jnp.dot(spread, links, preferred_element_type=jnp.float32).astype(jnp.bfloat16)


def block(data_ref, group):
    part = data_ref[:, group]
    return part.reshape(part.shape[0] * part.shape[1], part.shape[2])


def push_update(genes_here, data_ref, second, out_ref, chunk):
    groups, padded = data_ref.shape[1], data_ref.shape[3]
    halves = second.shape[0] // chunk
    blocks = padded // LANES
    for group in range(groups):
        update = jnp.dot(second, block(data_ref, group), preferred_element_type=jnp.float32)
        lane = lax.broadcasted_iota(jnp.int32, update.shape, 1)
        update = jnp.where(lane < genes_here, update, 0.0).astype(jnp.bfloat16)
        for at in range(blocks):
            for half in range(halves):
                out_ref[(group * blocks + at) * halves + half, :chunk] = update[
                    half * chunk : (half + 1) * chunk, at * LANES : (at + 1) * LANES
                ]


def pull_update(chunks_ref, update_ref):
    groups, width, padded = update_ref.shape
    chunk = chunks_ref.shape[1]
    halves = width // chunk
    blocks = padded // LANES
    for group in range(groups):
        for at in range(blocks):
            for half in range(halves):
                update_ref[
                    group, half * chunk : (half + 1) * chunk, at * LANES : (at + 1) * LANES
                ] = chunks_ref[(group * blocks + at) * halves + half]


def gram_of(update_ref, genes_total):
    gram = None
    for group in range(update_ref.shape[0]):
        update = update_ref[group]
        part = lax.dot_general(
            update, update, (((1,), (1,)), ((), ())), preferred_element_type=jnp.float32
        )
        gram = part if gram is None else gram + part
    return gram / genes_total


def regroup_kernel(rows_of, genes_here, data_ref, links_ref, out_ref, order_ref):
    parts, rows, genes = out_ref.shape
    tile_cells = parts * rows_of
    span = order_ref.shape[0]
    share = span // parts
    last = pl.num_programs(0) - 1
    here = genes_here % genes

    @pl.when(pl.program_id(0) == 0)
    def _():
        to = lax.broadcasted_iota(jnp.int32, (span, span), 0)
        at = lax.broadcasted_iota(jnp.int32, (span, span), 1)
        source = (to % share // rows_of) * tile_cells + to // share * rows_of + to % rows_of
        order_ref[...] = (source == at).astype(jnp.bfloat16)

    def move(data):
        for turn in range(rows // share):
            taken = lax.dot_general(
                order_ref[...],
                data[:, turn * span : (turn + 1) * span],
                (((1,), (1,)), ((), ())),
                preferred_element_type=jnp.float32,
            )
            out_ref[:, turn * share : (turn + 1) * share] = taken.astype(jnp.bfloat16).reshape(
                parts, share, genes
            )

    @pl.when(pl.program_id(0) < last)
    def _():
        move(data_ref[...])

    @pl.when(pl.program_id(0) == last)
    def _():
        data = data_ref[:here].astype(jnp.float32)
        move(jnp.concatenate([data, links_ref[...]], axis=0).astype(jnp.bfloat16))


def share_second(second, out_ref, chunk, groups):
    width, cells = second.shape
    rows = cells * groups // out_ref.shape[0]
    tall = out_ref.shape[1] - chunk
    slabs = width // groups // tall
    lane = lax.broadcasted_iota(jnp.int32, (tall, LANES), 1)
    for at in range(cells // LANES):
        wide = second[:, at * LANES : (at + 1) * LANES].astype(jnp.float32)
        for group in range(groups):
            for device in range(LANES // rows):
                share = jnp.zeros((tall, LANES), jnp.float32)
                for slab in range(slabs):
                    first_row = (group * slabs + slab) * tall
                    turned = pltpu.roll(
                        wide[first_row : first_row + tall],
                        (slab - device) * rows % LANES,
                        1,
                    )
                    share = jnp.where(lane // rows == slab, turned, share)
                to = (at * (LANES // rows) + device) * groups + group
                out_ref[to, chunk:] = share.astype(jnp.bfloat16)


def first_kernel(
    genes_here, slots, own_ref, data_ref, start_ref, out_ref, links_ref, degree_ref
):
    devices, groups, rows, padded = data_ref.shape
    tiles = devices * slots
    packed = block(data_ref, 0)[:, padded - LANES :].astype(jnp.float32)
    offset = genes_here - (padded - LANES)
    links, degree = link_matrix(
        packed[:, offset : offset + 3], tiles, rows // slots, slots, rows // slots
    )
    links_ref[...] = links
    degree_ref[...] = degree
    scores = None
    for shift in range(groups):
        group = lax.rem(own_ref[0] + groups - shift, groups)
        part = lax.dot_general(
            start_ref[shift],
            block(data_ref, group),
            (((1,), (1,)), ((), ())),
            preferred_element_type=jnp.float32,
        )
        scores = part if scores is None else scores + part
    scores = scores / math.sqrt(genes_here * groups)
    second = diffuse(scores, links, degree[:1])
    push_update(genes_here, data_ref, second, out_ref, out_ref.shape[1])


def next_kernel(genes_here, chunks_ref, data_ref, links_ref, degree_ref, out_ref, update_ref):
    chunk = chunks_ref.shape[1]
    groups = data_ref.shape[1]
    genes_total = genes_here * groups
    pull_update(chunks_ref, update_ref)
    inverse = inverse_factor(gram_of(update_ref, genes_total))
    scores = None
    for group in range(groups):
        part = lax.dot_general(
            update_ref[group],
            block(data_ref, group),
            (((1,), (1,)), ((), ())),
            preferred_element_type=jnp.float32,
        )
        scores = part if scores is None else scores + part
    scores = jnp.dot(
        inverse, scores, precision=HIGHEST, preferred_element_type=jnp.float32
    ) / math.sqrt(genes_total)
    second = diffuse(scores, links_ref[...], degree_ref[:1])
    push_update(genes_here, data_ref, second, out_ref, chunk)
    if out_ref.shape[1] > chunk:
        share_second(second, out_ref, chunk, groups)


def last_kernel(genes_here, own_ref, chunks_ref, out_ref, update_ref):
    pull_update(chunks_ref, update_ref)
    genes_total = genes_here * update_ref.shape[0]
    inverse = inverse_factor(gram_of(update_ref, genes_total))
    mine = update_ref[own_ref[0]].astype(jnp.float32)
    loadings = jnp.dot(inverse, mine, precision=HIGHEST, preferred_element_type=jnp.float32)
    out_ref[...] = loadings[:, :genes_here]


def sum_kernel(chunks_ref, out_ref):
    parts = chunks_ref[:, : out_ref.shape[1]].astype(jnp.float32)
    total = jnp.sum(parts, axis=0).astype(jnp.bfloat16)
    out_ref[...] = jnp.broadcast_to(total[None], out_ref.shape)


def call(kernel, out_shape, scratch=(), scalars=0, arrays=0):
    in_specs = [pl.BlockSpec(memory_space=pltpu.SMEM)] * scalars
    in_specs += [pl.BlockSpec(memory_space=pltpu.VMEM)] * arrays
    return pl.pallas_call(
        kernel,
        out_shape=out_shape,
        in_specs=in_specs,
        out_specs=jax.tree.map(lambda _: pl.BlockSpec(memory_space=pltpu.VMEM), out_shape),
        scratch_shapes=list(scratch),
        compiler_params=pltpu.CompilerParams(vmem_limit_bytes=32 * 1024 * 1024),
    )


def by_cell(data, start, link_dev, link_slot, link_weight):
    axes = ("cells", "genes")
    devices, groups = lax.axis_size("cells"), lax.axis_size("genes")
    parts = devices * groups
    slots, neighbours = link_dev.shape
    genes_here, width = data.shape[1], start.shape[1]
    tile_cells = data.shape[0] // slots
    rows_of = tile_cells // parts
    rows = slots * rows_of
    padded = -(-genes_here // (2 * LANES)) * 2 * LANES
    cells = devices * rows
    chunk = groups * width * padded // (parts * LANES)
    own = lax.axis_index("genes").astype(jnp.int32).reshape(1)

    links = jnp.stack([link_dev, link_slot, link_weight]).astype(jnp.float32)
    links = jnp.pad(links, ((0, padded - genes_here - 3), (0, 0), (0, rows_of - neighbours)))
    links = jnp.broadcast_to(links[:, :, None], (links.shape[0], slots, parts, rows_of))
    links = links.reshape(links.shape[0], slots * tile_cells)
    span = max(1, 16 // rows_of) * tile_cells
    genes = 2 * LANES
    moved = pl.pallas_call(
        functools.partial(regroup_kernel, rows_of, genes_here),
        grid=(padded // genes,),
        out_shape=jax.ShapeDtypeStruct((parts, rows, padded), jnp.bfloat16),
        in_specs=[
            pl.BlockSpec((genes, slots * tile_cells), lambda at: (at, 0)),
            pl.BlockSpec(links.shape, lambda at: (0, 0)),
        ],
        out_specs=pl.BlockSpec((parts, rows, genes), lambda at: (0, 0, at)),
        scratch_shapes=[pltpu.VMEM((span, span), jnp.bfloat16)],
        compiler_params=pltpu.CompilerParams(vmem_limit_bytes=60 * 1024 * 1024),
    )(data.T, links)
    moved = lax.all_to_all(moved, axes, 0, 0, tiled=True).reshape(devices, groups, rows, padded)
    narrow = jnp.pad(start.astype(jnp.bfloat16).T, ((0, 0), (0, padded - genes_here)))
    starts = [narrow]
    for shift in range(1, groups):
        pairs = [(at, (at + shift) % groups) for at in range(groups)]
        starts.append(lax.ppermute(narrow, "genes", pairs))
    starts = jnp.stack(starts)

    chunks = jax.ShapeDtypeStruct((parts, chunk, LANES), jnp.bfloat16)
    update = pltpu.VMEM((groups, width, padded), jnp.bfloat16)
    links = jax.ShapeDtypeStruct((cells, cells), jnp.bfloat16)
    degree = jax.ShapeDtypeStruct((8, cells), jnp.float32)
    extra = jax.ShapeDtypeStruct((parts, chunk + 16, LANES), jnp.bfloat16)

    def gather(arrived):
        summed = call(sum_kernel, chunks, arrays=1)(arrived)
        return lax.all_to_all(summed, axes, 0, 0, tiled=True)

    pushed, links, degree = call(
        functools.partial(first_kernel, genes_here, slots),
        (chunks, links, degree),
        scalars=1,
        arrays=2,
    )(own, moved, starts)
    arrived = lax.all_to_all(pushed, axes, 0, 0, tiled=True)
    for step in range(1, ITERS):
        pushed = call(
            functools.partial(next_kernel, genes_here),
            extra if step == ITERS - 1 else chunks,
            (update,),
            arrays=4,
        )(gather(arrived), moved, links, degree)
        arrived = lax.all_to_all(pushed, axes, 0, 0, tiled=True)
    loadings = call(
        functools.partial(last_kernel, genes_here),
        jax.ShapeDtypeStruct((width, genes_here), jnp.float32),
        (update,),
        scalars=1,
        arrays=1,
    )(own, gather(arrived))

    part_width = width // groups
    slabs = part_width // 16
    smoothed = arrived[:, chunk:, : slabs * rows].reshape(parts, 16, slabs, slots, rows_of)
    smoothed = smoothed.transpose(2, 1, 3, 0, 4)
    return loadings.T, smoothed.reshape(part_width, slots * tile_cells)


def by_tile(data, start, link_dev, link_slot, link_weight):
    devices = lax.axis_size("cells")
    groups = lax.axis_size("genes")
    tiles_here, neighbours = link_dev.shape
    tile_cells = data.shape[0] // tiles_here
    genes_total = data.shape[1] * groups
    width = start.shape[1]
    part_width = width // groups
    capacity = max(2, 2 * tiles_here * neighbours // devices)
    slot_count = devices * capacity
    links = tiles_here * neighbours
    columns = part_width * tile_cells
    flat_dev = link_dev.reshape(links)
    flat_slot = link_slot.reshape(links)
    flat_weight = link_weight.reshape(links)
    dev_hits = (flat_dev[:, None] == jnp.arange(devices, dtype=jnp.int32)[None, :]).astype(
        jnp.int32
    )
    earlier = jnp.cumsum(dev_hits, axis=0) - dev_hits
    ranking = jnp.sum(earlier * dev_hits, axis=1)
    position = flat_dev * capacity + ranking
    placed = (position[:, None] == jnp.arange(slot_count, dtype=jnp.int32)[None, :]).astype(
        jnp.int32
    )
    wanted = jnp.sum(placed * (flat_slot + 1)[:, None], axis=0).reshape(devices, capacity)
    wanted_weight = jnp.sum(placed * flat_weight[:, None], axis=0).reshape(devices, capacity)
    asked_pair = (
        lax.all_to_all(wanted, "cells", split_axis=0, concat_axis=0, tiled=True),
        lax.all_to_all(wanted_weight, "cells", split_axis=0, concat_axis=0, tiled=True),
    )
    asked = asked_pair[0].reshape(slot_count)
    asked_weight = asked_pair[1].reshape(slot_count)
    tile_ids = jnp.arange(tiles_here, dtype=jnp.int32)
    serve_match = ((asked - 1)[:, None] == tile_ids[None, :]).astype(jnp.int32)
    serve = serve_match.astype(jnp.bfloat16)
    collect = (serve_match * asked_weight[:, None]).T.astype(jnp.bfloat16)
    placed_tiles = placed.reshape(tiles_here, neighbours, slot_count)
    link_matrix = jnp.sum(placed_tiles * link_weight[:, :, None], axis=1).astype(jnp.bfloat16)
    sender = jnp.sum(placed_tiles, axis=1).astype(jnp.bfloat16)
    degree = (self_weight + jnp.sum(link_weight, axis=1).astype(jnp.float32))[:, None]
    loadings = start
    smoothed = jnp.zeros((part_width, tiles_here * tile_cells), jnp.bfloat16)
    for step in range(ITERS):
        narrow = loadings.astype(jnp.bfloat16)
        partial_scores = lax.dot_general(
            narrow, data, (((0,), (1,)), ((), ())), preferred_element_type=jnp.float32
        )
        summed = lax.psum(partial_scores.astype(jnp.bfloat16), "genes").astype(jnp.float32)
        mine = lax.dynamic_slice_in_dim(summed, lax.axis_index("genes") * part_width, part_width, 0)
        scores = (mine / math.sqrt(genes_total)).astype(jnp.bfloat16)
        tiles = (
            scores.reshape(part_width, tiles_here, tile_cells)
            .transpose(1, 0, 2)
            .reshape(tiles_here, columns)
        )
        outgoing = jnp.dot(serve, tiles, preferred_element_type=jnp.float32).astype(jnp.bfloat16)
        linked = jnp.dot(
            link_matrix,
            lax.all_to_all(
                outgoing.reshape(devices, capacity, columns),
                "cells",
                split_axis=0,
                concat_axis=0,
                tiled=True,
            ).reshape(slot_count, -1),
            preferred_element_type=jnp.float32,
        )
        first = lax.optimization_barrier(
            ((self_weight * tiles.astype(jnp.float32) + linked) / degree).astype(jnp.bfloat16)
        )
        spread = lax.optimization_barrier(
            (self_weight * first.astype(jnp.float32) / degree).astype(jnp.bfloat16)
        )
        returning = lax.dot_general(
            sender, spread, (((0,), (0,)), ((), ())), preferred_element_type=jnp.float32
        ).astype(jnp.bfloat16)
        pushed = jnp.dot(
            collect,
            lax.all_to_all(
                returning.reshape(devices, capacity, columns),
                "cells",
                split_axis=0,
                concat_axis=0,
                tiled=True,
            ).reshape(slot_count, -1),
            preferred_element_type=jnp.float32,
        )
        second = (self_weight * spread.astype(jnp.float32) + pushed).astype(jnp.bfloat16)
        smoothed = (
            second.reshape(tiles_here, part_width, tile_cells)
            .transpose(1, 0, 2)
            .reshape(part_width, tiles_here * tile_cells)
        )
        update = lax.dot_general(
            data,
            lax.all_gather(smoothed, "genes", axis=0, tiled=True),
            (((0,), (1,)), ((), ())),
            preferred_element_type=jnp.float32,
        )
        update = lax.psum(update, "cells")
        gram_part = jnp.dot(
            update.T, update, precision=lax.Precision.HIGHEST, preferred_element_type=jnp.float32
        )
        gram = lax.psum(gram_part, "genes") / genes_total
        factor = jnp.linalg.cholesky(gram)
        loadings = lax.linalg.triangular_solve(
            factor, update, left_side=False, lower=True, transpose_a=True
        )
    return (loadings, smoothed)


def per_device(data, start, link_dev, link_slot, link_weight):
    groups = lax.axis_size("genes")
    parts = lax.axis_size("cells") * groups
    slots, neighbours = link_dev.shape
    tile_cells = data.shape[0] // slots
    genes_here, width = data.shape[1], start.shape[1]
    padded = -(-genes_here // (2 * LANES)) * 2 * LANES
    rows = slots * tile_cells // parts
    fits = (
        tile_cells % (8 * parts) == 0
        and neighbours <= tile_cells // parts
        and rows % 16 == 0
        and LANES % rows == 0
        and genes_here % 8 == 0
        and 3 <= padded - genes_here <= LANES
        and width % (16 * groups) == 0
        and width // groups // 16 * rows <= LANES
        and width * padded * groups % (parts * LANES * 16) == 0
    )
    way = by_cell if fits else by_tile
    return way(data, start, link_dev, link_slot, link_weight)


def solution(mesh):
    placed = (
        P("cells", "genes"),
        P("genes", None),
        P("cells", None),
        P("cells", None),
        P("cells", None),
    )
    return jax.shard_map(
        per_device,
        mesh=mesh,
        in_specs=placed,
        out_specs=(P("genes", None), P("genes", "cells")),
        check_vma=False,
    )
```

```python
import functools
import math

import jax
import jax.numpy as jnp
from jax import lax
from jax.experimental import pallas as pl
from jax.experimental.pallas import tpu as pltpu
from jax.sharding import Mesh
from jax.sharding import PartitionSpec as P

ITERS = 3
LANES = 128

self_weight = 8.0
HIGHEST = lax.Precision.HIGHEST


def inverse_factor(gram):
    width = gram.shape[0]
    rows = lax.broadcasted_iota(jnp.int32, (width, width), 0)
    cols = lax.broadcasted_iota(jnp.int32, (width, width), 1)
    diagonal = jnp.where(rows == cols, gram, 0.0)
    down = lax.rsqrt(jnp.sum(diagonal, axis=1, keepdims=True))
    along = lax.rsqrt(jnp.sum(diagonal, axis=0, keepdims=True))
    scaled = gram * down * along
    state = jnp.concatenate([jnp.where(rows == cols, along, 0.0), scaled], axis=1)
    strips = [state[at : at + 8] for at in range(0, width, 8)]
    shape = strips[0].shape
    place = lax.broadcasted_iota(jnp.int32, shape, 0)
    done = []
    for panel, strip in enumerate(strips):
        base = width + 8 * panel

        def column(of, j):
            return jnp.broadcast_to(of[:, base + j : base + j + 1], shape)

        columns = [column(strip, j) for j in range(8)]
        core = {
            (i, j): jnp.broadcast_to(columns[j][i : i + 1], shape)
            for j in range(8)
            for i in range(j, 8)
        }
        lines = [jnp.broadcast_to(strip[j : j + 1], shape) for j in range(8)]
        factor, solved = {}, [None] * 8
        for j in range(0, 8, 2):
            a, b, c = core[j, j], core[j + 1, j], core[j + 1, j + 1]
            inverse = 1.0 / (a * c - b * b)
            step = b * (1.0 / a)
            ia, ib, ic = c * inverse, b * inverse, a * inverse
            for i in range(j + 2, 8):
                factor[i, j] = core[i, j] * ia - core[i, j + 1] * ib
                factor[i, j + 1] = core[i, j + 1] * ic - core[i, j] * ib
            for i in range(j + 2, 8):
                for m in range(j + 2, i + 1):
                    core[i, m] -= factor[i, j] * core[m, j] + factor[i, j + 1] * core[m, j + 1]
                lines[i] -= factor[i, j] * lines[j] + factor[i, j + 1] * lines[j + 1]
            solved[j] = ia * lines[j] - ib * lines[j + 1]
            solved[j + 1] = ic * lines[j + 1] - ib * lines[j]
            lines[j + 1] -= step * lines[j]
            core[j + 1, j + 1] = c - step * b
        for j in reversed(range(0, 8, 2)):
            for i in range(j + 2, 8):
                solved[j] -= factor[i, j] * solved[i]
                solved[j + 1] -= factor[i, j + 1] * solved[i]
        for later in range(panel + 1, len(strips)):
            terms = [column(strips[later], j) * solved[j] for j in range(8)]
            while len(terms) > 1:
                terms = [terms[at] + terms[at + 1] for at in range(0, len(terms), 2)]
            strips[later] = strips[later] - terms[0]
        final = lines[0] * lax.rsqrt(core[0, 0])
        for j in range(1, 8):
            final = jnp.where(place == j, lines[j] * lax.rsqrt(core[j, j]), final)
        done.append(final)
    return jnp.concatenate(done, axis=0)[:, :width]


def link_matrix(packed, tiles, neighbours, slots, rows_of):
    own_dev, own_slot, own_weight = packed[:, 0:1], packed[:, 1:2], packed[:, 2:3]
    target = own_dev * slots + own_slot
    lane = lax.broadcasted_iota(jnp.int32, (tiles * neighbours, tiles), 1).astype(jnp.float32)
    hits = jnp.where(lane == target, own_weight, 0.0)
    weights = jnp.sum(hits.reshape(tiles, neighbours, tiles), axis=1)
    tile_row = lax.broadcasted_iota(jnp.int32, (tiles, tiles), 0)
    tile_col = lax.broadcasted_iota(jnp.int32, (tiles, tiles), 1)
    weights = weights + jnp.where(tile_row == tile_col, self_weight, 0.0)
    cells = tiles * rows_of
    tile_of = lax.broadcasted_iota(jnp.int32, (cells, tiles), 0) // rows_of
    expand = (tile_of == lax.broadcasted_iota(jnp.int32, (cells, tiles), 1)).astype(jnp.bfloat16)
    tall = jnp.dot(expand, weights.astype(jnp.bfloat16), preferred_element_type=jnp.float32)
    full = lax.dot_general(
        tall.astype(jnp.bfloat16),
        expand,
        (((1,), (1,)), ((), ())),
        preferred_element_type=jnp.float32,
    )
    same = (
        lax.broadcasted_iota(jnp.int32, (cells, cells), 0) % rows_of
        == lax.broadcasted_iota(jnp.int32, (cells, cells), 1) % rows_of
    )
    full = jnp.where(same, full, 0.0).astype(jnp.bfloat16)
    ones = jnp.ones((8, cells), jnp.bfloat16)
    degree = lax.dot_general(
        ones, full, (((1,), (1,)), ((), ())), preferred_element_type=jnp.float32
    )
    return full, degree


def diffuse(scores, links, degree):
    scores = scores.astype(jnp.bfloat16)
    total = lax.dot_general(
        scores, links, (((1,), (1,)), ((), ())), preferred_element_type=jnp.float32
    )
    first = (total / degree).astype(jnp.bfloat16).astype(jnp.float32)
    spread = (self_weight * first / degree).astype(jnp.bfloat16)
    return jnp.dot(spread, links, preferred_element_type=jnp.float32).astype(jnp.bfloat16)


def block(data_ref, group):
    part = data_ref[:, group]
    return part.reshape(part.shape[0] * part.shape[1], part.shape[2])


def push_update(genes_here, data_ref, second, cut_ref):
    groups, padded = data_ref.shape[1], data_ref.shape[3]
    cores = cut_ref.shape[0]
    chunk = second.shape[0] // cores
    blocks = padded // LANES
    for group in range(groups):
        update = jnp.dot(second, block(data_ref, group), preferred_element_type=jnp.float32)
        lane = lax.broadcasted_iota(jnp.int32, update.shape, 1)
        update = jnp.where(lane < genes_here, update, 0.0).astype(jnp.bfloat16)
        for at in range(blocks):
            for core in range(cores):
                cut_ref[core, group * blocks + at, :chunk] = update[
                    core * chunk : (core + 1) * chunk, at * LANES : (at + 1) * LANES
                ]


def pull_update(core, mine_ref, other_ref, update_ref):
    groups, _, _, padded = update_ref.shape
    blocks = padded // LANES
    for group in range(groups):
        for at in range(blocks):
            lanes = slice(at * LANES, (at + 1) * LANES)
            update_ref[group, core, :, lanes] = mine_ref[group * blocks + at]
            update_ref[group, 1 - core, :, lanes] = other_ref[group * blocks + at]


def columns_of(update_ref, group):
    update = update_ref[group]
    return update.reshape(update.shape[0] * update.shape[1], update.shape[2])


def gram_of(update_ref, genes_total):
    gram = None
    for group in range(update_ref.shape[0]):
        update = columns_of(update_ref, group)
        part = lax.dot_general(
            update, update, (((1,), (1,)), ((), ())), preferred_element_type=jnp.float32
        )
        gram = part if gram is None else gram + part
    return gram / genes_total


def regroup_kernel(
    rows_of, data_any, dev_any, slot_any, weight_any, out_ref, data_ref, link_ref, data_sem, link_sem
):
    genes_here, cells = data_ref.shape
    parts, rows, padded = out_ref.shape
    slots, neighbours = link_ref.shape[1:]
    tile_cells = cells // slots
    share = max(16, rows_of)
    span = share * parts
    turns = rows // share
    link_copies = [
        pltpu.make_async_copy(source, link_ref.at[at], link_sem.at[at])
        for at, source in enumerate((dev_any, slot_any, weight_any))
    ]
    for copy in link_copies:
        copy.start()
    data_copies = []
    for turn in range(turns):
        part = pl.ds(turn * span, span)
        data_copies.append(
            pltpu.make_async_copy(
                data_any.at[:, part], data_ref.at[:, part], data_sem.at[turn]
            )
        )
        data_copies[turn].start()

    to = lax.broadcasted_iota(jnp.int32, (span, span), 0)
    at = lax.broadcasted_iota(jnp.int32, (span, span), 1)
    source = (to % share // rows_of) * tile_cells + to // share * rows_of + to % rows_of
    order = (source == at).astype(jnp.bfloat16)
    spread = (
        lax.broadcasted_iota(jnp.int32, (neighbours, cells), 0)
        == lax.broadcasted_iota(jnp.int32, (neighbours, cells), 1) % rows_of
    ).astype(jnp.float32)
    tile = lax.broadcasted_iota(jnp.int32, (slots, cells), 0)
    own_tile = tile == lax.broadcasted_iota(jnp.int32, (slots, cells), 1) // tile_cells
    row = lax.broadcasted_iota(jnp.int32, (padded - genes_here, cells), 0)
    links = jnp.zeros((padded - genes_here, cells), jnp.float32)
    for at, copy in enumerate(link_copies):
        copy.wait()
        wide = jnp.dot(
            link_ref[at].astype(jnp.float32), spread, preferred_element_type=jnp.float32
        )
        wide = jnp.sum(jnp.where(own_tile, wide, 0.0), axis=0, keepdims=True)
        links = jnp.where(row == at, wide, links)
    whole = padded - LANES

    def moved(part):
        taken = lax.dot_general(
            order, part, (((1,), (1,)), ((), ())), preferred_element_type=jnp.float32
        )
        return taken.astype(jnp.bfloat16).reshape(parts, share, part.shape[0])

    for turn in range(turns):
        part = slice(turn * span, (turn + 1) * span)
        keep = slice(turn * share, (turn + 1) * share)
        data_copies[turn].wait()
        out_ref[:, keep, :whole] = moved(data_ref[:whole, part])
        rest = data_ref[whole:genes_here, part].astype(jnp.float32)
        rest = jnp.concatenate([rest, links[:, part]], axis=0)
        out_ref[:, keep, whole:] = moved(rest.astype(jnp.bfloat16))


def share_second(core, second, cut_ref, chunk, groups):
    width, cells = second.shape
    cores, blocks, tall = cut_ref.shape[:3]
    rows = cells * groups // (cores * blocks)
    tall = tall - chunk
    slabs = width // groups // tall
    lane = lax.broadcasted_iota(jnp.int32, (tall, LANES), 1) // rows - core * slabs
    for at in range(cells // LANES):
        wide = second[:, at * LANES : (at + 1) * LANES].astype(jnp.float32)
        for group in range(groups):
            for device in range(LANES // rows):
                share = jnp.zeros((tall, LANES), jnp.float32)
                for slab in range(slabs):
                    first_row = (group * slabs + slab) * tall
                    for turn in range(cores):
                        turned = pltpu.roll(
                            wide[first_row : first_row + tall],
                            (turn * slabs + slab - device) * rows % LANES,
                            1,
                        )
                        share = jnp.where((lane == slab) & (core == turn), turned, share)
                chip, to = divmod(at * (LANES // rows) + device, cores)
                cut_ref[to, chip * groups + group, chunk:] = share.astype(jnp.bfloat16)


def order_shares(arrived_ref, chunk, out_ref, groups, cores, slots):
    part_width, cells = out_ref.shape
    blocks, tall = arrived_ref.shape[:2]
    tall = tall - chunk
    parts = blocks * cores
    rows_of = cells // (slots * parts)
    rows = slots * rows_of
    slabs = part_width // tall
    together = LANES // rows_of
    lane = lax.broadcasted_iota(jnp.int32, (tall, LANES), 1) // rows_of
    for slab in range(slabs):
        for slot in range(slots):
            for first in range(0, parts, together):
                whole = jnp.zeros((tall, LANES), jnp.float32)
                for at in range(together):
                    chip, rest = divmod(first + at, cores * groups)
                    core, group = divmod(rest, groups)
                    source = (core * slabs + slab) * rows + slot * rows_of
                    share = arrived_ref[chip * groups + group, chunk:].astype(jnp.float32)
                    turned = pltpu.roll(share, (at * rows_of - source) % LANES, 1)
                    whole = jnp.where(lane == at, turned, whole)
                to = (slot * parts + first) * rows_of
                out_ref[slab * tall : (slab + 1) * tall, to : to + LANES] = whole.astype(
                    jnp.bfloat16
                )


def first_kernel(
    genes_here,
    slots,
    place_ref,
    data_ref,
    start_ref,
    mine_ref,
    other_ref,
    links_ref,
    degree_ref,
    cut_ref,
):
    devices, groups, rows, padded = data_ref.shape
    tiles = devices * slots
    core, own = place_ref[0], place_ref[1]
    packed = block(data_ref, 0)[:, padded - LANES :].astype(jnp.float32)
    offset = genes_here - (padded - LANES)
    links, degree = link_matrix(
        packed[:, offset : offset + 3], tiles, rows // slots, slots, rows // slots
    )
    links_ref[...] = links
    degree_ref[...] = degree
    scores = None
    for shift in range(groups):
        group = lax.rem(own + groups - shift, groups)
        part = lax.dot_general(
            start_ref[shift],
            block(data_ref, group),
            (((1,), (1,)), ((), ())),
            preferred_element_type=jnp.float32,
        )
        scores = part if scores is None else scores + part
    scores = scores / math.sqrt(genes_here * groups)
    second = diffuse(scores, links, degree[:1])
    push_update(genes_here, data_ref, second, cut_ref)
    mine_ref[...] = cut_ref[core]
    other_ref[...] = cut_ref[1 - core]


def next_kernel(
    genes_here,
    place_ref,
    half_ref,
    rest_ref,
    data_ref,
    links_ref,
    degree_ref,
    mine_ref,
    other_ref,
    update_ref,
    cut_ref,
):
    core = place_ref[0]
    groups = data_ref.shape[1]
    chunk = half_ref.shape[1]
    genes_total = genes_here * groups
    pull_update(core, half_ref, rest_ref, update_ref)
    inverse = inverse_factor(gram_of(update_ref, genes_total))
    scores = None
    for group in range(groups):
        part = lax.dot_general(
            columns_of(update_ref, group),
            block(data_ref, group),
            (((1,), (1,)), ((), ())),
            preferred_element_type=jnp.float32,
        )
        scores = part if scores is None else scores + part
    scores = jnp.dot(
        inverse, scores, precision=HIGHEST, preferred_element_type=jnp.float32
    ) / math.sqrt(genes_total)
    second = diffuse(scores, links_ref[...], degree_ref[:1])
    push_update(genes_here, data_ref, second, cut_ref)
    if cut_ref.shape[2] > chunk:
        share_second(core, second, cut_ref, chunk, groups)
    mine_ref[...] = cut_ref[core]
    other_ref[...] = cut_ref[1 - core]


def last_kernel(
    genes_here, slots, place_ref, half_ref, rest_ref, arrived_ref, out_ref, smoothed_ref, update_ref
):
    core, own = place_ref[0], place_ref[1]
    groups, cores = update_ref.shape[:2]
    pull_update(core, half_ref, rest_ref, update_ref)
    genes_total = genes_here * groups
    inverse = inverse_factor(gram_of(update_ref, genes_total))
    mine = columns_of(update_ref, own).astype(jnp.float32)
    loadings = jnp.dot(inverse, mine, precision=HIGHEST, preferred_element_type=jnp.float32)
    out_ref[...] = loadings[:, :genes_here]
    order_shares(arrived_ref, half_ref.shape[1], smoothed_ref, groups, cores, slots)


def add_kernel(mine_ref, arrived_ref, out_ref):
    total = mine_ref[...].astype(jnp.float32) + arrived_ref[...].astype(jnp.float32)
    out_ref[...] = total.astype(jnp.bfloat16)


def sum_kernel(chunks_ref, out_ref):
    parts = chunks_ref[:, : out_ref.shape[1]].astype(jnp.float32)
    total = jnp.sum(parts, axis=0).astype(jnp.bfloat16)
    out_ref[...] = jnp.broadcast_to(total[None], out_ref.shape)


def like(array):
    return jax.ShapeDtypeStruct(array.shape, array.dtype)


def call(kernel, out_shape, scratch=(), scalars=0, arrays=0):
    in_specs = [pl.BlockSpec(memory_space=pltpu.SMEM)] * scalars
    in_specs += [pl.BlockSpec(memory_space=pltpu.VMEM)] * arrays
    return pl.pallas_call(
        kernel,
        out_shape=out_shape,
        in_specs=in_specs,
        out_specs=jax.tree.map(lambda _: pl.BlockSpec(memory_space=pltpu.VMEM), out_shape),
        scratch_shapes=list(scratch),
        compiler_params=pltpu.CompilerParams(vmem_limit_bytes=32 * 1024 * 1024),
    )


def by_cell(data, start, link_dev, link_slot, link_weight):
    cores, groups = lax.axis_size("core"), lax.axis_size("genes")
    devices = lax.axis_size("chips") * cores
    parts = devices * groups
    blocks = parts // cores
    slots, neighbours = link_dev.shape
    genes_here, width = data.shape[1], start.shape[1]
    tile_cells = data.shape[0] // slots
    rows_of = tile_cells // parts
    rows = slots * rows_of
    padded = -(-genes_here // LANES) * LANES
    cells = devices * rows
    chunk = width // cores
    place = jnp.stack([lax.axis_index("core"), lax.axis_index("genes")]).astype(jnp.int32)

    def exchange(array):
        return lax.all_to_all(array, ("chips", "genes"), 0, 0, tiled=True)

    def swap(array):
        return lax.ppermute(array, "core", [(0, 1), (1, 0)])

    narrow = jnp.pad(start.astype(jnp.bfloat16).T, ((0, 0), (0, padded - genes_here)))
    starts = [narrow]
    for shift in range(1, groups):
        pairs = [(at, (at + shift) % groups) for at in range(groups)]
        starts.append(lax.ppermute(narrow, "genes", pairs))
    starts = jnp.stack(starts)
    moved = pl.pallas_call(
        functools.partial(regroup_kernel, rows_of),
        out_shape=jax.ShapeDtypeStruct((parts, rows, padded), jnp.bfloat16),
        in_specs=[pl.BlockSpec(memory_space=pl.ANY)] * 4,
        out_specs=pl.BlockSpec(memory_space=pltpu.VMEM),
        scratch_shapes=[
            pltpu.VMEM((genes_here, slots * tile_cells), jnp.bfloat16),
            pltpu.VMEM((3, slots, neighbours), jnp.int32),
            pltpu.SemaphoreType.DMA((rows // max(16, rows_of),)),
            pltpu.SemaphoreType.DMA((3,)),
        ],
        compiler_params=pltpu.CompilerParams(vmem_limit_bytes=32 * 1024 * 1024),
    )(data.T, link_dev, link_slot, link_weight)
    moved, starts = lax.optimization_barrier((moved, starts))
    moved = lax.all_to_all(moved, ("chips", "core", "genes"), 0, 0, tiled=True)
    moved = moved.reshape(devices, groups, rows, padded)

    def cut(tall):
        return (
            jax.ShapeDtypeStruct((blocks, tall, LANES), jnp.bfloat16),
            pltpu.VMEM((cores, blocks, tall, LANES), jnp.bfloat16),
        )

    update = pltpu.VMEM((groups, cores, chunk, padded), jnp.bfloat16)
    links = jax.ShapeDtypeStruct((cells, cells), jnp.bfloat16)
    degree = jax.ShapeDtypeStruct((8, cells), jnp.float32)

    def reduce(mine, other):
        return exchange(call(add_kernel, like(mine), arrays=2)(mine, swap(other)))

    def gather(arrived):
        half = exchange(call(sum_kernel, cut(chunk)[0], arrays=1)(arrived))
        return half, swap(half)

    share, scratch = cut(chunk)
    mine, other, links, degree = call(
        functools.partial(first_kernel, genes_here, slots),
        (share, share, links, degree),
        (scratch,),
        scalars=1,
        arrays=2,
    )(place, moved, starts)
    arrived = reduce(mine, other)
    for step in range(1, ITERS):
        share, scratch = cut(chunk + 16 if step == ITERS - 1 else chunk)
        mine, other = call(
            functools.partial(next_kernel, genes_here),
            (share, share),
            (update, scratch),
            scalars=1,
            arrays=5,
        )(place, *gather(arrived), moved, links, degree)
        arrived = reduce(mine, other)
    loadings, smoothed = call(
        functools.partial(last_kernel, genes_here, slots),
        (
            jax.ShapeDtypeStruct((width, genes_here), jnp.float32),
            jax.ShapeDtypeStruct((width // groups, slots * tile_cells), jnp.bfloat16),
        ),
        (update,),
        scalars=1,
        arrays=3,
    )(place, *gather(arrived), arrived)
    return loadings.T, smoothed


def by_tile(data, start, link_dev, link_slot, link_weight):
    devices = lax.axis_size("cells")
    groups = lax.axis_size("genes")
    tiles_here, neighbours = link_dev.shape
    tile_cells = data.shape[0] // tiles_here
    genes_total = data.shape[1] * groups
    width = start.shape[1]
    part_width = width // groups
    capacity = max(2, 2 * tiles_here * neighbours // devices)
    slot_count = devices * capacity
    links = tiles_here * neighbours
    columns = part_width * tile_cells
    flat_dev = link_dev.reshape(links)
    flat_slot = link_slot.reshape(links)
    flat_weight = link_weight.reshape(links)
    dev_hits = (flat_dev[:, None] == jnp.arange(devices, dtype=jnp.int32)[None, :]).astype(
        jnp.int32
    )
    earlier = jnp.cumsum(dev_hits, axis=0) - dev_hits
    ranking = jnp.sum(earlier * dev_hits, axis=1)
    position = flat_dev * capacity + ranking
    placed = (position[:, None] == jnp.arange(slot_count, dtype=jnp.int32)[None, :]).astype(
        jnp.int32
    )
    wanted = jnp.sum(placed * (flat_slot + 1)[:, None], axis=0).reshape(devices, capacity)
    wanted_weight = jnp.sum(placed * flat_weight[:, None], axis=0).reshape(devices, capacity)
    asked_pair = (
        lax.all_to_all(wanted, "cells", split_axis=0, concat_axis=0, tiled=True),
        lax.all_to_all(wanted_weight, "cells", split_axis=0, concat_axis=0, tiled=True),
    )
    asked = asked_pair[0].reshape(slot_count)
    asked_weight = asked_pair[1].reshape(slot_count)
    tile_ids = jnp.arange(tiles_here, dtype=jnp.int32)
    serve_match = ((asked - 1)[:, None] == tile_ids[None, :]).astype(jnp.int32)
    serve = serve_match.astype(jnp.bfloat16)
    collect = (serve_match * asked_weight[:, None]).T.astype(jnp.bfloat16)
    placed_tiles = placed.reshape(tiles_here, neighbours, slot_count)
    link_matrix = jnp.sum(placed_tiles * link_weight[:, :, None], axis=1).astype(jnp.bfloat16)
    sender = jnp.sum(placed_tiles, axis=1).astype(jnp.bfloat16)
    degree = (self_weight + jnp.sum(link_weight, axis=1).astype(jnp.float32))[:, None]
    loadings = start
    smoothed = jnp.zeros((part_width, tiles_here * tile_cells), jnp.bfloat16)
    for step in range(ITERS):
        narrow = loadings.astype(jnp.bfloat16)
        partial_scores = lax.dot_general(
            narrow, data, (((0,), (1,)), ((), ())), preferred_element_type=jnp.float32
        )
        summed = lax.psum(partial_scores.astype(jnp.bfloat16), "genes").astype(jnp.float32)
        mine = lax.dynamic_slice_in_dim(summed, lax.axis_index("genes") * part_width, part_width, 0)
        scores = (mine / math.sqrt(genes_total)).astype(jnp.bfloat16)
        tiles = (
            scores.reshape(part_width, tiles_here, tile_cells)
            .transpose(1, 0, 2)
            .reshape(tiles_here, columns)
        )
        outgoing = jnp.dot(serve, tiles, preferred_element_type=jnp.float32).astype(jnp.bfloat16)
        linked = jnp.dot(
            link_matrix,
            lax.all_to_all(
                outgoing.reshape(devices, capacity, columns),
                "cells",
                split_axis=0,
                concat_axis=0,
                tiled=True,
            ).reshape(slot_count, -1),
            preferred_element_type=jnp.float32,
        )
        first = lax.optimization_barrier(
            ((self_weight * tiles.astype(jnp.float32) + linked) / degree).astype(jnp.bfloat16)
        )
        spread = lax.optimization_barrier(
            (self_weight * first.astype(jnp.float32) / degree).astype(jnp.bfloat16)
        )
        returning = lax.dot_general(
            sender, spread, (((0,), (0,)), ((), ())), preferred_element_type=jnp.float32
        ).astype(jnp.bfloat16)
        pushed = jnp.dot(
            collect,
            lax.all_to_all(
                returning.reshape(devices, capacity, columns),
                "cells",
                split_axis=0,
                concat_axis=0,
                tiled=True,
            ).reshape(slot_count, -1),
            preferred_element_type=jnp.float32,
        )
        second = (self_weight * spread.astype(jnp.float32) + pushed).astype(jnp.bfloat16)
        smoothed = (
            second.reshape(tiles_here, part_width, tile_cells)
            .transpose(1, 0, 2)
            .reshape(part_width, tiles_here * tile_cells)
        )
        update = lax.dot_general(
            data,
            lax.all_gather(smoothed, "genes", axis=0, tiled=True),
            (((0,), (1,)), ((), ())),
            preferred_element_type=jnp.float32,
        )
        update = lax.psum(update, "cells")
        gram_part = jnp.dot(
            update.T, update, precision=lax.Precision.HIGHEST, preferred_element_type=jnp.float32
        )
        gram = lax.psum(gram_part, "genes") / genes_total
        factor = jnp.linalg.cholesky(gram)
        loadings = lax.linalg.triangular_solve(
            factor, update, left_side=False, lower=True, transpose_a=True
        )
    return (loadings, smoothed)


def fits_by_cell(mesh, data, start, link_dev):
    groups, parts = mesh.shape["genes"], mesh.size
    slots, neighbours = link_dev.shape[0] * groups // parts, link_dev.shape[1]
    tile_cells = data.shape[0] // link_dev.shape[0]
    genes_here, width = data.shape[1] // groups, start.shape[1]
    padded = -(-genes_here // LANES) * LANES
    rows_of = tile_cells // parts
    rows = slots * rows_of
    return (
        mesh.shape["cells"] % 2 == 0
        and tile_cells % (8 * parts) == 0
        and neighbours <= rows_of
        and rows % 16 == 0
        and rows % max(16, rows_of) == 0
        and LANES % rows == 0
        and genes_here % 8 == 0
        and padded - genes_here >= 3
        and groups * padded // LANES == parts // 2
        and width % (32 * groups) == 0
        and width // groups // 16 * rows * 2 <= LANES
    )


def solution(mesh):
    chips = Mesh(
        mesh.devices.reshape(mesh.shape["cells"] // 2, 2, mesh.shape["genes"]),
        ("chips", "core", "genes"),
    )

    def program(data, start, link_dev, link_slot, link_weight):
        if fits_by_cell(mesh, data, start, link_dev):
            way, over, cells = by_cell, chips, ("chips", "core")
        else:
            way, over, cells = by_tile, mesh, "cells"
        return jax.shard_map(
            way,
            mesh=over,
            in_specs=(P(cells, "genes"), P("genes", None)) + (P(cells, None),) * 3,
            out_specs=(P("genes", None), P("genes", cells)),
            check_vma=False,
        )(data, start, link_dev, link_slot, link_weight)

    return program
```

```python
import functools
import math

import jax
import jax.numpy as jnp
from jax import lax
from jax.experimental import pallas as pl
from jax.experimental.pallas import tpu as pltpu
from jax.sharding import Mesh
from jax.sharding import PartitionSpec as P

ITERS = 3
LANES = 128
AMPLIFIED = 4.0

self_weight = 8.0
HIGHEST = lax.Precision.HIGHEST


def inverse_factor(gram):
    width = gram.shape[0]
    rows = lax.broadcasted_iota(jnp.int32, (width, width), 0)
    cols = lax.broadcasted_iota(jnp.int32, (width, width), 1)
    diagonal = jnp.where(rows == cols, gram, 0.0)
    down = lax.rsqrt(jnp.sum(diagonal, axis=1, keepdims=True))
    along = lax.rsqrt(jnp.sum(diagonal, axis=0, keepdims=True))
    scaled = gram * down * along
    state = jnp.concatenate([(rows == cols).astype(jnp.float32), scaled], axis=1)
    strips = [state[at : at + 8] for at in range(0, width, 8)]
    shape = strips[0].shape
    place = lax.broadcasted_iota(jnp.int32, shape, 0)
    done = []
    for panel, strip in enumerate(strips):
        base = width + 8 * panel

        def column(of, j):
            return jnp.broadcast_to(of[:, base + j : base + j + 1], shape)

        columns = [column(strip, j) for j in range(8)]
        core = {
            (i, j): jnp.broadcast_to(columns[j][i : i + 1], shape)
            for j in range(8)
            for i in range(j, 8)
        }
        lines = [jnp.broadcast_to(strip[j : j + 1], shape) for j in range(8)]
        below = range(panel + 1, len(strips))
        rest = {(at, j): column(strips[at], j) for at in below for j in range(8)}
        for j in range(0, 8, 2):
            a, b, c = core[j, j], core[j + 1, j], core[j + 1, j + 1]
            inverse = 1.0 / (a * c - b * b)
            step = b * (1.0 / a)
            ia, ib, ic = c * inverse, b * inverse, a * inverse

            def factors(first, second):
                return first * ia - second * ib, second * ic - first * ib

            for i in range(j + 2, 8):
                first, second = factors(core[i, j], core[i, j + 1])
                for m in range(j + 2, i + 1):
                    core[i, m] -= first * core[m, j] + second * core[m, j + 1]
                lines[i] -= first * lines[j] + second * lines[j + 1]
            for at in below:
                first, second = factors(rest[at, j], rest[at, j + 1])
                for m in range(j + 2, 8):
                    rest[at, m] -= first * core[m, j] + second * core[m, j + 1]
                strips[at] -= first * lines[j] + second * lines[j + 1]
            lines[j + 1] -= step * lines[j]
            core[j + 1, j + 1] = c - step * b
        final = lines[0] * lax.rsqrt(core[0, 0])
        for j in range(1, 8):
            final = jnp.where(place == j, lines[j] * lax.rsqrt(core[j, j]), final)
        done.append(final)
    inverse = jnp.concatenate(done, axis=0)[:, :width]
    return inverse * along, jnp.sum(inverse * inverse, axis=1, keepdims=True)


def link_matrix(packed, tiles, neighbours, slots, rows_of):
    own_dev, own_slot, own_weight = packed[:, 0:1], packed[:, 1:2], packed[:, 2:3]
    target = own_dev * slots + own_slot
    lane = lax.broadcasted_iota(jnp.int32, (tiles * neighbours, tiles), 1).astype(jnp.float32)
    hits = jnp.where(lane == target, own_weight, 0.0)
    weights = jnp.sum(hits.reshape(tiles, neighbours, tiles), axis=1)
    tile_row = lax.broadcasted_iota(jnp.int32, (tiles, tiles), 0)
    tile_col = lax.broadcasted_iota(jnp.int32, (tiles, tiles), 1)
    weights = weights + jnp.where(tile_row == tile_col, self_weight, 0.0)
    cells = tiles * rows_of
    tile_of = lax.broadcasted_iota(jnp.int32, (cells, tiles), 0) // rows_of
    expand = (tile_of == lax.broadcasted_iota(jnp.int32, (cells, tiles), 1)).astype(jnp.bfloat16)
    tall = jnp.dot(expand, weights.astype(jnp.bfloat16), preferred_element_type=jnp.float32)
    full = lax.dot_general(
        tall.astype(jnp.bfloat16),
        expand,
        (((1,), (1,)), ((), ())),
        preferred_element_type=jnp.float32,
    )
    same = (
        lax.broadcasted_iota(jnp.int32, (cells, cells), 0) % rows_of
        == lax.broadcasted_iota(jnp.int32, (cells, cells), 1) % rows_of
    )
    full = jnp.where(same, full, 0.0).astype(jnp.bfloat16)
    ones = jnp.ones((8, cells), jnp.bfloat16)
    degree = lax.dot_general(
        ones, full, (((1,), (1,)), ((), ())), preferred_element_type=jnp.float32
    )
    return full, degree


def diffuse(scores, links, degree):
    scores = scores.astype(jnp.bfloat16)
    total = lax.dot_general(
        scores, links, (((1,), (1,)), ((), ())), preferred_element_type=jnp.float32
    )
    first = (total / degree).astype(jnp.bfloat16).astype(jnp.float32)
    spread = (self_weight * first / degree).astype(jnp.bfloat16)
    return jnp.dot(spread, links, preferred_element_type=jnp.float32).astype(jnp.bfloat16)


def block(data_ref, group):
    part = data_ref[:, group]
    return part.reshape(part.shape[0] * part.shape[1], part.shape[2])


def push_update(genes_here, data_ref, second, cut_ref):
    groups, padded = data_ref.shape[1], data_ref.shape[3]
    cores = cut_ref.shape[0]
    chunk = second.shape[0] // cores
    blocks = padded // LANES
    for group in range(groups):
        update = jnp.dot(second, block(data_ref, group), preferred_element_type=jnp.float32)
        lane = lax.broadcasted_iota(jnp.int32, update.shape, 1)
        update = jnp.where(lane < genes_here, update, 0.0).astype(cut_ref.dtype)
        for at in range(blocks):
            for core in range(cores):
                cut_ref[core, group * blocks + at, :chunk] = update[
                    core * chunk : (core + 1) * chunk, at * LANES : (at + 1) * LANES
                ]


def pull_update(core, mine_ref, other_ref, update_ref):
    groups, _, _, padded = update_ref.shape
    blocks = padded // LANES
    for group in range(groups):
        for at in range(blocks):
            lanes = slice(at * LANES, (at + 1) * LANES)
            update_ref[group, core, :, lanes] = mine_ref[group * blocks + at]
            update_ref[group, 1 - core, :, lanes] = other_ref[group * blocks + at]


def columns_of(update_ref, group):
    update = update_ref[group]
    return update.reshape(update.shape[0] * update.shape[1], update.shape[2])


def normaliser(update_ref, genes_total):
    exact = update_ref.dtype == jnp.float32
    gram = None
    for group in range(update_ref.shape[0]):
        update = columns_of(update_ref, group)
        part = lax.dot_general(
            update,
            update,
            (((1,), (1,)), ((), ())),
            precision=HIGHEST if exact else None,
            preferred_element_type=jnp.float32,
        )
        gram = part if gram is None else gram + part
    return inverse_factor(gram / genes_total)


def score(left, data_ref, groups):
    total = None
    for at, group in enumerate(groups):
        part = lax.dot_general(
            left(at),
            block(data_ref, group),
            (((1,), (1,)), ((), ())),
            preferred_element_type=jnp.float32,
        )
        total = part if total is None else total + part
    return total


def regroup_kernel(
    rows_of,
    data_any,
    dev_any,
    slot_any,
    weight_any,
    out_any,
    data_ref,
    link_ref,
    out_ref,
    data_sem,
    link_sem,
    out_sem,
):
    genes_here, cells = data_ref.shape
    parts, rows, padded = out_ref.shape
    slots, neighbours = link_ref.shape[1:]
    tile_cells = cells // slots
    share = max(16, rows_of)
    joined = share // rows_of
    whole = padded - LANES
    link_copies = [
        pltpu.make_async_copy(source, link_ref.at[at], link_sem.at[at])
        for at, source in enumerate((dev_any, slot_any, weight_any))
    ]
    tile_at = [pl.ds(tile * tile_cells, tile_cells) for tile in range(slots)]
    data_copies = [
        pltpu.make_async_copy(data_any.at[:, at], data_ref.at[:, at], data_sem.at[tile])
        for tile, at in enumerate(tile_at)
    ]
    for copy in link_copies + data_copies:
        copy.start()

    spread = (
        lax.broadcasted_iota(jnp.int32, (neighbours, cells), 0)
        == lax.broadcasted_iota(jnp.int32, (neighbours, cells), 1) % rows_of
    ).astype(jnp.float32)
    tile = lax.broadcasted_iota(jnp.int32, (slots, cells), 0)
    own_tile = tile == lax.broadcasted_iota(jnp.int32, (slots, cells), 1) // tile_cells
    row = lax.broadcasted_iota(jnp.int32, (padded - genes_here, cells), 0)
    links = jnp.zeros((padded - genes_here, cells), jnp.float32)
    for at, copy in enumerate(link_copies):
        copy.wait()
        wide = jnp.dot(
            link_ref[at].astype(jnp.float32), spread, preferred_element_type=jnp.float32
        )
        wide = jnp.sum(jnp.where(own_tile, wide, 0.0), axis=0, keepdims=True)
        links = jnp.where(row == at, wide, links)

    def turned(part):
        return part.T.astype(jnp.float32).reshape(parts, rows_of, part.shape[0])

    out_copies = []
    for first in range(0, slots, joined):
        main, rest = [], []
        for tile in range(first, first + joined):
            data_copies[tile].wait()
            at = slice(tile * tile_cells, (tile + 1) * tile_cells)
            main.append(turned(data_ref[:whole, at]))
            end = data_ref[whole:genes_here, at].astype(jnp.float32)
            end = jnp.concatenate([end, links[:, at]], axis=0)
            rest.append(turned(end.astype(jnp.bfloat16)))
        keep = slice(first * rows_of, first * rows_of + share)
        out_ref[:, keep, :whole] = jnp.concatenate(main, axis=1).astype(jnp.bfloat16)
        out_ref[:, keep, whole:] = jnp.concatenate(rest, axis=1).astype(jnp.bfloat16)
        keep = pl.ds(first * rows_of, share)
        out_copies.append(
            pltpu.make_async_copy(
                out_ref.at[:, keep], out_any.at[:, keep], out_sem.at[first // joined]
            )
        )
        out_copies[-1].start()
    for copy in out_copies:
        copy.wait()


def share_second(core, second, cut_ref, chunk, groups):
    width, cells = second.shape
    cores, blocks, tall = cut_ref.shape[:3]
    rows = cells * groups // (cores * blocks)
    tall = tall - chunk
    slabs = width // groups // tall
    lane = lax.broadcasted_iota(jnp.int32, (tall, LANES), 1) // rows - core * slabs
    for at in range(cells // LANES):
        wide = second[:, at * LANES : (at + 1) * LANES].astype(jnp.float32)
        for group in range(groups):
            for device in range(LANES // rows):
                share = jnp.zeros((tall, LANES), jnp.float32)
                for slab in range(slabs):
                    first_row = (group * slabs + slab) * tall
                    for turn in range(cores):
                        turned = pltpu.roll(
                            wide[first_row : first_row + tall],
                            (turn * slabs + slab - device) * rows % LANES,
                            1,
                        )
                        share = jnp.where((lane == slab) & (core == turn), turned, share)
                chip, to = divmod(at * (LANES // rows) + device, cores)
                cut_ref[to, chip * groups + group, chunk:] = share.astype(cut_ref.dtype)


def order_shares(arrived_ref, chunk, out_ref, groups, cores, slots):
    part_width, cells = out_ref.shape
    blocks, tall = arrived_ref.shape[:2]
    tall = tall - chunk
    parts = blocks * cores
    rows_of = cells // (slots * parts)
    rows = slots * rows_of
    slabs = part_width // tall
    together = LANES // rows_of
    lane = lax.broadcasted_iota(jnp.int32, (tall, LANES), 1) // rows_of
    for slab in range(slabs):
        for slot in range(slots):
            for first in range(0, parts, together):
                whole = jnp.zeros((tall, LANES), jnp.float32)
                for at in range(together):
                    chip, rest = divmod(first + at, cores * groups)
                    core, group = divmod(rest, groups)
                    source = (core * slabs + slab) * rows + slot * rows_of
                    share = arrived_ref[chip * groups + group, chunk:].astype(jnp.float32)
                    turned = pltpu.roll(share, (at * rows_of - source) % LANES, 1)
                    whole = jnp.where(lane == at, turned, whole)
                to = (slot * parts + first) * rows_of
                out_ref[slab * tall : (slab + 1) * tall, to : to + LANES] = whole.astype(
                    jnp.bfloat16
                )


def first_kernel(
    genes_here,
    slots,
    place_ref,
    data_ref,
    start_ref,
    mine_ref,
    other_ref,
    links_ref,
    degree_ref,
    cut_ref,
):
    devices, groups, rows, padded = data_ref.shape
    tiles = devices * slots
    core, own = place_ref[0], place_ref[1]
    packed = block(data_ref, 0)[:, padded - LANES :].astype(jnp.float32)
    offset = genes_here - (padded - LANES)
    links, degree = link_matrix(
        packed[:, offset : offset + 3], tiles, rows // slots, slots, rows // slots
    )
    links_ref[...] = links
    degree_ref[...] = degree
    order = [lax.rem(own + groups - shift, groups) for shift in range(groups)]
    scores = score(lambda shift: start_ref[shift], data_ref, order)
    scores = scores / math.sqrt(genes_here * groups)
    second = diffuse(scores, links, degree[:1])
    push_update(genes_here, data_ref, second, cut_ref)
    mine_ref[...] = cut_ref[core]
    other_ref[...] = cut_ref[1 - core]


def next_kernel(
    genes_here,
    place_ref,
    half_ref,
    rest_ref,
    data_ref,
    links_ref,
    degree_ref,
    mine_ref,
    other_ref,
    worst_ref,
    update_ref,
    cut_ref,
):
    core = place_ref[0]
    groups = data_ref.shape[1]
    chunk = half_ref.shape[1]
    genes_total = genes_here * groups
    pull_update(core, half_ref, rest_ref, update_ref)
    inverse, amplified = normaliser(update_ref, genes_total)
    worst_ref[...] = jnp.broadcast_to(amplified, worst_ref.shape)

    def apply(array):
        return jnp.dot(inverse, array, precision=HIGHEST, preferred_element_type=jnp.float32)

    if update_ref.dtype == jnp.float32:
        scores = score(
            lambda group: apply(columns_of(update_ref, group)).astype(jnp.bfloat16),
            data_ref,
            range(groups),
        )
    else:
        scores = apply(
            score(lambda group: columns_of(update_ref, group), data_ref, range(groups))
        )
    second = diffuse(scores / math.sqrt(genes_total), links_ref[...], degree_ref[:1])
    push_update(genes_here, data_ref, second, cut_ref)
    if cut_ref.shape[2] > chunk:
        share_second(core, second, cut_ref, chunk, groups)
    mine_ref[...] = cut_ref[core]
    other_ref[...] = cut_ref[1 - core]


def last_kernel(
    genes_here,
    slots,
    place_ref,
    half_ref,
    rest_ref,
    arrived_ref,
    *refs,
):
    *earlier, out_ref, smoothed_ref, good_ref, update_ref = refs
    core, own = place_ref[0], place_ref[1]
    groups, cores = update_ref.shape[:2]
    pull_update(core, half_ref, rest_ref, update_ref)
    genes_total = genes_here * groups
    inverse, amplified = normaliser(update_ref, genes_total)
    good = amplified <= AMPLIFIED
    for worst_ref in earlier:
        good = good & (worst_ref[:, :1] <= AMPLIFIED)
    good_ref[0] = jnp.min(good.astype(jnp.int32))
    mine = columns_of(update_ref, own).astype(jnp.float32)
    loadings = jnp.dot(inverse, mine, precision=HIGHEST, preferred_element_type=jnp.float32)
    out_ref[...] = loadings[:, :genes_here]
    order_shares(arrived_ref, half_ref.shape[1], smoothed_ref, groups, cores, slots)


def add_kernel(mine_ref, arrived_ref, out_ref):
    total = mine_ref[...].astype(jnp.float32) + arrived_ref[...].astype(jnp.float32)
    out_ref[...] = total.astype(out_ref.dtype)


def sum_kernel(chunks_ref, out_ref):
    parts = chunks_ref[:, : out_ref.shape[1]].astype(jnp.float32)
    total = jnp.sum(parts, axis=0).astype(out_ref.dtype)
    out_ref[...] = jnp.broadcast_to(total[None], out_ref.shape)


def like(array):
    return jax.ShapeDtypeStruct(array.shape, array.dtype)


def call(kernel, out_shape, scratch=(), scalars=0, arrays=0):
    in_specs = [pl.BlockSpec(memory_space=pltpu.SMEM)] * scalars
    in_specs += [pl.BlockSpec(memory_space=pltpu.VMEM)] * arrays
    return pl.pallas_call(
        kernel,
        out_shape=out_shape,
        in_specs=in_specs,
        out_specs=jax.tree.map(
            lambda leaf: pl.BlockSpec(memory_space=pltpu.VMEM if leaf.ndim > 1 else pltpu.SMEM),
            out_shape,
        ),
        scratch_shapes=list(scratch),
        compiler_params=pltpu.CompilerParams(vmem_limit_bytes=32 * 1024 * 1024),
    )


def by_cell(kept, data, start, link_dev, link_slot, link_weight):
    cores, groups = lax.axis_size("core"), lax.axis_size("genes")
    devices = lax.axis_size("chips") * cores
    parts = devices * groups
    blocks = parts // cores
    slots, neighbours = link_dev.shape
    genes_here, width = data.shape[1], start.shape[1]
    tile_cells = data.shape[0] // slots
    rows_of = tile_cells // parts
    rows = slots * rows_of
    padded = -(-genes_here // LANES) * LANES
    cells = devices * rows
    chunk = width // cores
    place = jnp.stack([lax.axis_index("core"), lax.axis_index("genes")]).astype(jnp.int32)

    def exchange(array):
        return lax.all_to_all(array, ("chips", "genes"), 0, 0, tiled=True)

    def swap(array):
        return lax.ppermute(array, "core", [(0, 1), (1, 0)])

    narrow = jnp.pad(start.astype(jnp.bfloat16).T, ((0, 0), (0, padded - genes_here)))
    starts = [narrow]
    for shift in range(1, groups):
        pairs = [(at, (at + shift) % groups) for at in range(groups)]
        starts.append(lax.ppermute(narrow, "genes", pairs))
    starts = jnp.stack(starts)
    moved = pl.pallas_call(
        functools.partial(regroup_kernel, rows_of),
        out_shape=jax.ShapeDtypeStruct((parts, rows, padded), jnp.bfloat16),
        in_specs=[pl.BlockSpec(memory_space=pl.ANY)] * 4,
        out_specs=pl.BlockSpec(memory_space=pl.ANY),
        scratch_shapes=[
            pltpu.VMEM((genes_here, slots * tile_cells), jnp.bfloat16),
            pltpu.VMEM((3, slots, neighbours), jnp.int32),
            pltpu.VMEM((parts, rows, padded), jnp.bfloat16),
            pltpu.SemaphoreType.DMA((slots,)),
            pltpu.SemaphoreType.DMA((3,)),
            pltpu.SemaphoreType.DMA((rows // max(16, rows_of),)),
        ],
        compiler_params=pltpu.CompilerParams(vmem_limit_bytes=60 * 1024 * 1024),
    )(data.T, link_dev, link_slot, link_weight)
    moved = lax.all_to_all(moved, ("chips", "core", "genes"), 0, 0, tiled=True)
    moved = moved.reshape(devices, groups, rows, padded)

    def cut(tall):
        return (
            jax.ShapeDtypeStruct((blocks, tall, LANES), kept),
            pltpu.VMEM((cores, blocks, tall, LANES), kept),
        )

    update = pltpu.VMEM((groups, cores, chunk, padded), kept)
    worst = jax.ShapeDtypeStruct((width, LANES), jnp.float32)
    earlier = []
    links = jax.ShapeDtypeStruct((cells, cells), jnp.bfloat16)
    degree = jax.ShapeDtypeStruct((8, cells), jnp.float32)

    def reduce(mine, other):
        return exchange(call(add_kernel, like(mine), arrays=2)(mine, swap(other)))

    def gather(arrived):
        half = exchange(call(sum_kernel, cut(chunk)[0], arrays=1)(arrived))
        return half, swap(half)

    share, scratch = cut(chunk)
    mine, other, links, degree = call(
        functools.partial(first_kernel, genes_here, slots),
        (share, share, links, degree),
        (scratch,),
        scalars=1,
        arrays=2,
    )(place, moved, starts)
    arrived = reduce(mine, other)
    for step in range(1, ITERS):
        share, scratch = cut(chunk + 16 if step == ITERS - 1 else chunk)
        mine, other, amplified = call(
            functools.partial(next_kernel, genes_here),
            (share, share, worst),
            (update, scratch),
            scalars=1,
            arrays=5,
        )(place, *gather(arrived), moved, links, degree)
        earlier.append(amplified)
        arrived = reduce(mine, other)
    loadings, smoothed, good = call(
        functools.partial(last_kernel, genes_here, slots),
        (
            jax.ShapeDtypeStruct((width, genes_here), jnp.float32),
            jax.ShapeDtypeStruct((width // groups, slots * tile_cells), jnp.bfloat16),
            jax.ShapeDtypeStruct((1,), jnp.int32),
        ),
        (update,),
        scalars=1,
        arrays=3 + len(earlier),
    )(place, *gather(arrived), arrived, *earlier)
    return loadings.T, smoothed, good[0] == 1


def by_condition(*arguments):
    loadings, smoothed, good = by_cell(jnp.bfloat16, *arguments)
    return lax.cond(
        good,
        lambda *_: (loadings, smoothed),
        lambda *again: by_cell(jnp.float32, *again)[:2],
        *arguments,
    )


def by_tile(data, start, link_dev, link_slot, link_weight):
    devices = lax.axis_size("cells")
    groups = lax.axis_size("genes")
    tiles_here, neighbours = link_dev.shape
    tile_cells = data.shape[0] // tiles_here
    genes_total = data.shape[1] * groups
    width = start.shape[1]
    part_width = width // groups
    capacity = max(2, 2 * tiles_here * neighbours // devices)
    slot_count = devices * capacity
    links = tiles_here * neighbours
    columns = part_width * tile_cells
    flat_dev = link_dev.reshape(links)
    flat_slot = link_slot.reshape(links)
    flat_weight = link_weight.reshape(links)
    dev_hits = (flat_dev[:, None] == jnp.arange(devices, dtype=jnp.int32)[None, :]).astype(
        jnp.int32
    )
    earlier = jnp.cumsum(dev_hits, axis=0) - dev_hits
    ranking = jnp.sum(earlier * dev_hits, axis=1)
    position = flat_dev * capacity + ranking
    placed = (position[:, None] == jnp.arange(slot_count, dtype=jnp.int32)[None, :]).astype(
        jnp.int32
    )
    wanted = jnp.sum(placed * (flat_slot + 1)[:, None], axis=0).reshape(devices, capacity)
    wanted_weight = jnp.sum(placed * flat_weight[:, None], axis=0).reshape(devices, capacity)
    asked_pair = (
        lax.all_to_all(wanted, "cells", split_axis=0, concat_axis=0, tiled=True),
        lax.all_to_all(wanted_weight, "cells", split_axis=0, concat_axis=0, tiled=True),
    )
    asked = asked_pair[0].reshape(slot_count)
    asked_weight = asked_pair[1].reshape(slot_count)
    tile_ids = jnp.arange(tiles_here, dtype=jnp.int32)
    serve_match = ((asked - 1)[:, None] == tile_ids[None, :]).astype(jnp.int32)
    serve = serve_match.astype(jnp.bfloat16)
    collect = (serve_match * asked_weight[:, None]).T.astype(jnp.bfloat16)
    placed_tiles = placed.reshape(tiles_here, neighbours, slot_count)
    link_matrix = jnp.sum(placed_tiles * link_weight[:, :, None], axis=1).astype(jnp.bfloat16)
    sender = jnp.sum(placed_tiles, axis=1).astype(jnp.bfloat16)
    degree = (self_weight + jnp.sum(link_weight, axis=1).astype(jnp.float32))[:, None]
    loadings = start
    smoothed = jnp.zeros((part_width, tiles_here * tile_cells), jnp.bfloat16)
    for step in range(ITERS):
        narrow = loadings.astype(jnp.bfloat16)
        partial_scores = lax.dot_general(
            narrow, data, (((0,), (1,)), ((), ())), preferred_element_type=jnp.float32
        )
        summed = lax.psum(partial_scores.astype(jnp.bfloat16), "genes").astype(jnp.float32)
        mine = lax.dynamic_slice_in_dim(summed, lax.axis_index("genes") * part_width, part_width, 0)
        scores = (mine / math.sqrt(genes_total)).astype(jnp.bfloat16)
        tiles = (
            scores.reshape(part_width, tiles_here, tile_cells)
            .transpose(1, 0, 2)
            .reshape(tiles_here, columns)
        )
        outgoing = jnp.dot(serve, tiles, preferred_element_type=jnp.float32).astype(jnp.bfloat16)
        linked = jnp.dot(
            link_matrix,
            lax.all_to_all(
                outgoing.reshape(devices, capacity, columns),
                "cells",
                split_axis=0,
                concat_axis=0,
                tiled=True,
            ).reshape(slot_count, -1),
            preferred_element_type=jnp.float32,
        )
        first = lax.optimization_barrier(
            ((self_weight * tiles.astype(jnp.float32) + linked) / degree).astype(jnp.bfloat16)
        )
        spread = lax.optimization_barrier(
            (self_weight * first.astype(jnp.float32) / degree).astype(jnp.bfloat16)
        )
        returning = lax.dot_general(
            sender, spread, (((0,), (0,)), ((), ())), preferred_element_type=jnp.float32
        ).astype(jnp.bfloat16)
        pushed = jnp.dot(
            collect,
            lax.all_to_all(
                returning.reshape(devices, capacity, columns),
                "cells",
                split_axis=0,
                concat_axis=0,
                tiled=True,
            ).reshape(slot_count, -1),
            preferred_element_type=jnp.float32,
        )
        second = (self_weight * spread.astype(jnp.float32) + pushed).astype(jnp.bfloat16)
        smoothed = (
            second.reshape(tiles_here, part_width, tile_cells)
            .transpose(1, 0, 2)
            .reshape(part_width, tiles_here * tile_cells)
        )
        update = lax.dot_general(
            data,
            lax.all_gather(smoothed, "genes", axis=0, tiled=True),
            (((0,), (1,)), ((), ())),
            preferred_element_type=jnp.float32,
        )
        update = lax.psum(update, "cells")
        gram_part = jnp.dot(
            update.T, update, precision=lax.Precision.HIGHEST, preferred_element_type=jnp.float32
        )
        gram = lax.psum(gram_part, "genes") / genes_total
        factor = jnp.linalg.cholesky(gram)
        loadings = lax.linalg.triangular_solve(
            factor, update, left_side=False, lower=True, transpose_a=True
        )
    return (loadings, smoothed)


def fits_by_cell(mesh, data, start, link_dev):
    groups, parts = mesh.shape["genes"], mesh.size
    slots, neighbours = link_dev.shape[0] * groups // parts, link_dev.shape[1]
    tile_cells = data.shape[0] // link_dev.shape[0]
    genes_here, width = data.shape[1] // groups, start.shape[1]
    padded = -(-genes_here // LANES) * LANES
    rows_of = tile_cells // parts
    rows = slots * rows_of
    return (
        mesh.shape["cells"] % 2 == 0
        and tile_cells % (8 * parts) == 0
        and neighbours <= rows_of
        and rows % 16 == 0
        and rows % max(16, rows_of) == 0
        and LANES % rows == 0
        and genes_here % 8 == 0
        and padded - genes_here >= 3
        and groups * padded // LANES == parts // 2
        and width % (32 * groups) == 0
        and width // groups // 16 * rows * 2 <= LANES
    )


def solution(mesh):
    chips = Mesh(
        mesh.devices.reshape(mesh.shape["cells"] // 2, 2, mesh.shape["genes"]),
        ("chips", "core", "genes"),
    )

    def program(data, start, link_dev, link_slot, link_weight):
        if fits_by_cell(mesh, data, start, link_dev):
            way, over, cells = by_condition, chips, ("chips", "core")
        else:
            way, over, cells = by_tile, mesh, "cells"
        return jax.shard_map(
            way,
            mesh=over,
            in_specs=(P(cells, "genes"), P("genes", None)) + (P(cells, None),) * 3,
            out_specs=(P("genes", None), P("genes", cells)),
            check_vma=False,
        )(data, start, link_dev, link_slot, link_weight)

    return program
```

```python
import functools
import math

import jax
import jax.numpy as jnp
from jax import lax
from jax.experimental import pallas as pl
from jax.experimental.pallas import tpu as pltpu
from jax.sharding import Mesh
from jax.sharding import PartitionSpec as P

ITERS = 3
LANES = 128
AMPLIFIED = 4.0

self_weight = 8.0
HIGHEST = lax.Precision.HIGHEST


def inverse_factor(gram):
    width = gram.shape[0]
    rows = lax.broadcasted_iota(jnp.int32, (width, width), 0)
    cols = lax.broadcasted_iota(jnp.int32, (width, width), 1)
    diagonal = jnp.where(rows == cols, gram, 0.0)
    down = lax.rsqrt(jnp.sum(diagonal, axis=1, keepdims=True))
    along = lax.rsqrt(jnp.sum(diagonal, axis=0, keepdims=True))
    scaled = gram * down * along
    state = jnp.concatenate([(rows == cols).astype(jnp.float32), scaled], axis=1)
    strips = [state[at : at + 8] for at in range(0, width, 8)]
    shape = strips[0].shape
    place = lax.broadcasted_iota(jnp.int32, shape, 0)
    done = []
    for panel, strip in enumerate(strips):
        base = width + 8 * panel

        def column(of, j):
            return jnp.broadcast_to(of[:, base + j : base + j + 1], shape)

        columns = [column(strip, j) for j in range(8)]
        core = {
            (i, j): jnp.broadcast_to(columns[j][i : i + 1], shape)
            for j in range(8)
            for i in range(j, 8)
        }
        lines = [jnp.broadcast_to(strip[j : j + 1], shape) for j in range(8)]
        below = range(panel + 1, len(strips))
        rest = {(at, j): column(strips[at], j) for at in below for j in range(8)}
        for j in range(0, 8, 2):
            a, b, c = core[j, j], core[j + 1, j], core[j + 1, j + 1]
            area = a * c - b * b
            over = 1.0 / a
            step = b * over
            later = a * (1.0 / area)
            left = {i: core[i, j + 1] - step * core[i, j] for i in range(j + 2, 8)}
            lines[j + 1] -= step * lines[j]
            core[j + 1, j + 1] = area * over
            for i in range(j + 2, 8):
                first, second = core[i, j] * over, left[i] * later
                for m in range(j + 2, i + 1):
                    core[i, m] -= first * core[m, j] + second * left[m]
                lines[i] -= first * lines[j] + second * lines[j + 1]
            for at in below:
                first = rest[at, j] * over
                second = (rest[at, j + 1] - step * rest[at, j]) * later
                for m in range(j + 2, 8):
                    rest[at, m] -= first * core[m, j] + second * left[m]
                strips[at] -= first * lines[j] + second * lines[j + 1]
        final = lines[0] * lax.rsqrt(core[0, 0])
        for j in range(1, 8):
            final = jnp.where(place == j, lines[j] * lax.rsqrt(core[j, j]), final)
        done.append(final)
    inverse = jnp.concatenate(done, axis=0)[:, :width]
    return inverse * along, jnp.sum(inverse * inverse, axis=1, keepdims=True)


def link_matrix(packed, tiles, neighbours, slots, rows_of):
    own_dev, own_slot, own_weight = packed[:, 0:1], packed[:, 1:2], packed[:, 2:3]
    target = own_dev * slots + own_slot
    lane = lax.broadcasted_iota(jnp.int32, (tiles * neighbours, tiles), 1).astype(jnp.float32)
    hits = jnp.where(lane == target, own_weight, 0.0)
    weights = jnp.sum(hits.reshape(tiles, neighbours, tiles), axis=1)
    tile_row = lax.broadcasted_iota(jnp.int32, (tiles, tiles), 0)
    tile_col = lax.broadcasted_iota(jnp.int32, (tiles, tiles), 1)
    weights = weights + jnp.where(tile_row == tile_col, self_weight, 0.0)
    cells = tiles * rows_of
    tile_of = lax.broadcasted_iota(jnp.int32, (cells, tiles), 0) // rows_of
    expand = (tile_of == lax.broadcasted_iota(jnp.int32, (cells, tiles), 1)).astype(jnp.bfloat16)
    tall = jnp.dot(expand, weights.astype(jnp.bfloat16), preferred_element_type=jnp.float32)
    full = lax.dot_general(
        tall.astype(jnp.bfloat16),
        expand,
        (((1,), (1,)), ((), ())),
        preferred_element_type=jnp.float32,
    )
    same = (
        lax.broadcasted_iota(jnp.int32, (cells, cells), 0) % rows_of
        == lax.broadcasted_iota(jnp.int32, (cells, cells), 1) % rows_of
    )
    full = jnp.where(same, full, 0.0).astype(jnp.bfloat16)
    ones = jnp.ones((8, cells), jnp.bfloat16)
    degree = lax.dot_general(
        ones, full, (((1,), (1,)), ((), ())), preferred_element_type=jnp.float32
    )
    return full, degree


def diffuse(scores, links, degree):
    scores = scores.astype(jnp.bfloat16)
    total = lax.dot_general(
        scores, links, (((1,), (1,)), ((), ())), preferred_element_type=jnp.float32
    )
    first = (total / degree).astype(jnp.bfloat16).astype(jnp.float32)
    spread = (self_weight * first / degree).astype(jnp.bfloat16)
    return jnp.dot(spread, links, preferred_element_type=jnp.float32).astype(jnp.bfloat16)


def block(data_ref, group):
    part = data_ref[:, group]
    return part.reshape(part.shape[0] * part.shape[1], part.shape[2])


def push_update(core, genes_here, data_ref, second, mine_ref, other_ref):
    groups, padded = data_ref.shape[1], data_ref.shape[3]
    chunk = second.shape[0] // 2
    blocks = padded // LANES
    for group in range(groups):
        update = jnp.dot(second, block(data_ref, group), preferred_element_type=jnp.float32)
        lane = lax.broadcasted_iota(jnp.int32, update.shape, 1)
        update = jnp.where(lane < genes_here, update, 0.0)
        upper, lower = update[:chunk], update[chunk:]
        mine = jnp.where(core == 0, upper, lower).astype(mine_ref.dtype)
        other = jnp.where(core == 0, lower, upper).astype(mine_ref.dtype)
        for at in range(blocks):
            lanes = slice(at * LANES, (at + 1) * LANES)
            mine_ref[group * blocks + at, :chunk] = mine[:, lanes]
            other_ref[group * blocks + at, :chunk] = other[:, lanes]


def pull_update(core, mine_ref, other_ref, update_ref):
    groups, _, _, padded = update_ref.shape
    blocks = padded // LANES
    for group in range(groups):
        for at in range(blocks):
            lanes = slice(at * LANES, (at + 1) * LANES)
            update_ref[group, core, :, lanes] = mine_ref[group * blocks + at]
            update_ref[group, 1 - core, :, lanes] = other_ref[group * blocks + at]


def columns_of(update_ref, group):
    update = update_ref[group]
    return update.reshape(update.shape[0] * update.shape[1], update.shape[2])


def normaliser(update_ref, genes_total):
    exact = update_ref.dtype == jnp.float32
    gram = None
    for group in range(update_ref.shape[0]):
        update = columns_of(update_ref, group)
        part = lax.dot_general(
            update,
            update,
            (((1,), (1,)), ((), ())),
            precision=HIGHEST if exact else None,
            preferred_element_type=jnp.float32,
        )
        gram = part if gram is None else gram + part
    return inverse_factor(gram / genes_total)


def score(left, data_ref, groups):
    total = None
    for at, group in enumerate(groups):
        part = lax.dot_general(
            left(at),
            block(data_ref, group),
            (((1,), (1,)), ((), ())),
            preferred_element_type=jnp.float32,
        )
        total = part if total is None else total + part
    return total


def regroup_kernel(
    rows_of,
    data_any,
    dev_any,
    slot_any,
    weight_any,
    out_any,
    data_ref,
    link_ref,
    out_ref,
    data_sem,
    link_sem,
    out_sem,
):
    genes_here, cells = data_ref.shape
    parts, rows, padded = out_ref.shape
    slots, neighbours = link_ref.shape[1:]
    tile_cells = cells // slots
    share = max(16, rows_of)
    joined = share // rows_of
    whole = padded - LANES
    link_copies = [
        pltpu.make_async_copy(source, link_ref.at[at], link_sem.at[at])
        for at, source in enumerate((dev_any, slot_any, weight_any))
    ]
    tile_at = [pl.ds(tile * tile_cells, tile_cells) for tile in range(slots)]
    data_copies = [
        pltpu.make_async_copy(data_any.at[:, at], data_ref.at[:, at], data_sem.at[tile])
        for tile, at in enumerate(tile_at)
    ]
    for copy in data_copies[:1] + link_copies + data_copies[1:]:
        copy.start()

    def wide_links():
        spread = (
            lax.broadcasted_iota(jnp.int32, (neighbours, cells), 0)
            == lax.broadcasted_iota(jnp.int32, (neighbours, cells), 1) % rows_of
        ).astype(jnp.float32)
        tile = lax.broadcasted_iota(jnp.int32, (slots, cells), 0)
        own_tile = tile == lax.broadcasted_iota(jnp.int32, (slots, cells), 1) // tile_cells
        row = lax.broadcasted_iota(jnp.int32, (padded - genes_here, cells), 0)
        links = jnp.zeros((padded - genes_here, cells), jnp.float32)
        for at, copy in enumerate(link_copies):
            copy.wait()
            wide = jnp.dot(
                link_ref[at].astype(jnp.float32), spread, preferred_element_type=jnp.float32
            )
            wide = jnp.sum(jnp.where(own_tile, wide, 0.0), axis=0, keepdims=True)
            links = jnp.where(row == at, wide, links)
        return links

    def turned(part):
        return part.T.astype(jnp.float32).reshape(parts, rows_of, part.shape[0])

    out_copies, links = [], None
    for first in range(0, slots, joined):
        main, rest = [], []
        for tile in range(first, first + joined):
            data_copies[tile].wait()
            at = slice(tile * tile_cells, (tile + 1) * tile_cells)
            main.append(turned(data_ref[:whole, at]))
            links = wide_links() if links is None else links
            end = data_ref[whole:genes_here, at].astype(jnp.float32)
            end = jnp.concatenate([end, links[:, at]], axis=0)
            rest.append(turned(end.astype(jnp.bfloat16)))
        keep = slice(first * rows_of, first * rows_of + share)
        out_ref[:, keep, :whole] = jnp.concatenate(main, axis=1).astype(jnp.bfloat16)
        out_ref[:, keep, whole:] = jnp.concatenate(rest, axis=1).astype(jnp.bfloat16)
        keep = pl.ds(first * rows_of, share)
        out_copies.append(
            pltpu.make_async_copy(
                out_ref.at[:, keep], out_any.at[:, keep], out_sem.at[first // joined]
            )
        )
        out_copies[-1].start()
    for copy in out_copies:
        copy.wait()


def share_second(core, second, mine_ref, other_ref, chunk, groups):
    width, cells = second.shape
    blocks, tall = mine_ref.shape[:2]
    cores = 2
    rows = cells * groups // (cores * blocks)
    tall = tall - chunk
    slabs = width // groups // tall
    lane = lax.broadcasted_iota(jnp.int32, (tall, LANES), 1) // rows - core * slabs
    for at in range(cells // LANES):
        wide = second[:, at * LANES : (at + 1) * LANES].astype(jnp.float32)
        shares = []
        for group in range(groups):
            for device in range(LANES // rows):
                share = jnp.zeros((tall, LANES), jnp.float32)
                for slab in range(slabs):
                    first_row = (group * slabs + slab) * tall
                    for turn in range(cores):
                        turned = pltpu.roll(
                            wide[first_row : first_row + tall],
                            (turn * slabs + slab - device) * rows % LANES,
                            1,
                        )
                        share = jnp.where((lane == slab) & (core == turn), turned, share)
                shares.append(share.astype(mine_ref.dtype))
        for device in range(0, LANES // rows, cores):
            chip = (at * (LANES // rows) + device) // cores
            for group in range(groups):
                first = shares[group * (LANES // rows) + device]
                second_core = shares[group * (LANES // rows) + device + 1]
                to = chip * groups + group
                mine_ref[to, chunk:] = jnp.where(core == 0, first, second_core)
                other_ref[to, chunk:] = jnp.where(core == 0, second_core, first)


def order_shares(arrived_ref, chunk, out_ref, groups, cores, slots):
    part_width, cells = out_ref.shape
    blocks, tall = arrived_ref.shape[:2]
    tall = tall - chunk
    parts = blocks * cores
    rows_of = cells // (slots * parts)
    rows = slots * rows_of
    slabs = part_width // tall
    together = LANES // rows_of
    lane = lax.broadcasted_iota(jnp.int32, (tall, LANES), 1) // rows_of
    for slab in range(slabs):
        for slot in range(slots):
            for first in range(0, parts, together):
                whole = jnp.zeros((tall, LANES), jnp.float32)
                for at in range(together):
                    chip, rest = divmod(first + at, cores * groups)
                    core, group = divmod(rest, groups)
                    source = (core * slabs + slab) * rows + slot * rows_of
                    share = arrived_ref[chip * groups + group, chunk:].astype(jnp.float32)
                    turned = pltpu.roll(share, (at * rows_of - source) % LANES, 1)
                    whole = jnp.where(lane == at, turned, whole)
                to = (slot * parts + first) * rows_of
                out_ref[slab * tall : (slab + 1) * tall, to : to + LANES] = whole.astype(
                    jnp.bfloat16
                )


def first_kernel(
    genes_here,
    slots,
    place_ref,
    data_ref,
    start_ref,
    mine_ref,
    other_ref,
    links_ref,
    degree_ref,
):
    devices, groups, rows, padded = data_ref.shape
    tiles = devices * slots
    core, own = place_ref[0], place_ref[1]
    packed = block(data_ref, 0)[:, padded - LANES :].astype(jnp.float32)
    offset = genes_here - (padded - LANES)
    links, degree = link_matrix(
        packed[:, offset : offset + 3], tiles, rows // slots, slots, rows // slots
    )
    links_ref[...] = links
    degree_ref[...] = degree
    order = [lax.rem(own + groups - shift, groups) for shift in range(groups)]
    scores = score(lambda shift: start_ref[shift], data_ref, order)
    scores = scores / math.sqrt(genes_here * groups)
    second = diffuse(scores, links, degree[:1])
    push_update(core, genes_here, data_ref, second, mine_ref, other_ref)


def next_kernel(
    genes_here,
    place_ref,
    half_ref,
    rest_ref,
    data_ref,
    links_ref,
    degree_ref,
    mine_ref,
    other_ref,
    worst_ref,
    update_ref,
):
    core = place_ref[0]
    groups = data_ref.shape[1]
    chunk = half_ref.shape[1]
    genes_total = genes_here * groups
    pull_update(core, half_ref, rest_ref, update_ref)
    inverse, amplified = normaliser(update_ref, genes_total)
    worst_ref[...] = jnp.broadcast_to(amplified, worst_ref.shape)

    def apply(array):
        return jnp.dot(inverse, array, precision=HIGHEST, preferred_element_type=jnp.float32)

    if update_ref.dtype == jnp.float32:
        scores = score(
            lambda group: apply(columns_of(update_ref, group)).astype(jnp.bfloat16),
            data_ref,
            range(groups),
        )
    else:
        scores = apply(
            score(lambda group: columns_of(update_ref, group), data_ref, range(groups))
        )
    second = diffuse(scores / math.sqrt(genes_total), links_ref[...], degree_ref[:1])
    push_update(core, genes_here, data_ref, second, mine_ref, other_ref)
    if mine_ref.shape[1] > chunk:
        share_second(core, second, mine_ref, other_ref, chunk, groups)


def last_kernel(
    genes_here,
    slots,
    place_ref,
    half_ref,
    rest_ref,
    arrived_ref,
    *refs,
):
    *earlier, out_ref, smoothed_ref, good_ref, update_ref = refs
    core, own = place_ref[0], place_ref[1]
    groups, cores = update_ref.shape[:2]
    pull_update(core, half_ref, rest_ref, update_ref)
    genes_total = genes_here * groups
    inverse, amplified = normaliser(update_ref, genes_total)
    good = amplified <= AMPLIFIED
    for worst_ref in earlier:
        good = good & (worst_ref[:, :1] <= AMPLIFIED)
    good_ref[0] = jnp.min(good.astype(jnp.int32))
    mine = columns_of(update_ref, own).astype(jnp.float32)
    loadings = jnp.dot(inverse, mine, precision=HIGHEST, preferred_element_type=jnp.float32)
    out_ref[...] = loadings[:, :genes_here]
    order_shares(arrived_ref, half_ref.shape[1], smoothed_ref, groups, cores, slots)


def add_kernel(mine_ref, arrived_ref, out_ref):
    total = mine_ref[...].astype(jnp.float32) + arrived_ref[...].astype(jnp.float32)
    out_ref[...] = total.astype(out_ref.dtype)


def sum_kernel(chunks_ref, out_ref):
    parts = chunks_ref[:, : out_ref.shape[1]].astype(jnp.float32)
    total = jnp.sum(parts, axis=0).astype(out_ref.dtype)
    out_ref[...] = jnp.broadcast_to(total[None], out_ref.shape)


def like(array):
    return jax.ShapeDtypeStruct(array.shape, array.dtype)


def call(kernel, out_shape, scratch=(), scalars=0, arrays=0):
    in_specs = [pl.BlockSpec(memory_space=pltpu.SMEM)] * scalars
    in_specs += [pl.BlockSpec(memory_space=pltpu.VMEM)] * arrays
    return pl.pallas_call(
        kernel,
        out_shape=out_shape,
        in_specs=in_specs,
        out_specs=jax.tree.map(
            lambda leaf: pl.BlockSpec(memory_space=pltpu.VMEM if leaf.ndim > 1 else pltpu.SMEM),
            out_shape,
        ),
        scratch_shapes=list(scratch),
        compiler_params=pltpu.CompilerParams(vmem_limit_bytes=32 * 1024 * 1024),
    )


def by_cell(kept, data, start, link_dev, link_slot, link_weight):
    cores, groups = lax.axis_size("core"), lax.axis_size("genes")
    devices = lax.axis_size("chips") * cores
    parts = devices * groups
    blocks = parts // cores
    slots, neighbours = link_dev.shape
    genes_here, width = data.shape[1], start.shape[1]
    tile_cells = data.shape[0] // slots
    rows_of = tile_cells // parts
    rows = slots * rows_of
    padded = -(-genes_here // LANES) * LANES
    cells = devices * rows
    chunk = width // cores
    place = jnp.stack([lax.axis_index("core"), lax.axis_index("genes")]).astype(jnp.int32)

    def exchange(array):
        return lax.all_to_all(array, ("chips", "genes"), 0, 0, tiled=True)

    def swap(array):
        return lax.ppermute(array, "core", [(0, 1), (1, 0)])

    narrow = jnp.pad(start.astype(jnp.bfloat16).T, ((0, 0), (0, padded - genes_here)))
    starts = [narrow]
    for shift in range(1, groups):
        pairs = [(at, (at + shift) % groups) for at in range(groups)]
        starts.append(lax.ppermute(narrow, "genes", pairs))
    starts = jnp.stack(starts)
    moved = pl.pallas_call(
        functools.partial(regroup_kernel, rows_of),
        out_shape=jax.ShapeDtypeStruct((parts, rows, padded), jnp.bfloat16),
        in_specs=[pl.BlockSpec(memory_space=pl.ANY)] * 4,
        out_specs=pl.BlockSpec(memory_space=pl.ANY),
        scratch_shapes=[
            pltpu.VMEM((genes_here, slots * tile_cells), jnp.bfloat16),
            pltpu.VMEM((3, slots, neighbours), jnp.int32),
            pltpu.VMEM((parts, rows, padded), jnp.bfloat16),
            pltpu.SemaphoreType.DMA((slots,)),
            pltpu.SemaphoreType.DMA((3,)),
            pltpu.SemaphoreType.DMA((rows // max(16, rows_of),)),
        ],
        compiler_params=pltpu.CompilerParams(vmem_limit_bytes=60 * 1024 * 1024),
    )(data.T, link_dev, link_slot, link_weight)
    moved = lax.all_to_all(moved, ("chips", "core", "genes"), 0, 0, tiled=True)
    moved = moved.reshape(devices, groups, rows, padded)

    def cut(tall):
        return jax.ShapeDtypeStruct((blocks, tall, LANES), kept)

    update = pltpu.VMEM((groups, cores, chunk, padded), kept)
    worst = jax.ShapeDtypeStruct((width, LANES), jnp.float32)
    earlier = []
    links = jax.ShapeDtypeStruct((cells, cells), jnp.bfloat16)
    degree = jax.ShapeDtypeStruct((8, cells), jnp.float32)

    def reduce(mine, other):
        return exchange(call(add_kernel, like(mine), arrays=2)(mine, swap(other)))

    def gather(arrived):
        half = exchange(call(sum_kernel, cut(chunk), arrays=1)(arrived))
        return half, swap(half)

    share = cut(chunk)
    mine, other, links, degree = call(
        functools.partial(first_kernel, genes_here, slots),
        (share, share, links, degree),
        scalars=1,
        arrays=2,
    )(place, moved, starts)
    arrived = reduce(mine, other)
    for step in range(1, ITERS):
        share = cut(chunk + 16 if step == ITERS - 1 else chunk)
        mine, other, amplified = call(
            functools.partial(next_kernel, genes_here),
            (share, share, worst),
            (update,),
            scalars=1,
            arrays=5,
        )(place, *gather(arrived), moved, links, degree)
        earlier.append(amplified)
        arrived = reduce(mine, other)
    loadings, smoothed, good = call(
        functools.partial(last_kernel, genes_here, slots),
        (
            jax.ShapeDtypeStruct((width, genes_here), jnp.float32),
            jax.ShapeDtypeStruct((width // groups, slots * tile_cells), jnp.bfloat16),
            jax.ShapeDtypeStruct((1,), jnp.int32),
        ),
        (update,),
        scalars=1,
        arrays=3 + len(earlier),
    )(place, *gather(arrived), arrived, *earlier)
    return loadings.T, smoothed, good[0] == 1


def by_condition(*arguments):
    loadings, smoothed, good = by_cell(jnp.bfloat16, *arguments)
    return lax.cond(
        good,
        lambda *_: (loadings, smoothed),
        lambda *again: by_cell(jnp.float32, *again)[:2],
        *arguments,
    )


def by_tile(data, start, link_dev, link_slot, link_weight):
    devices = lax.axis_size("cells")
    groups = lax.axis_size("genes")
    tiles_here, neighbours = link_dev.shape
    tile_cells = data.shape[0] // tiles_here
    genes_total = data.shape[1] * groups
    width = start.shape[1]
    part_width = width // groups
    capacity = max(2, 2 * tiles_here * neighbours // devices)
    slot_count = devices * capacity
    links = tiles_here * neighbours
    columns = part_width * tile_cells
    flat_dev = link_dev.reshape(links)
    flat_slot = link_slot.reshape(links)
    flat_weight = link_weight.reshape(links)
    dev_hits = (flat_dev[:, None] == jnp.arange(devices, dtype=jnp.int32)[None, :]).astype(
        jnp.int32
    )
    earlier = jnp.cumsum(dev_hits, axis=0) - dev_hits
    ranking = jnp.sum(earlier * dev_hits, axis=1)
    position = flat_dev * capacity + ranking
    placed = (position[:, None] == jnp.arange(slot_count, dtype=jnp.int32)[None, :]).astype(
        jnp.int32
    )
    wanted = jnp.sum(placed * (flat_slot + 1)[:, None], axis=0).reshape(devices, capacity)
    wanted_weight = jnp.sum(placed * flat_weight[:, None], axis=0).reshape(devices, capacity)
    asked_pair = (
        lax.all_to_all(wanted, "cells", split_axis=0, concat_axis=0, tiled=True),
        lax.all_to_all(wanted_weight, "cells", split_axis=0, concat_axis=0, tiled=True),
    )
    asked = asked_pair[0].reshape(slot_count)
    asked_weight = asked_pair[1].reshape(slot_count)
    tile_ids = jnp.arange(tiles_here, dtype=jnp.int32)
    serve_match = ((asked - 1)[:, None] == tile_ids[None, :]).astype(jnp.int32)
    serve = serve_match.astype(jnp.bfloat16)
    collect = (serve_match * asked_weight[:, None]).T.astype(jnp.bfloat16)
    placed_tiles = placed.reshape(tiles_here, neighbours, slot_count)
    link_matrix = jnp.sum(placed_tiles * link_weight[:, :, None], axis=1).astype(jnp.bfloat16)
    sender = jnp.sum(placed_tiles, axis=1).astype(jnp.bfloat16)
    degree = (self_weight + jnp.sum(link_weight, axis=1).astype(jnp.float32))[:, None]
    loadings = start
    smoothed = jnp.zeros((part_width, tiles_here * tile_cells), jnp.bfloat16)
    for step in range(ITERS):
        narrow = loadings.astype(jnp.bfloat16)
        partial_scores = lax.dot_general(
            narrow, data, (((0,), (1,)), ((), ())), preferred_element_type=jnp.float32
        )
        summed = lax.psum(partial_scores.astype(jnp.bfloat16), "genes").astype(jnp.float32)
        mine = lax.dynamic_slice_in_dim(summed, lax.axis_index("genes") * part_width, part_width, 0)
        scores = (mine / math.sqrt(genes_total)).astype(jnp.bfloat16)
        tiles = (
            scores.reshape(part_width, tiles_here, tile_cells)
            .transpose(1, 0, 2)
            .reshape(tiles_here, columns)
        )
        outgoing = jnp.dot(serve, tiles, preferred_element_type=jnp.float32).astype(jnp.bfloat16)
        linked = jnp.dot(
            link_matrix,
            lax.all_to_all(
                outgoing.reshape(devices, capacity, columns),
                "cells",
                split_axis=0,
                concat_axis=0,
                tiled=True,
            ).reshape(slot_count, -1),
            preferred_element_type=jnp.float32,
        )
        first = lax.optimization_barrier(
            ((self_weight * tiles.astype(jnp.float32) + linked) / degree).astype(jnp.bfloat16)
        )
        spread = lax.optimization_barrier(
            (self_weight * first.astype(jnp.float32) / degree).astype(jnp.bfloat16)
        )
        returning = lax.dot_general(
            sender, spread, (((0,), (0,)), ((), ())), preferred_element_type=jnp.float32
        ).astype(jnp.bfloat16)
        pushed = jnp.dot(
            collect,
            lax.all_to_all(
                returning.reshape(devices, capacity, columns),
                "cells",
                split_axis=0,
                concat_axis=0,
                tiled=True,
            ).reshape(slot_count, -1),
            preferred_element_type=jnp.float32,
        )
        second = (self_weight * spread.astype(jnp.float32) + pushed).astype(jnp.bfloat16)
        smoothed = (
            second.reshape(tiles_here, part_width, tile_cells)
            .transpose(1, 0, 2)
            .reshape(part_width, tiles_here * tile_cells)
        )
        update = lax.dot_general(
            data,
            lax.all_gather(smoothed, "genes", axis=0, tiled=True),
            (((0,), (1,)), ((), ())),
            preferred_element_type=jnp.float32,
        )
        update = lax.psum(update, "cells")
        gram_part = jnp.dot(
            update.T, update, precision=lax.Precision.HIGHEST, preferred_element_type=jnp.float32
        )
        gram = lax.psum(gram_part, "genes") / genes_total
        factor = jnp.linalg.cholesky(gram)
        loadings = lax.linalg.triangular_solve(
            factor, update, left_side=False, lower=True, transpose_a=True
        )
    return (loadings, smoothed)


def fits_by_cell(mesh, data, start, link_dev):
    groups, parts = mesh.shape["genes"], mesh.size
    slots, neighbours = link_dev.shape[0] * groups // parts, link_dev.shape[1]
    tile_cells = data.shape[0] // link_dev.shape[0]
    genes_here, width = data.shape[1] // groups, start.shape[1]
    padded = -(-genes_here // LANES) * LANES
    rows_of = tile_cells // parts
    rows = slots * rows_of
    return (
        mesh.shape["cells"] % 2 == 0
        and tile_cells % (8 * parts) == 0
        and neighbours <= rows_of
        and rows % 16 == 0
        and rows % max(16, rows_of) == 0
        and LANES % rows == 0
        and genes_here % 8 == 0
        and padded - genes_here >= 3
        and groups * padded // LANES == parts // 2
        and width % (32 * groups) == 0
        and width // groups // 16 * rows * 2 <= LANES
    )


def solution(mesh):
    chips = Mesh(
        mesh.devices.reshape(mesh.shape["cells"] // 2, 2, mesh.shape["genes"]),
        ("chips", "core", "genes"),
    )

    def program(data, start, link_dev, link_slot, link_weight):
        if fits_by_cell(mesh, data, start, link_dev):
            way, over, cells = by_condition, chips, ("chips", "core")
        else:
            way, over, cells = by_tile, mesh, "cells"
        return jax.shard_map(
            way,
            mesh=over,
            in_specs=(P(cells, "genes"), P("genes", None)) + (P(cells, None),) * 3,
            out_specs=(P("genes", None), P("genes", cells)),
            check_vma=False,
        )(data, start, link_dev, link_slot, link_weight)

    return program
```

```python
import functools
import math

import jax
import jax.numpy as jnp
from jax import lax
from jax.experimental import pallas as pl
from jax.experimental.pallas import tpu as pltpu
from jax.sharding import Mesh
from jax.sharding import PartitionSpec as P

ITERS = 3
LANES = 128
AMPLIFIED = 4.0

self_weight = 8.0
HIGHEST = lax.Precision.HIGHEST


def inverse_factor(gram, spread_ref):
    width = gram.shape[0]
    rows = lax.broadcasted_iota(jnp.int32, (width, width), 0)
    cols = lax.broadcasted_iota(jnp.int32, (width, width), 1)
    diagonal = jnp.where(rows == cols, gram, 0.0)
    down = lax.rsqrt(jnp.sum(diagonal, axis=1, keepdims=True))
    along = lax.rsqrt(jnp.sum(diagonal, axis=0, keepdims=True))
    scaled = gram * down * along
    state = jnp.concatenate([(rows == cols).astype(jnp.float32), scaled], axis=1)
    strips = [state[at : at + 8] for at in range(0, width, 8)]
    shape = strips[0].shape
    place = lax.broadcasted_iota(jnp.int32, shape, 0)
    done = []
    for panel, strip in enumerate(strips):
        base = width + 8 * panel

        def column(of, j):
            return jnp.broadcast_to(of[:, base + j : base + j + 1], shape)

        slot = spread_ref.at[panel % 2]
        for j in range(8):
            slot[j] = column(strip, j)
        slot[8] = strip

        def row(of, i):
            return slot[of, pl.ds(i, 8, stride=0)]

        core = {(i, j): row(j, i) for j in range(8) for i in range(j, 8)}
        lines = [row(8, j) for j in range(8)]
        below = range(panel + 1, len(strips))
        rest = {(at, j): column(strips[at], j) for at in below for j in range(8)}
        for j in range(0, 8, 2):
            a, b, c = core[j, j], core[j + 1, j], core[j + 1, j + 1]
            area = a * c - b * b
            over = 1.0 / a
            step = b * over
            later = a * (1.0 / area)
            left = {i: core[i, j + 1] - step * core[i, j] for i in range(j + 2, 8)}
            lines[j + 1] -= step * lines[j]
            core[j + 1, j + 1] = area * over
            for i in range(j + 2, 8):
                first, second = core[i, j] * over, left[i] * later
                for m in range(j + 2, i + 1):
                    core[i, m] -= first * core[m, j] + second * left[m]
                lines[i] -= first * lines[j] + second * lines[j + 1]
            for at in below:
                first = rest[at, j] * over
                second = (rest[at, j + 1] - step * rest[at, j]) * later
                for m in range(j + 2, 8):
                    rest[at, m] -= first * core[m, j] + second * left[m]
                strips[at] -= first * lines[j] + second * lines[j + 1]
        final = lines[0] * lax.rsqrt(core[0, 0])
        for j in range(1, 8):
            final = jnp.where(place == j, lines[j] * lax.rsqrt(core[j, j]), final)
        done.append(final)
    inverse = jnp.concatenate(done, axis=0)[:, :width]
    return inverse * along, jnp.sum(inverse * inverse, axis=1, keepdims=True)


def link_matrix(packed, tiles, neighbours, slots, rows_of):
    own_dev, own_slot, own_weight = packed[:, 0:1], packed[:, 1:2], packed[:, 2:3]
    target = own_dev * slots + own_slot
    lane = lax.broadcasted_iota(jnp.int32, (tiles * neighbours, tiles), 1).astype(jnp.float32)
    hits = jnp.where(lane == target, own_weight, 0.0)
    weights = jnp.sum(hits.reshape(tiles, neighbours, tiles), axis=1)
    tile_row = lax.broadcasted_iota(jnp.int32, (tiles, tiles), 0)
    tile_col = lax.broadcasted_iota(jnp.int32, (tiles, tiles), 1)
    weights = weights + jnp.where(tile_row == tile_col, self_weight, 0.0)
    cells = tiles * rows_of
    tile_of = lax.broadcasted_iota(jnp.int32, (cells, tiles), 0) // rows_of
    expand = (tile_of == lax.broadcasted_iota(jnp.int32, (cells, tiles), 1)).astype(jnp.bfloat16)
    tall = jnp.dot(expand, weights.astype(jnp.bfloat16), preferred_element_type=jnp.float32)
    full = lax.dot_general(
        tall.astype(jnp.bfloat16),
        expand,
        (((1,), (1,)), ((), ())),
        preferred_element_type=jnp.float32,
    )
    same = (
        lax.broadcasted_iota(jnp.int32, (cells, cells), 0) % rows_of
        == lax.broadcasted_iota(jnp.int32, (cells, cells), 1) % rows_of
    )
    full = jnp.where(same, full, 0.0).astype(jnp.bfloat16)
    ones = jnp.ones((8, cells), jnp.bfloat16)
    degree = lax.dot_general(
        ones, full, (((1,), (1,)), ((), ())), preferred_element_type=jnp.float32
    )
    return full, degree


def diffuse(scores, links, degree):
    scores = scores.astype(jnp.bfloat16)
    total = lax.dot_general(
        scores, links, (((1,), (1,)), ((), ())), preferred_element_type=jnp.float32
    )
    first = (total / degree).astype(jnp.bfloat16).astype(jnp.float32)
    spread = (self_weight * first / degree).astype(jnp.bfloat16)
    return jnp.dot(spread, links, preferred_element_type=jnp.float32).astype(jnp.bfloat16)


def block(data_ref, group):
    part = data_ref[:, group]
    return part.reshape(part.shape[0] * part.shape[1], part.shape[2])


def push_update(genes_here, data_ref, group, second, out_ref, chunk):
    update = jnp.dot(second, block(data_ref, group), preferred_element_type=jnp.float32)
    lane = lax.broadcasted_iota(jnp.int32, update.shape, 1)
    update = jnp.where(lane < genes_here, update, 0.0).astype(out_ref.dtype)
    halves = update.shape[0] // chunk
    for at in range(update.shape[1] // LANES):
        for half in range(halves):
            out_ref[at * halves + half, :chunk] = update[
                half * chunk : (half + 1) * chunk, at * LANES : (at + 1) * LANES
            ]


def pull_update(chunks_ref, update_ref):
    width, padded = update_ref.shape
    chunk = chunks_ref.shape[1]
    halves = width // chunk
    for at in range(padded // LANES):
        for half in range(halves):
            update_ref[
                half * chunk : (half + 1) * chunk, at * LANES : (at + 1) * LANES
            ] = chunks_ref[at * halves + half]


def pull_both(core, half_ref, rest_ref, update_ref):
    pull_update(half_ref, update_ref.at[core])
    pull_update(rest_ref, update_ref.at[1 - core])


def gram_of(update):
    return lax.dot_general(
        update,
        update,
        (((1,), (1,)), ((), ())),
        precision=HIGHEST if update.dtype == jnp.float32 else None,
        preferred_element_type=jnp.float32,
    )


def normaliser(update_ref, genes_total, spread_ref):
    gram = gram_of(update_ref[0])
    for group in range(1, update_ref.shape[0]):
        gram = gram + gram_of(update_ref[group])
    return inverse_factor(gram / genes_total, spread_ref)


def apply(inverse, array):
    return jnp.dot(inverse, array, precision=HIGHEST, preferred_element_type=jnp.float32)


def score(left, data_ref, groups):
    total = None
    for at, group in enumerate(groups):
        part = lax.dot_general(
            left(at),
            block(data_ref, group),
            (((1,), (1,)), ((), ())),
            preferred_element_type=jnp.float32,
        )
        total = part if total is None else total + part
    return total


def regroup_kernel(
    rows_of,
    data_any,
    dev_any,
    slot_any,
    weight_any,
    out_any,
    data_ref,
    link_ref,
    out_ref,
    data_sem,
    link_sem,
    out_sem,
):
    genes_here, cells = data_ref.shape
    parts, rows, padded = out_ref.shape
    slots, neighbours = link_ref.shape[1:]
    tile_cells = cells // slots
    share = max(16, rows_of)
    joined = share // rows_of
    whole = padded - LANES
    link_copies = [
        pltpu.make_async_copy(source, link_ref.at[at], link_sem.at[at])
        for at, source in enumerate((dev_any, slot_any, weight_any))
    ]
    tile_at = [pl.ds(tile * tile_cells, tile_cells) for tile in range(slots)]
    data_copies = [
        pltpu.make_async_copy(data_any.at[:, at], data_ref.at[:, at], data_sem.at[tile])
        for tile, at in enumerate(tile_at)
    ]
    for copy in data_copies[:1] + link_copies + data_copies[1:]:
        copy.start()

    def wide_links():
        spread = (
            lax.broadcasted_iota(jnp.int32, (neighbours, cells), 0)
            == lax.broadcasted_iota(jnp.int32, (neighbours, cells), 1) % rows_of
        ).astype(jnp.float32)
        tile = lax.broadcasted_iota(jnp.int32, (slots, cells), 0)
        own_tile = tile == lax.broadcasted_iota(jnp.int32, (slots, cells), 1) // tile_cells
        row = lax.broadcasted_iota(jnp.int32, (padded - genes_here, cells), 0)
        links = jnp.zeros((padded - genes_here, cells), jnp.float32)
        for at, copy in enumerate(link_copies):
            copy.wait()
            wide = jnp.dot(
                link_ref[at].astype(jnp.float32), spread, preferred_element_type=jnp.float32
            )
            wide = jnp.sum(jnp.where(own_tile, wide, 0.0), axis=0, keepdims=True)
            links = jnp.where(row == at, wide, links)
        return links

    def turned(part):
        return part.T.astype(jnp.float32).reshape(parts, rows_of, part.shape[0])

    out_copies, links = [], None
    for first in range(0, slots, joined):
        main, rest = [], []
        for tile in range(first, first + joined):
            data_copies[tile].wait()
            at = slice(tile * tile_cells, (tile + 1) * tile_cells)
            main.append(turned(data_ref[:whole, at]))
            links = wide_links() if links is None else links
            end = data_ref[whole:genes_here, at].astype(jnp.float32)
            end = jnp.concatenate([end, links[:, at]], axis=0)
            rest.append(turned(end.astype(jnp.bfloat16)))
        keep = slice(first * rows_of, first * rows_of + share)
        out_ref[:, keep, :whole] = jnp.concatenate(main, axis=1).astype(jnp.bfloat16)
        out_ref[:, keep, whole:] = jnp.concatenate(rest, axis=1).astype(jnp.bfloat16)
        keep = pl.ds(first * rows_of, share)
        out_copies.append(
            pltpu.make_async_copy(
                out_ref.at[:, keep], out_any.at[:, keep], out_sem.at[first // joined]
            )
        )
        out_copies[-1].start()
    for copy in out_copies:
        copy.wait()


def share_second(core, to, second, out_ref, chunk, groups):
    width, cells = second.shape
    blocks, tall = out_ref.shape[:2]
    cores = 2
    rows = cells * groups // (cores * blocks)
    tall = tall - chunk
    slabs = width // groups // tall
    lane = lax.broadcasted_iota(jnp.int32, (tall, LANES), 1) // rows
    chips = LANES // rows // cores
    for at in range(cells // LANES):
        wide = second[:, at * LANES : (at + 1) * LANES].astype(jnp.float32)
        for chip in range(chips):
            for group in range(groups):
                share = jnp.zeros((tall, LANES), jnp.float32)
                for slab in range(slabs):
                    first_row = (group * slabs + slab) * tall
                    place = core * slabs + slab
                    shift = (place - chip * cores - to) * rows
                    turned = pltpu.roll(
                        wide[first_row : first_row + tall],
                        lax.rem(shift + LANES, LANES),
                        1,
                    )
                    share = jnp.where(lane == place, turned, share)
                out_ref[(at * chips + chip) * groups + group, chunk:] = share.astype(
                    out_ref.dtype
                )


def order_shares(arrived_ref, chunk, out_ref, groups, cores, slots):
    part_width, cells = out_ref.shape
    blocks, tall = arrived_ref.shape[:2]
    tall = tall - chunk
    parts = blocks * cores
    rows_of = cells // (slots * parts)
    rows = slots * rows_of
    slabs = part_width // tall
    together = LANES // rows_of
    lane = lax.broadcasted_iota(jnp.int32, (tall, LANES), 1) // rows_of
    for slab in range(slabs):
        for slot in range(slots):
            for first in range(0, parts, together):
                whole = jnp.zeros((tall, LANES), jnp.float32)
                for at in range(together):
                    chip, rest = divmod(first + at, cores * groups)
                    core, group = divmod(rest, groups)
                    source = (core * slabs + slab) * rows + slot * rows_of
                    share = arrived_ref[chip * groups + group, chunk:].astype(jnp.float32)
                    turned = pltpu.roll(share, (at * rows_of - source) % LANES, 1)
                    whole = jnp.where(lane == at, turned, whole)
                to = (slot * parts + first) * rows_of
                out_ref[slab * tall : (slab + 1) * tall, to : to + LANES] = whole.astype(
                    jnp.bfloat16
                )


def first_kernel(
    genes_here,
    slots,
    place_ref,
    data_ref,
    start_ref,
    other_ref,
    second_ref,
    links_ref,
    degree_ref,
):
    devices, groups, rows, padded = data_ref.shape
    tiles = devices * slots
    core, own = place_ref[0], place_ref[1]
    packed = block(data_ref, 0)[:, padded - LANES :].astype(jnp.float32)
    offset = genes_here - (padded - LANES)
    links, degree = link_matrix(
        packed[:, offset : offset + 3], tiles, rows // slots, slots, rows // slots
    )
    links_ref[...] = links
    degree_ref[...] = degree
    order = [lax.rem(own + groups - shift, groups) for shift in range(groups)]
    scores = score(lambda shift: start_ref[shift], data_ref, order)
    scores = scores / math.sqrt(genes_here * groups)
    second = diffuse(scores, links, degree[:1])
    second_ref[...] = second
    push_update(genes_here, data_ref, 1 - core, second, other_ref, other_ref.shape[1])


def half_kernel(place_ref, half_ref, data_ref, scores_ref, gram_ref, update_ref):
    pull_update(half_ref, update_ref)
    gram_ref[...] = gram_of(update_ref[...])
    scores_ref[...] = score(lambda _: update_ref[...], data_ref, [place_ref[0]])


def next_kernel(
    genes_here,
    chunk,
    place_ref,
    scores_ref,
    gram_ref,
    rest_ref,
    data_ref,
    links_ref,
    degree_ref,
    other_ref,
    second_ref,
    worst_ref,
    update_ref,
    spread_ref,
):
    core = place_ref[0]
    groups = data_ref.shape[1]
    genes_total = genes_here * groups
    pull_update(rest_ref, update_ref)
    gram = (gram_ref[...] + gram_of(update_ref[...])) / genes_total
    inverse, amplified = inverse_factor(gram, spread_ref)
    worst_ref[...] = jnp.broadcast_to(amplified, worst_ref.shape)
    scores = scores_ref[...] + score(lambda _: update_ref[...], data_ref, [1 - core])
    scores = apply(inverse, scores) / math.sqrt(genes_total)
    second = diffuse(scores, links_ref[...], degree_ref[:1])
    second_ref[...] = second
    push_update(genes_here, data_ref, 1 - core, second, other_ref, chunk)
    if other_ref.shape[1] > chunk:
        share_second(core, 1 - core, second, other_ref, chunk, groups)


def exact_kernel(
    genes_here,
    chunk,
    place_ref,
    half_ref,
    rest_ref,
    data_ref,
    links_ref,
    degree_ref,
    other_ref,
    second_ref,
    worst_ref,
    update_ref,
    spread_ref,
):
    core = place_ref[0]
    groups = data_ref.shape[1]
    genes_total = genes_here * groups
    pull_both(core, half_ref, rest_ref, update_ref)
    inverse, amplified = normaliser(update_ref, genes_total, spread_ref)
    worst_ref[...] = jnp.broadcast_to(amplified, worst_ref.shape)
    scores = score(
        lambda group: apply(inverse, update_ref[group]).astype(jnp.bfloat16),
        data_ref,
        range(groups),
    ) / math.sqrt(genes_total)
    second = diffuse(scores, links_ref[...], degree_ref[:1])
    second_ref[...] = second
    push_update(genes_here, data_ref, 1 - core, second, other_ref, chunk)
    if other_ref.shape[1] > chunk:
        share_second(core, 1 - core, second, other_ref, chunk, groups)


def mine_kernel(genes_here, chunk, place_ref, data_ref, second_ref, mine_ref):
    core, second = place_ref[0], second_ref[...]
    push_update(genes_here, data_ref, core, second, mine_ref, chunk)
    if mine_ref.shape[1] > chunk:
        share_second(core, core, second, mine_ref, chunk, data_ref.shape[1])


def own_kernel(slots, place_ref, half_ref, arrived_ref, smoothed_ref, gram_ref, update_ref):
    pull_update(half_ref, update_ref)
    gram_ref[...] = gram_of(update_ref[...])
    order_shares(arrived_ref, half_ref.shape[1], smoothed_ref, 2, 2, slots)


def last_kernel(genes_here, place_ref, half_ref, rest_ref, gram_ref, *refs):
    *earlier, out_ref, good_ref, update_ref, spread_ref = refs
    core, own = place_ref[0], place_ref[1]
    groups = update_ref.shape[0]
    pull_both(core, half_ref, rest_ref, update_ref)
    gram = gram_ref[...] + gram_of(update_ref[1 - core])
    inverse, amplified = inverse_factor(gram / (genes_here * groups), spread_ref)
    good = amplified <= AMPLIFIED
    for worst_ref in earlier:
        good = good & (worst_ref[:, :1] <= AMPLIFIED)
    good_ref[0] = jnp.min(good.astype(jnp.int32))
    loadings = apply(inverse, update_ref[own].astype(jnp.float32))
    out_ref[...] = loadings[:, :genes_here]


def add_kernel(mine_ref, arrived_ref, out_ref):
    total = mine_ref[...].astype(jnp.float32) + arrived_ref[...].astype(jnp.float32)
    out_ref[...] = total.astype(out_ref.dtype)


def sum_kernel(chunks_ref, out_ref):
    parts = chunks_ref[:, : out_ref.shape[1]].astype(jnp.float32)
    total = jnp.sum(parts, axis=0).astype(out_ref.dtype)
    out_ref[...] = jnp.broadcast_to(total[None], out_ref.shape)


def like(array):
    return jax.ShapeDtypeStruct(array.shape, array.dtype)


def call(kernel, out_shape, scratch=(), scalars=0, arrays=0):
    in_specs = [pl.BlockSpec(memory_space=pltpu.SMEM)] * scalars
    in_specs += [pl.BlockSpec(memory_space=pltpu.VMEM)] * arrays
    return pl.pallas_call(
        kernel,
        out_shape=out_shape,
        in_specs=in_specs,
        out_specs=jax.tree.map(
            lambda leaf: pl.BlockSpec(memory_space=pltpu.VMEM if leaf.ndim > 1 else pltpu.SMEM),
            out_shape,
        ),
        scratch_shapes=list(scratch),
        compiler_params=pltpu.CompilerParams(vmem_limit_bytes=32 * 1024 * 1024),
    )


def by_cell(kept, data, start, link_dev, link_slot, link_weight):
    cores, groups = lax.axis_size("core"), lax.axis_size("genes")
    devices = lax.axis_size("chips") * cores
    parts = devices * groups
    blocks = parts // cores
    slots, neighbours = link_dev.shape
    genes_here, width = data.shape[1], start.shape[1]
    tile_cells = data.shape[0] // slots
    rows_of = tile_cells // parts
    rows = slots * rows_of
    padded = -(-genes_here // LANES) * LANES
    cells = devices * rows
    chunk = width // cores
    place = jnp.stack([lax.axis_index("core"), lax.axis_index("genes")]).astype(jnp.int32)

    def exchange(array):
        return lax.all_to_all(array, ("chips", "genes"), 0, 0, tiled=True)

    def swap(array):
        return lax.ppermute(array, "core", [(0, 1), (1, 0)])

    narrow = jnp.pad(start.astype(jnp.bfloat16).T, ((0, 0), (0, padded - genes_here)))
    starts = [narrow]
    for shift in range(1, groups):
        pairs = [(at, (at + shift) % groups) for at in range(groups)]
        starts.append(lax.ppermute(narrow, "genes", pairs))
    starts = jnp.stack(starts)
    moved = pl.pallas_call(
        functools.partial(regroup_kernel, rows_of),
        out_shape=jax.ShapeDtypeStruct((parts, rows, padded), jnp.bfloat16),
        in_specs=[pl.BlockSpec(memory_space=pl.ANY)] * 4,
        out_specs=pl.BlockSpec(memory_space=pl.ANY),
        scratch_shapes=[
            pltpu.VMEM((genes_here, slots * tile_cells), jnp.bfloat16),
            pltpu.VMEM((3, slots, neighbours), jnp.int32),
            pltpu.VMEM((parts, rows, padded), jnp.bfloat16),
            pltpu.SemaphoreType.DMA((slots,)),
            pltpu.SemaphoreType.DMA((3,)),
            pltpu.SemaphoreType.DMA((rows // max(16, rows_of),)),
        ],
        compiler_params=pltpu.CompilerParams(vmem_limit_bytes=60 * 1024 * 1024),
    )(data.T, link_dev, link_slot, link_weight)
    moved = lax.all_to_all(moved, ("chips", "core", "genes"), 0, 0, tiled=True)
    moved = moved.reshape(devices, groups, rows, padded)

    def cut(tall):
        return jax.ShapeDtypeStruct((blocks, tall, LANES), kept)

    def shape(*sizes, dtype=jnp.float32):
        return jax.ShapeDtypeStruct(sizes, dtype)

    part = pltpu.VMEM((width, padded), kept)
    update = pltpu.VMEM((groups, width, padded), kept)
    spread = pltpu.VMEM((2, 9, 8, 2 * width), jnp.float32)
    second_shape = shape(width, cells, dtype=jnp.bfloat16)
    worst = shape(width, LANES)
    earlier = []

    def reduce(other, second):
        swapped = swap(other)
        mine = call(
            functools.partial(mine_kernel, genes_here, chunk), like(other), scalars=1, arrays=2
        )(place, moved, second)
        return exchange(call(add_kernel, like(other), arrays=2)(mine, swapped))

    def gather(arrived):
        half = exchange(call(sum_kernel, cut(chunk), arrays=1)(arrived))
        return half, swap(half)

    other, second, links, degree = call(
        functools.partial(first_kernel, genes_here, slots),
        (cut(chunk), second_shape, shape(cells, cells, dtype=jnp.bfloat16), shape(8, cells)),
        scalars=1,
        arrays=2,
    )(place, moved, starts)
    arrived = reduce(other, second)
    for step in range(1, ITERS):
        share = cut(chunk + 16 if step == ITERS - 1 else chunk)
        half, rest = gather(arrived)
        if kept == jnp.float32:
            kernel, known, scratch = exact_kernel, (half, rest), update
        else:
            scores, gram = call(
                half_kernel,
                (shape(width, cells), shape(width, width)),
                (part,),
                scalars=1,
                arrays=2,
            )(place, half, moved)
            kernel, known, scratch = next_kernel, (scores, gram, rest), part
        other, second, amplified = call(
            functools.partial(kernel, genes_here, chunk),
            (share, second_shape, worst),
            (scratch, spread),
            scalars=1,
            arrays=3 + len(known),
        )(place, *known, moved, links, degree)
        earlier.append(amplified)
        arrived = reduce(other, second)
    half, rest = gather(arrived)
    smoothed, gram = call(
        functools.partial(own_kernel, slots),
        (
            shape(width // groups, slots * tile_cells, dtype=jnp.bfloat16),
            shape(width, width),
        ),
        (part,),
        scalars=1,
        arrays=2,
    )(place, half, arrived)
    loadings, good = call(
        functools.partial(last_kernel, genes_here),
        (shape(width, genes_here), shape(1, dtype=jnp.int32)),
        (update, spread),
        scalars=1,
        arrays=3 + len(earlier),
    )(place, half, rest, gram, *earlier)
    return loadings.T, smoothed, good[0] == 1


def by_condition(*arguments):
    loadings, smoothed, good = by_cell(jnp.bfloat16, *arguments)
    return lax.cond(
        good,
        lambda *_: (loadings, smoothed),
        lambda *again: by_cell(jnp.float32, *again)[:2],
        *arguments,
    )


def by_tile(data, start, link_dev, link_slot, link_weight):
    devices = lax.axis_size("cells")
    groups = lax.axis_size("genes")
    tiles_here, neighbours = link_dev.shape
    tile_cells = data.shape[0] // tiles_here
    genes_total = data.shape[1] * groups
    width = start.shape[1]
    part_width = width // groups
    capacity = max(2, 2 * tiles_here * neighbours // devices)
    slot_count = devices * capacity
    links = tiles_here * neighbours
    columns = part_width * tile_cells
    flat_dev = link_dev.reshape(links)
    flat_slot = link_slot.reshape(links)
    flat_weight = link_weight.reshape(links)
    dev_hits = (flat_dev[:, None] == jnp.arange(devices, dtype=jnp.int32)[None, :]).astype(
        jnp.int32
    )
    earlier = jnp.cumsum(dev_hits, axis=0) - dev_hits
    ranking = jnp.sum(earlier * dev_hits, axis=1)
    position = flat_dev * capacity + ranking
    placed = (position[:, None] == jnp.arange(slot_count, dtype=jnp.int32)[None, :]).astype(
        jnp.int32
    )
    wanted = jnp.sum(placed * (flat_slot + 1)[:, None], axis=0).reshape(devices, capacity)
    wanted_weight = jnp.sum(placed * flat_weight[:, None], axis=0).reshape(devices, capacity)
    asked_pair = (
        lax.all_to_all(wanted, "cells", split_axis=0, concat_axis=0, tiled=True),
        lax.all_to_all(wanted_weight, "cells", split_axis=0, concat_axis=0, tiled=True),
    )
    asked = asked_pair[0].reshape(slot_count)
    asked_weight = asked_pair[1].reshape(slot_count)
    tile_ids = jnp.arange(tiles_here, dtype=jnp.int32)
    serve_match = ((asked - 1)[:, None] == tile_ids[None, :]).astype(jnp.int32)
    serve = serve_match.astype(jnp.bfloat16)
    collect = (serve_match * asked_weight[:, None]).T.astype(jnp.bfloat16)
    placed_tiles = placed.reshape(tiles_here, neighbours, slot_count)
    link_matrix = jnp.sum(placed_tiles * link_weight[:, :, None], axis=1).astype(jnp.bfloat16)
    sender = jnp.sum(placed_tiles, axis=1).astype(jnp.bfloat16)
    degree = (self_weight + jnp.sum(link_weight, axis=1).astype(jnp.float32))[:, None]
    loadings = start
    smoothed = jnp.zeros((part_width, tiles_here * tile_cells), jnp.bfloat16)
    for step in range(ITERS):
        narrow = loadings.astype(jnp.bfloat16)
        partial_scores = lax.dot_general(
            narrow, data, (((0,), (1,)), ((), ())), preferred_element_type=jnp.float32
        )
        summed = lax.psum(partial_scores.astype(jnp.bfloat16), "genes").astype(jnp.float32)
        mine = lax.dynamic_slice_in_dim(summed, lax.axis_index("genes") * part_width, part_width, 0)
        scores = (mine / math.sqrt(genes_total)).astype(jnp.bfloat16)
        tiles = (
            scores.reshape(part_width, tiles_here, tile_cells)
            .transpose(1, 0, 2)
            .reshape(tiles_here, columns)
        )
        outgoing = jnp.dot(serve, tiles, preferred_element_type=jnp.float32).astype(jnp.bfloat16)
        linked = jnp.dot(
            link_matrix,
            lax.all_to_all(
                outgoing.reshape(devices, capacity, columns),
                "cells",
                split_axis=0,
                concat_axis=0,
                tiled=True,
            ).reshape(slot_count, -1),
            preferred_element_type=jnp.float32,
        )
        first = lax.optimization_barrier(
            ((self_weight * tiles.astype(jnp.float32) + linked) / degree).astype(jnp.bfloat16)
        )
        spread = lax.optimization_barrier(
            (self_weight * first.astype(jnp.float32) / degree).astype(jnp.bfloat16)
        )
        returning = lax.dot_general(
            sender, spread, (((0,), (0,)), ((), ())), preferred_element_type=jnp.float32
        ).astype(jnp.bfloat16)
        pushed = jnp.dot(
            collect,
            lax.all_to_all(
                returning.reshape(devices, capacity, columns),
                "cells",
                split_axis=0,
                concat_axis=0,
                tiled=True,
            ).reshape(slot_count, -1),
            preferred_element_type=jnp.float32,
        )
        second = (self_weight * spread.astype(jnp.float32) + pushed).astype(jnp.bfloat16)
        smoothed = (
            second.reshape(tiles_here, part_width, tile_cells)
            .transpose(1, 0, 2)
            .reshape(part_width, tiles_here * tile_cells)
        )
        update = lax.dot_general(
            data,
            lax.all_gather(smoothed, "genes", axis=0, tiled=True),
            (((0,), (1,)), ((), ())),
            preferred_element_type=jnp.float32,
        )
        update = lax.psum(update, "cells")
        gram_part = jnp.dot(
            update.T, update, precision=lax.Precision.HIGHEST, preferred_element_type=jnp.float32
        )
        gram = lax.psum(gram_part, "genes") / genes_total
        factor = jnp.linalg.cholesky(gram)
        loadings = lax.linalg.triangular_solve(
            factor, update, left_side=False, lower=True, transpose_a=True
        )
    return (loadings, smoothed)


def fits_by_cell(mesh, data, start, link_dev):
    groups, parts = mesh.shape["genes"], mesh.size
    slots, neighbours = link_dev.shape[0] * groups // parts, link_dev.shape[1]
    tile_cells = data.shape[0] // link_dev.shape[0]
    genes_here, width = data.shape[1] // groups, start.shape[1]
    padded = -(-genes_here // LANES) * LANES
    rows_of = tile_cells // parts
    rows = slots * rows_of
    return (
        mesh.shape["cells"] % 2 == 0
        and groups == 2
        and tile_cells % (8 * parts) == 0
        and neighbours <= rows_of
        and rows % 16 == 0
        and rows % max(16, rows_of) == 0
        and LANES % rows == 0
        and genes_here % 8 == 0
        and padded - genes_here >= 3
        and groups * padded // LANES == parts // 2
        and width % (32 * groups) == 0
        and width // groups // 16 * rows * 2 <= LANES
    )


def solution(mesh):
    chips = Mesh(
        mesh.devices.reshape(mesh.shape["cells"] // 2, 2, mesh.shape["genes"]),
        ("chips", "core", "genes"),
    )

    def program(data, start, link_dev, link_slot, link_weight):
        if fits_by_cell(mesh, data, start, link_dev):
            way, over, cells = by_condition, chips, ("chips", "core")
        else:
            way, over, cells = by_tile, mesh, "cells"
        return jax.shard_map(
            way,
            mesh=over,
            in_specs=(P(cells, "genes"), P("genes", None)) + (P(cells, None),) * 3,
            out_specs=(P("genes", None), P("genes", cells)),
            check_vma=False,
        )(data, start, link_dev, link_slot, link_weight)

    return program
```

```python
import functools
import math

import jax
import jax.numpy as jnp
from jax import lax
from jax.experimental import pallas as pl
from jax.experimental.pallas import tpu as pltpu
from jax.sharding import Mesh
from jax.sharding import PartitionSpec as P

ITERS = 3
LANES = 128
AMPLIFIED = 4.0

self_weight = 8.0
HIGHEST = lax.Precision.HIGHEST


def inverse_factor(gram, spread_ref):
    width = gram.shape[0]
    rows = lax.broadcasted_iota(jnp.int32, (width, width), 0)
    cols = lax.broadcasted_iota(jnp.int32, (width, width), 1)
    diagonal = jnp.where(rows == cols, gram, 0.0)
    down = lax.rsqrt(jnp.sum(diagonal, axis=1, keepdims=True))
    along = lax.rsqrt(jnp.sum(diagonal, axis=0, keepdims=True))
    scaled = gram * down * along
    state = jnp.concatenate([(rows == cols).astype(jnp.float32), scaled], axis=1)
    strips = [state[at : at + 8] for at in range(0, width, 8)]
    shape = strips[0].shape
    place = lax.broadcasted_iota(jnp.int32, shape, 0)
    done = []
    for panel, strip in enumerate(strips):
        base = width + 8 * panel

        def column(of, j):
            return jnp.broadcast_to(of[:, base + j : base + j + 1], shape)

        slot = spread_ref.at[panel % 2]
        for j in range(8):
            slot[j] = column(strip, j)
        slot[8] = strip

        def row(of, i):
            return slot[of, pl.ds(i, 8, stride=0)]

        core = {(i, j): row(j, i) for j in range(8) for i in range(j, 8)}
        lines = [row(8, j) for j in range(8)]
        below = range(panel + 1, len(strips))
        rest = {(at, j): column(strips[at], j) for at in below for j in range(8)}
        for j in range(0, 8, 2):
            a, b, c = core[j, j], core[j + 1, j], core[j + 1, j + 1]
            area = a * c - b * b
            over = 1.0 / a
            step = b * over
            later = a * (1.0 / area)
            left = {i: core[i, j + 1] - step * core[i, j] for i in range(j + 2, 8)}
            lines[j + 1] -= step * lines[j]
            core[j + 1, j + 1] = area * over
            for i in range(j + 2, 8):
                first, second = core[i, j] * over, left[i] * later
                for m in range(j + 2, i + 1):
                    core[i, m] -= first * core[m, j] + second * left[m]
                lines[i] -= first * lines[j] + second * lines[j + 1]
            for at in below:
                first = rest[at, j] * over
                second = (rest[at, j + 1] - step * rest[at, j]) * later
                for m in range(j + 2, 8):
                    rest[at, m] -= first * core[m, j] + second * left[m]
                strips[at] -= first * lines[j] + second * lines[j + 1]
        final = lines[0] * lax.rsqrt(core[0, 0])
        for j in range(1, 8):
            final = jnp.where(place == j, lines[j] * lax.rsqrt(core[j, j]), final)
        done.append(final)
    inverse = jnp.concatenate(done, axis=0)[:, :width]
    return inverse * along, jnp.sum(inverse * inverse, axis=1, keepdims=True)


def link_matrix(packed, tiles, neighbours, slots, rows_of):
    own_dev, own_slot, own_weight = packed[:, 0:1], packed[:, 1:2], packed[:, 2:3]
    target = own_dev * slots + own_slot
    lane = lax.broadcasted_iota(jnp.int32, (tiles * neighbours, tiles), 1).astype(jnp.float32)
    hits = jnp.where(lane == target, own_weight, 0.0)
    weights = jnp.sum(hits.reshape(tiles, neighbours, tiles), axis=1, keepdims=True)
    cells = tiles * rows_of
    tall = jnp.broadcast_to(weights, (tiles, rows_of, tiles)).reshape(cells, tiles)
    tile_of = lax.broadcasted_iota(jnp.int32, (cells, tiles), 0) // rows_of
    own = tile_of == lax.broadcasted_iota(jnp.int32, (cells, tiles), 1)
    tall = tall + jnp.where(own, self_weight, 0.0)
    expand = own.astype(jnp.bfloat16)
    full = lax.dot_general(
        tall.astype(jnp.bfloat16),
        expand,
        (((1,), (1,)), ((), ())),
        preferred_element_type=jnp.float32,
    )
    same = (
        lax.broadcasted_iota(jnp.int32, (cells, cells), 0) % rows_of
        == lax.broadcasted_iota(jnp.int32, (cells, cells), 1) % rows_of
    )
    full = jnp.where(same, full, 0.0).astype(jnp.bfloat16)
    ones = jnp.ones((8, cells), jnp.bfloat16)
    degree = lax.dot_general(
        ones, full, (((1,), (1,)), ((), ())), preferred_element_type=jnp.float32
    )
    return full, degree


def diffuse(scores, links, degree):
    scores = scores.astype(jnp.bfloat16)
    total = lax.dot_general(
        scores, links, (((1,), (1,)), ((), ())), preferred_element_type=jnp.float32
    )
    first = (total / degree).astype(jnp.bfloat16).astype(jnp.float32)
    spread = (self_weight * first / degree).astype(jnp.bfloat16)
    return jnp.dot(spread, links, preferred_element_type=jnp.float32).astype(jnp.bfloat16)


def block(data_ref, group):
    part = data_ref[:, group]
    return part.reshape(part.shape[0] * part.shape[1], part.shape[2])


def push_update(genes_here, data_ref, group, second, out_ref, chunk):
    update = jnp.dot(second, block(data_ref, group), preferred_element_type=jnp.float32)
    lane = lax.broadcasted_iota(jnp.int32, update.shape, 1)
    update = jnp.where(lane < genes_here, update, 0.0).astype(out_ref.dtype)
    halves = update.shape[0] // chunk
    for at in range(update.shape[1] // LANES):
        for half in range(halves):
            out_ref[at * halves + half, :chunk] = update[
                half * chunk : (half + 1) * chunk, at * LANES : (at + 1) * LANES
            ]


def pull_update(chunks_ref, update_ref):
    width, padded = update_ref.shape
    chunk = chunks_ref.shape[1]
    halves = width // chunk
    for at in range(padded // LANES):
        for half in range(halves):
            update_ref[
                half * chunk : (half + 1) * chunk, at * LANES : (at + 1) * LANES
            ] = chunks_ref[at * halves + half]


def pull_both(core, half_ref, rest_ref, update_ref):
    pull_update(half_ref, update_ref.at[core])
    pull_update(rest_ref, update_ref.at[1 - core])


def gram_of(update):
    return lax.dot_general(
        update,
        update,
        (((1,), (1,)), ((), ())),
        precision=HIGHEST if update.dtype == jnp.float32 else None,
        preferred_element_type=jnp.float32,
    )


def normaliser(update_ref, genes_total, spread_ref):
    gram = gram_of(update_ref[0])
    for group in range(1, update_ref.shape[0]):
        gram = gram + gram_of(update_ref[group])
    return inverse_factor(gram / genes_total, spread_ref)


def apply(inverse, array):
    return jnp.dot(inverse, array, precision=HIGHEST, preferred_element_type=jnp.float32)


def score(left, data_ref, groups):
    total = None
    for at, group in enumerate(groups):
        part = lax.dot_general(
            left(at),
            block(data_ref, group),
            (((1,), (1,)), ((), ())),
            preferred_element_type=jnp.float32,
        )
        total = part if total is None else total + part
    return total


def regroup_kernel(
    rows_of,
    data_any,
    dev_any,
    slot_any,
    weight_any,
    out_any,
    data_ref,
    link_ref,
    out_ref,
    data_sem,
    link_sem,
    out_sem,
):
    genes_here, cells = data_ref.shape
    parts, rows, padded = out_ref.shape
    slots, neighbours = link_ref.shape[1:]
    tile_cells = cells // slots
    share = max(16, rows_of)
    joined = share // rows_of
    whole = padded - LANES
    link_copies = [
        pltpu.make_async_copy(source, link_ref.at[at], link_sem.at[at])
        for at, source in enumerate((dev_any, slot_any, weight_any))
    ]
    tile_at = [pl.ds(tile * tile_cells, tile_cells) for tile in range(slots)]
    data_copies = [
        pltpu.make_async_copy(data_any.at[:, at], data_ref.at[:, at], data_sem.at[tile])
        for tile, at in enumerate(tile_at)
    ]
    for copy in data_copies[:1] + link_copies + data_copies[1:]:
        copy.start()

    def wide_links():
        spread = (
            lax.broadcasted_iota(jnp.int32, (neighbours, cells), 0)
            == lax.broadcasted_iota(jnp.int32, (neighbours, cells), 1) % rows_of
        ).astype(jnp.float32)
        tile = lax.broadcasted_iota(jnp.int32, (slots, cells), 0)
        own_tile = tile == lax.broadcasted_iota(jnp.int32, (slots, cells), 1) // tile_cells
        row = lax.broadcasted_iota(jnp.int32, (padded - genes_here, cells), 0)
        links = jnp.zeros((padded - genes_here, cells), jnp.float32)
        for at, copy in enumerate(link_copies):
            copy.wait()
            wide = jnp.dot(
                link_ref[at].astype(jnp.float32), spread, preferred_element_type=jnp.float32
            )
            wide = jnp.sum(jnp.where(own_tile, wide, 0.0), axis=0, keepdims=True)
            links = jnp.where(row == at, wide, links)
        return links

    def turned(part):
        return part.T.astype(jnp.float32).reshape(parts, rows_of, part.shape[0])

    out_copies, links = [], None
    for first in range(0, slots, joined):
        main, rest = [], []
        for tile in range(first, first + joined):
            data_copies[tile].wait()
            at = slice(tile * tile_cells, (tile + 1) * tile_cells)
            main.append(turned(data_ref[:whole, at]))
            links = wide_links() if links is None else links
            end = data_ref[whole:genes_here, at].astype(jnp.float32)
            end = jnp.concatenate([end, links[:, at]], axis=0)
            rest.append(turned(end.astype(jnp.bfloat16)))
        keep = slice(first * rows_of, first * rows_of + share)
        out_ref[:, keep, :whole] = jnp.concatenate(main, axis=1).astype(jnp.bfloat16)
        out_ref[:, keep, whole:] = jnp.concatenate(rest, axis=1).astype(jnp.bfloat16)
        keep = pl.ds(first * rows_of, share)
        out_copies.append(
            pltpu.make_async_copy(
                out_ref.at[:, keep], out_any.at[:, keep], out_sem.at[first // joined]
            )
        )
        out_copies[-1].start()
    for copy in out_copies:
        copy.wait()


def share_second(core, to, second, out_ref, chunk, groups):
    width, cells = second.shape
    blocks, tall = out_ref.shape[:2]
    cores = 2
    rows = cells * groups // (cores * blocks)
    tall = tall - chunk
    slabs = width // groups // tall
    lane = lax.broadcasted_iota(jnp.int32, (tall, LANES), 1) // rows
    chips = LANES // rows // cores
    for at in range(cells // LANES):
        wide = second[:, at * LANES : (at + 1) * LANES].astype(jnp.float32)
        for chip in range(chips):
            for group in range(groups):
                share = jnp.zeros((tall, LANES), jnp.float32)
                for slab in range(slabs):
                    first_row = (group * slabs + slab) * tall
                    place = core * slabs + slab
                    shift = (place - chip * cores - to) * rows
                    turned = pltpu.roll(
                        wide[first_row : first_row + tall],
                        lax.rem(shift + LANES, LANES),
                        1,
                    )
                    share = jnp.where(lane == place, turned, share)
                out_ref[(at * chips + chip) * groups + group, chunk:] = share.astype(
                    out_ref.dtype
                )


def order_shares(arrived_ref, chunk, out_ref, groups, cores, slots):
    part_width, cells = out_ref.shape
    blocks, tall = arrived_ref.shape[:2]
    tall = tall - chunk
    parts = blocks * cores
    rows_of = cells // (slots * parts)
    rows = slots * rows_of
    slabs = part_width // tall
    together = LANES // rows_of
    lane = lax.broadcasted_iota(jnp.int32, (tall, LANES), 1) // rows_of
    for slab in range(slabs):
        for slot in range(slots):
            for first in range(0, parts, together):
                whole = jnp.zeros((tall, LANES), jnp.float32)
                for at in range(together):
                    chip, rest = divmod(first + at, cores * groups)
                    core, group = divmod(rest, groups)
                    source = (core * slabs + slab) * rows + slot * rows_of
                    share = arrived_ref[chip * groups + group, chunk:].astype(jnp.float32)
                    turned = pltpu.roll(share, (at * rows_of - source) % LANES, 1)
                    whole = jnp.where(lane == at, turned, whole)
                to = (slot * parts + first) * rows_of
                out_ref[slab * tall : (slab + 1) * tall, to : to + LANES] = whole.astype(
                    jnp.bfloat16
                )


def first_kernel(
    genes_here,
    slots,
    place_ref,
    data_ref,
    start_ref,
    other_ref,
    second_ref,
    links_ref,
    degree_ref,
):
    devices, groups, rows, padded = data_ref.shape
    tiles = devices * slots
    core, own = place_ref[0], place_ref[1]
    packed = block(data_ref, 0)[:, padded - LANES :].astype(jnp.float32)
    offset = genes_here - (padded - LANES)
    links, degree = link_matrix(
        packed[:, offset : offset + 3], tiles, rows // slots, slots, rows // slots
    )
    links_ref[...] = links
    degree_ref[...] = degree
    order = [lax.rem(own + groups - shift, groups) for shift in range(groups)]
    scores = score(lambda shift: start_ref[shift], data_ref, order)
    scores = scores / math.sqrt(genes_here * groups)
    second = diffuse(scores, links, degree[:1])
    second_ref[...] = second
    push_update(genes_here, data_ref, 1 - core, second, other_ref, other_ref.shape[1])


def half_kernel(place_ref, half_ref, data_ref, scores_ref, gram_ref, update_ref):
    pull_update(half_ref, update_ref)
    gram_ref[...] = gram_of(update_ref[...])
    scores_ref[...] = score(lambda _: update_ref[...], data_ref, [place_ref[0]])


def next_kernel(
    genes_here,
    chunk,
    place_ref,
    scores_ref,
    gram_ref,
    rest_ref,
    data_ref,
    links_ref,
    degree_ref,
    other_ref,
    second_ref,
    worst_ref,
    update_ref,
    spread_ref,
):
    core = place_ref[0]
    groups = data_ref.shape[1]
    genes_total = genes_here * groups
    pull_update(rest_ref, update_ref)
    gram = (gram_ref[...] + gram_of(update_ref[...])) / genes_total
    inverse, amplified = inverse_factor(gram, spread_ref)
    worst_ref[...] = jnp.broadcast_to(amplified, worst_ref.shape)
    scores = scores_ref[...] + score(lambda _: update_ref[...], data_ref, [1 - core])
    scores = apply(inverse, scores) / math.sqrt(genes_total)
    second = diffuse(scores, links_ref[...], degree_ref[:1])
    second_ref[...] = second
    push_update(genes_here, data_ref, 1 - core, second, other_ref, chunk)
    if other_ref.shape[1] > chunk:
        share_second(core, 1 - core, second, other_ref, chunk, groups)


def exact_kernel(
    genes_here,
    chunk,
    place_ref,
    half_ref,
    rest_ref,
    data_ref,
    links_ref,
    degree_ref,
    other_ref,
    second_ref,
    worst_ref,
    update_ref,
    spread_ref,
):
    core = place_ref[0]
    groups = data_ref.shape[1]
    genes_total = genes_here * groups
    pull_both(core, half_ref, rest_ref, update_ref)
    inverse, amplified = normaliser(update_ref, genes_total, spread_ref)
    worst_ref[...] = jnp.broadcast_to(amplified, worst_ref.shape)
    scores = score(
        lambda group: apply(inverse, update_ref[group]).astype(jnp.bfloat16),
        data_ref,
        range(groups),
    ) / math.sqrt(genes_total)
    second = diffuse(scores, links_ref[...], degree_ref[:1])
    second_ref[...] = second
    push_update(genes_here, data_ref, 1 - core, second, other_ref, chunk)
    if other_ref.shape[1] > chunk:
        share_second(core, 1 - core, second, other_ref, chunk, groups)


def mine_kernel(genes_here, chunk, place_ref, data_ref, second_ref, mine_ref):
    core, second = place_ref[0], second_ref[...]
    push_update(genes_here, data_ref, core, second, mine_ref, chunk)
    if mine_ref.shape[1] > chunk:
        share_second(core, core, second, mine_ref, chunk, data_ref.shape[1])


def own_kernel(slots, place_ref, half_ref, arrived_ref, smoothed_ref, gram_ref, update_ref):
    pull_update(half_ref, update_ref)
    gram_ref[...] = gram_of(update_ref[...])
    order_shares(arrived_ref, half_ref.shape[1], smoothed_ref, 2, 2, slots)


def last_kernel(genes_here, place_ref, half_ref, rest_ref, gram_ref, *refs):
    *earlier, out_ref, good_ref, update_ref, spread_ref = refs
    core, own = place_ref[0], place_ref[1]
    groups = update_ref.shape[0]
    pull_both(core, half_ref, rest_ref, update_ref)
    gram = gram_ref[...] + gram_of(update_ref[1 - core])
    inverse, amplified = inverse_factor(gram / (genes_here * groups), spread_ref)
    good = amplified <= AMPLIFIED
    for worst_ref in earlier:
        good = good & (worst_ref[:, :1] <= AMPLIFIED)
    good_ref[0] = jnp.min(good.astype(jnp.int32))
    loadings = apply(inverse, update_ref[own].astype(jnp.float32))
    out_ref[...] = loadings[:, :genes_here]


def add_kernel(mine_ref, arrived_ref, out_ref):
    total = mine_ref[...].astype(jnp.float32) + arrived_ref[...].astype(jnp.float32)
    out_ref[...] = total.astype(out_ref.dtype)


def sum_kernel(chunks_ref, out_ref):
    parts = chunks_ref[:, : out_ref.shape[1]].astype(jnp.float32)
    total = jnp.sum(parts, axis=0).astype(out_ref.dtype)
    out_ref[...] = jnp.broadcast_to(total[None], out_ref.shape)


def like(array):
    return jax.ShapeDtypeStruct(array.shape, array.dtype)


def call(kernel, out_shape, scratch=(), scalars=0, arrays=0):
    in_specs = [pl.BlockSpec(memory_space=pltpu.SMEM)] * scalars
    in_specs += [pl.BlockSpec(memory_space=pltpu.VMEM)] * arrays
    return pl.pallas_call(
        kernel,
        out_shape=out_shape,
        in_specs=in_specs,
        out_specs=jax.tree.map(
            lambda leaf: pl.BlockSpec(memory_space=pltpu.VMEM if leaf.ndim > 1 else pltpu.SMEM),
            out_shape,
        ),
        scratch_shapes=list(scratch),
        compiler_params=pltpu.CompilerParams(vmem_limit_bytes=32 * 1024 * 1024),
    )


def by_cell(kept, data, start, link_dev, link_slot, link_weight):
    cores, groups = lax.axis_size("core"), lax.axis_size("genes")
    devices = lax.axis_size("chips") * cores
    parts = devices * groups
    blocks = parts // cores
    slots, neighbours = link_dev.shape
    genes_here, width = data.shape[1], start.shape[1]
    tile_cells = data.shape[0] // slots
    rows_of = tile_cells // parts
    rows = slots * rows_of
    padded = -(-genes_here // LANES) * LANES
    cells = devices * rows
    chunk = width // cores
    place = jnp.stack([lax.axis_index("core"), lax.axis_index("genes")]).astype(jnp.int32)

    def exchange(array):
        return lax.all_to_all(array, ("chips", "genes"), 0, 0, tiled=True)

    def swap(array):
        return lax.ppermute(array, "core", [(0, 1), (1, 0)])

    narrow = jnp.pad(start.astype(jnp.bfloat16).T, ((0, 0), (0, padded - genes_here)))
    starts = [narrow]
    for shift in range(1, groups):
        pairs = [(at, (at + shift) % groups) for at in range(groups)]
        starts.append(lax.ppermute(narrow, "genes", pairs))
    starts = jnp.stack(starts)
    moved = pl.pallas_call(
        functools.partial(regroup_kernel, rows_of),
        out_shape=jax.ShapeDtypeStruct((parts, rows, padded), jnp.bfloat16),
        in_specs=[pl.BlockSpec(memory_space=pl.ANY)] * 4,
        out_specs=pl.BlockSpec(memory_space=pl.ANY),
        scratch_shapes=[
            pltpu.VMEM((genes_here, slots * tile_cells), jnp.bfloat16),
            pltpu.VMEM((3, slots, neighbours), jnp.int32),
            pltpu.VMEM((parts, rows, padded), jnp.bfloat16),
            pltpu.SemaphoreType.DMA((slots,)),
            pltpu.SemaphoreType.DMA((3,)),
            pltpu.SemaphoreType.DMA((rows // max(16, rows_of),)),
        ],
        compiler_params=pltpu.CompilerParams(vmem_limit_bytes=60 * 1024 * 1024),
    )(data.T, link_dev, link_slot, link_weight)
    moved = lax.all_to_all(moved, ("chips", "core", "genes"), 0, 0, tiled=True)
    moved = moved.reshape(devices, groups, rows, padded)

    def cut(tall):
        return jax.ShapeDtypeStruct((blocks, tall, LANES), kept)

    def shape(*sizes, dtype=jnp.float32):
        return jax.ShapeDtypeStruct(sizes, dtype)

    part = pltpu.VMEM((width, padded), kept)
    update = pltpu.VMEM((groups, width, padded), kept)
    spread = pltpu.VMEM((2, 9, 8, 2 * width), jnp.float32)
    second_shape = shape(width, cells, dtype=jnp.bfloat16)
    worst = shape(width, LANES)
    earlier = []

    def reduce(other, second):
        swapped = swap(other)
        mine = call(
            functools.partial(mine_kernel, genes_here, chunk), like(other), scalars=1, arrays=2
        )(place, moved, second)
        return exchange(call(add_kernel, like(other), arrays=2)(mine, swapped))

    def gather(arrived):
        half = exchange(call(sum_kernel, cut(chunk), arrays=1)(arrived))
        return half, swap(half)

    other, second, links, degree = call(
        functools.partial(first_kernel, genes_here, slots),
        (cut(chunk), second_shape, shape(cells, cells, dtype=jnp.bfloat16), shape(8, cells)),
        scalars=1,
        arrays=2,
    )(place, moved, starts)
    arrived = reduce(other, second)
    for step in range(1, ITERS):
        share = cut(chunk + 16 if step == ITERS - 1 else chunk)
        half, rest = gather(arrived)
        if kept == jnp.float32:
            kernel, known, scratch = exact_kernel, (half, rest), update
        else:
            scores, gram = call(
                half_kernel,
                (shape(width, cells), shape(width, width)),
                (part,),
                scalars=1,
                arrays=2,
            )(place, half, moved)
            kernel, known, scratch = next_kernel, (scores, gram, rest), part
        other, second, amplified = call(
            functools.partial(kernel, genes_here, chunk),
            (share, second_shape, worst),
            (scratch, spread),
            scalars=1,
            arrays=3 + len(known),
        )(place, *known, moved, links, degree)
        earlier.append(amplified)
        arrived = reduce(other, second)
    half, rest = gather(arrived)
    smoothed, gram = call(
        functools.partial(own_kernel, slots),
        (
            shape(width // groups, slots * tile_cells, dtype=jnp.bfloat16),
            shape(width, width),
        ),
        (part,),
        scalars=1,
        arrays=2,
    )(place, half, arrived)
    loadings, good = call(
        functools.partial(last_kernel, genes_here),
        (shape(width, genes_here), shape(1, dtype=jnp.int32)),
        (update, spread),
        scalars=1,
        arrays=3 + len(earlier),
    )(place, half, rest, gram, *earlier)
    return loadings.T, smoothed, good[0] == 1


def by_condition(*arguments):
    loadings, smoothed, good = by_cell(jnp.bfloat16, *arguments)
    return lax.while_loop(
        lambda state: jnp.logical_not(state[2]),
        lambda _: by_cell(jnp.float32, *arguments)[:2] + (jnp.array(True),),
        (loadings, smoothed, good),
    )[:2]


def by_tile(data, start, link_dev, link_slot, link_weight):
    devices = lax.axis_size("cells")
    groups = lax.axis_size("genes")
    tiles_here, neighbours = link_dev.shape
    tile_cells = data.shape[0] // tiles_here
    genes_total = data.shape[1] * groups
    width = start.shape[1]
    part_width = width // groups
    capacity = max(2, 2 * tiles_here * neighbours // devices)
    slot_count = devices * capacity
    links = tiles_here * neighbours
    columns = part_width * tile_cells
    flat_dev = link_dev.reshape(links)
    flat_slot = link_slot.reshape(links)
    flat_weight = link_weight.reshape(links)
    dev_hits = (flat_dev[:, None] == jnp.arange(devices, dtype=jnp.int32)[None, :]).astype(
        jnp.int32
    )
    earlier = jnp.cumsum(dev_hits, axis=0) - dev_hits
    ranking = jnp.sum(earlier * dev_hits, axis=1)
    position = flat_dev * capacity + ranking
    placed = (position[:, None] == jnp.arange(slot_count, dtype=jnp.int32)[None, :]).astype(
        jnp.int32
    )
    wanted = jnp.sum(placed * (flat_slot + 1)[:, None], axis=0).reshape(devices, capacity)
    wanted_weight = jnp.sum(placed * flat_weight[:, None], axis=0).reshape(devices, capacity)
    asked_pair = (
        lax.all_to_all(wanted, "cells", split_axis=0, concat_axis=0, tiled=True),
        lax.all_to_all(wanted_weight, "cells", split_axis=0, concat_axis=0, tiled=True),
    )
    asked = asked_pair[0].reshape(slot_count)
    asked_weight = asked_pair[1].reshape(slot_count)
    tile_ids = jnp.arange(tiles_here, dtype=jnp.int32)
    serve_match = ((asked - 1)[:, None] == tile_ids[None, :]).astype(jnp.int32)
    serve = serve_match.astype(jnp.bfloat16)
    collect = (serve_match * asked_weight[:, None]).T.astype(jnp.bfloat16)
    placed_tiles = placed.reshape(tiles_here, neighbours, slot_count)
    link_matrix = jnp.sum(placed_tiles * link_weight[:, :, None], axis=1).astype(jnp.bfloat16)
    sender = jnp.sum(placed_tiles, axis=1).astype(jnp.bfloat16)
    degree = (self_weight + jnp.sum(link_weight, axis=1).astype(jnp.float32))[:, None]
    loadings = start
    smoothed = jnp.zeros((part_width, tiles_here * tile_cells), jnp.bfloat16)
    for step in range(ITERS):
        narrow = loadings.astype(jnp.bfloat16)
        partial_scores = lax.dot_general(
            narrow, data, (((0,), (1,)), ((), ())), preferred_element_type=jnp.float32
        )
        summed = lax.psum(partial_scores.astype(jnp.bfloat16), "genes").astype(jnp.float32)
        mine = lax.dynamic_slice_in_dim(summed, lax.axis_index("genes") * part_width, part_width, 0)
        scores = (mine / math.sqrt(genes_total)).astype(jnp.bfloat16)
        tiles = (
            scores.reshape(part_width, tiles_here, tile_cells)
            .transpose(1, 0, 2)
            .reshape(tiles_here, columns)
        )
        outgoing = jnp.dot(serve, tiles, preferred_element_type=jnp.float32).astype(jnp.bfloat16)
        linked = jnp.dot(
            link_matrix,
            lax.all_to_all(
                outgoing.reshape(devices, capacity, columns),
                "cells",
                split_axis=0,
                concat_axis=0,
                tiled=True,
            ).reshape(slot_count, -1),
            preferred_element_type=jnp.float32,
        )
        first = lax.optimization_barrier(
            ((self_weight * tiles.astype(jnp.float32) + linked) / degree).astype(jnp.bfloat16)
        )
        spread = lax.optimization_barrier(
            (self_weight * first.astype(jnp.float32) / degree).astype(jnp.bfloat16)
        )
        returning = lax.dot_general(
            sender, spread, (((0,), (0,)), ((), ())), preferred_element_type=jnp.float32
        ).astype(jnp.bfloat16)
        pushed = jnp.dot(
            collect,
            lax.all_to_all(
                returning.reshape(devices, capacity, columns),
                "cells",
                split_axis=0,
                concat_axis=0,
                tiled=True,
            ).reshape(slot_count, -1),
            preferred_element_type=jnp.float32,
        )
        second = (self_weight * spread.astype(jnp.float32) + pushed).astype(jnp.bfloat16)
        smoothed = (
            second.reshape(tiles_here, part_width, tile_cells)
            .transpose(1, 0, 2)
            .reshape(part_width, tiles_here * tile_cells)
        )
        update = lax.dot_general(
            data,
            lax.all_gather(smoothed, "genes", axis=0, tiled=True),
            (((0,), (1,)), ((), ())),
            preferred_element_type=jnp.float32,
        )
        update = lax.psum(update, "cells")
        gram_part = jnp.dot(
            update.T, update, precision=lax.Precision.HIGHEST, preferred_element_type=jnp.float32
        )
        gram = lax.psum(gram_part, "genes") / genes_total
        factor = jnp.linalg.cholesky(gram)
        loadings = lax.linalg.triangular_solve(
            factor, update, left_side=False, lower=True, transpose_a=True
        )
    return (loadings, smoothed)


def fits_by_cell(mesh, data, start, link_dev):
    groups, parts = mesh.shape["genes"], mesh.size
    slots, neighbours = link_dev.shape[0] * groups // parts, link_dev.shape[1]
    tile_cells = data.shape[0] // link_dev.shape[0]
    genes_here, width = data.shape[1] // groups, start.shape[1]
    padded = -(-genes_here // LANES) * LANES
    rows_of = tile_cells // parts
    rows = slots * rows_of
    return (
        mesh.shape["cells"] % 2 == 0
        and groups == 2
        and tile_cells % (8 * parts) == 0
        and neighbours <= rows_of
        and rows % 16 == 0
        and rows % max(16, rows_of) == 0
        and LANES % rows == 0
        and genes_here % 8 == 0
        and padded - genes_here >= 3
        and groups * padded // LANES == parts // 2
        and width % (32 * groups) == 0
        and width // groups // 16 * rows * 2 <= LANES
    )


def solution(mesh):
    chips = Mesh(
        mesh.devices.reshape(mesh.shape["cells"] // 2, 2, mesh.shape["genes"]),
        ("chips", "core", "genes"),
    )

    def program(data, start, link_dev, link_slot, link_weight):
        if fits_by_cell(mesh, data, start, link_dev):
            way, over, cells = by_condition, chips, ("chips", "core")
        else:
            way, over, cells = by_tile, mesh, "cells"
        return jax.shard_map(
            way,
            mesh=over,
            in_specs=(P(cells, "genes"), P("genes", None)) + (P(cells, None),) * 3,
            out_specs=(P("genes", None), P("genes", cells)),
            check_vma=False,
        )(data, start, link_dev, link_slot, link_weight)

    return program
```

```python
import functools
import math

import jax
import jax.numpy as jnp
from jax import lax
from jax.experimental import pallas as pl
from jax.experimental.pallas import tpu as pltpu
from jax.sharding import Mesh
from jax.sharding import PartitionSpec as P

ITERS = 3
LANES = 128
AMPLIFIED = 4.0

self_weight = 8.0
HIGHEST = lax.Precision.HIGHEST


def inverse_factor(gram, spread_ref):
    width = gram.shape[0]
    rows = lax.broadcasted_iota(jnp.int32, (width, width), 0)
    cols = lax.broadcasted_iota(jnp.int32, (width, width), 1)
    diagonal = jnp.where(rows == cols, gram, 0.0)
    down = lax.rsqrt(jnp.sum(diagonal, axis=1, keepdims=True))
    along = lax.rsqrt(jnp.sum(diagonal, axis=0, keepdims=True))
    scaled = gram * down * along
    state = jnp.concatenate([(rows == cols).astype(jnp.float32), scaled], axis=1)
    strips = [state[at : at + 8] for at in range(0, width, 8)]
    shape = strips[0].shape
    place = lax.broadcasted_iota(jnp.int32, shape, 0)
    done = []

    def column(of, lane):
        return jnp.broadcast_to(of[:, lane : lane + 1], shape)

    ahead = [column(strips[0], width + j) for j in range(8)]
    for panel in range(len(strips)):
        base = width + 8 * panel
        slot = spread_ref.at[panel % 2]
        for j in range(8):
            slot[j] = ahead[j]
        slot[16] = strips[panel]

        def row(of, i):
            return slot[of, pl.ds(i, 8, stride=0)]

        core = {(i, j): row(j, i) for j in range(8) for i in range(j, 8)}
        lines = [row(16, j) for j in range(8)]
        below = range(panel + 1, len(strips))
        rest = {(at, j): column(strips[at], base + j) for at in below for j in range(8)}
        if below:
            ahead = [column(strips[panel + 1], base + 8 + j) for j in range(8)]
        for j in range(0, 8, 2):
            a, b, c = core[j, j], core[j + 1, j], core[j + 1, j + 1]
            area = a * c - b * b
            over = 1.0 / a
            step = b * over
            later = a * (1.0 / area)
            left = {i: core[i, j + 1] - step * core[i, j] for i in range(j + 2, 8)}
            lines[j + 1] -= step * lines[j]
            core[j + 1, j + 1] = area * over
            for i in range(j + 2, 8):
                first, second = core[i, j] * over, left[i] * later
                for m in range(j + 2, i + 1):
                    core[i, m] -= first * core[m, j] + second * left[m]
                lines[i] -= first * lines[j] + second * lines[j + 1]
            for at in below:
                rest[at, j + 1] -= step * rest[at, j]
                first, second = rest[at, j] * over, rest[at, j + 1] * later
                for m in range(j + 2, 8):
                    rest[at, m] -= first * core[m, j] + second * left[m]
                if at == panel + 1:
                    slot[8 + j], slot[9 + j] = rest[at, j], rest[at, j + 1]
                    for i in range(8):
                        ahead[i] -= first * row(8 + j, i) + second * row(9 + j, i)
                strips[at] -= first * lines[j] + second * lines[j + 1]
        final = lines[0] * lax.rsqrt(core[0, 0])
        for j in range(1, 8):
            final = jnp.where(place == j, lines[j] * lax.rsqrt(core[j, j]), final)
        done.append(final)
    inverse = jnp.concatenate(done, axis=0)[:, :width]
    return inverse * along, jnp.sum(inverse * inverse, axis=1, keepdims=True)


def link_matrix(packed, tiles, neighbours, slots, rows_of):
    own_dev, own_slot, own_weight = packed[:, 0:1], packed[:, 1:2], packed[:, 2:3]
    target = own_dev * slots + own_slot
    lane = lax.broadcasted_iota(jnp.int32, (tiles * neighbours, tiles), 1).astype(jnp.float32)
    hits = jnp.where(lane == target, own_weight, 0.0)
    weights = jnp.sum(hits.reshape(tiles, neighbours, tiles), axis=1, keepdims=True)
    cells = tiles * rows_of
    tall = jnp.broadcast_to(weights, (tiles, rows_of, tiles)).reshape(cells, tiles)
    tile_of = lax.broadcasted_iota(jnp.int32, (cells, tiles), 0) // rows_of
    own = tile_of == lax.broadcasted_iota(jnp.int32, (cells, tiles), 1)
    tall = tall + jnp.where(own, self_weight, 0.0)
    expand = own.astype(jnp.bfloat16)
    full = lax.dot_general(
        tall.astype(jnp.bfloat16),
        expand,
        (((1,), (1,)), ((), ())),
        preferred_element_type=jnp.float32,
    )
    same = (
        lax.broadcasted_iota(jnp.int32, (cells, cells), 0) % rows_of
        == lax.broadcasted_iota(jnp.int32, (cells, cells), 1) % rows_of
    )
    full = jnp.where(same, full, 0.0).astype(jnp.bfloat16)
    ones = jnp.ones((8, cells), jnp.bfloat16)
    degree = lax.dot_general(
        ones, full, (((1,), (1,)), ((), ())), preferred_element_type=jnp.float32
    )
    return full, degree


def diffuse(scores, links, degree):
    scores = scores.astype(jnp.bfloat16)
    total = lax.dot_general(
        scores, links, (((1,), (1,)), ((), ())), preferred_element_type=jnp.float32
    )
    first = (total / degree).astype(jnp.bfloat16).astype(jnp.float32)
    spread = (self_weight * first / degree).astype(jnp.bfloat16)
    return jnp.dot(spread, links, preferred_element_type=jnp.float32).astype(jnp.bfloat16)


def block(data_ref, group):
    part = data_ref[:, group]
    return part.reshape(part.shape[0] * part.shape[1], part.shape[2])


def push_update(genes_here, data_ref, group, second, out_ref, chunk):
    update = jnp.dot(second, block(data_ref, group), preferred_element_type=jnp.float32)
    lane = lax.broadcasted_iota(jnp.int32, update.shape, 1)
    update = jnp.where(lane < genes_here, update, 0.0).astype(out_ref.dtype)
    halves = update.shape[0] // chunk
    for at in range(update.shape[1] // LANES):
        for half in range(halves):
            out_ref[at * halves + half, :chunk] = update[
                half * chunk : (half + 1) * chunk, at * LANES : (at + 1) * LANES
            ]


def pull_update(chunks_ref, update_ref):
    width, padded = update_ref.shape
    chunk = chunks_ref.shape[1]
    halves = width // chunk
    for at in range(padded // LANES):
        for half in range(halves):
            update_ref[
                half * chunk : (half + 1) * chunk, at * LANES : (at + 1) * LANES
            ] = chunks_ref[at * halves + half]


def pull_both(core, half_ref, rest_ref, update_ref):
    pull_update(half_ref, update_ref.at[core])
    pull_update(rest_ref, update_ref.at[1 - core])


def gram_of(update):
    return lax.dot_general(
        update,
        update,
        (((1,), (1,)), ((), ())),
        precision=HIGHEST if update.dtype == jnp.float32 else None,
        preferred_element_type=jnp.float32,
    )


def normaliser(update_ref, genes_total, spread_ref):
    gram = gram_of(update_ref[0])
    for group in range(1, update_ref.shape[0]):
        gram = gram + gram_of(update_ref[group])
    return inverse_factor(gram / genes_total, spread_ref)


def apply(inverse, array):
    return jnp.dot(inverse, array, precision=HIGHEST, preferred_element_type=jnp.float32)


def score(left, data_ref, groups):
    total = None
    for at, group in enumerate(groups):
        part = lax.dot_general(
            left(at),
            block(data_ref, group),
            (((1,), (1,)), ((), ())),
            preferred_element_type=jnp.float32,
        )
        total = part if total is None else total + part
    return total


def regroup_kernel(
    rows_of,
    data_any,
    dev_any,
    slot_any,
    weight_any,
    out_any,
    data_ref,
    link_ref,
    out_ref,
    data_sem,
    link_sem,
    out_sem,
):
    genes_here, cells = data_ref.shape
    parts, rows, padded = out_ref.shape
    slots, neighbours = link_ref.shape[1:]
    tile_cells = cells // slots
    share = max(16, rows_of)
    joined = share // rows_of
    whole = padded - LANES
    link_copies = [
        pltpu.make_async_copy(source, link_ref.at[at], link_sem.at[at])
        for at, source in enumerate((dev_any, slot_any, weight_any))
    ]
    tile_at = [pl.ds(tile * tile_cells, tile_cells) for tile in range(slots)]
    data_copies = [
        pltpu.make_async_copy(data_any.at[:, at], data_ref.at[:, at], data_sem.at[tile])
        for tile, at in enumerate(tile_at)
    ]
    for copy in data_copies[:1] + link_copies + data_copies[1:]:
        copy.start()

    def wide_links():
        spread = (
            lax.broadcasted_iota(jnp.int32, (neighbours, cells), 0)
            == lax.broadcasted_iota(jnp.int32, (neighbours, cells), 1) % rows_of
        ).astype(jnp.float32)
        tile = lax.broadcasted_iota(jnp.int32, (slots, cells), 0)
        own_tile = tile == lax.broadcasted_iota(jnp.int32, (slots, cells), 1) // tile_cells
        row = lax.broadcasted_iota(jnp.int32, (padded - genes_here, cells), 0)
        links = jnp.zeros((padded - genes_here, cells), jnp.float32)
        for at, copy in enumerate(link_copies):
            copy.wait()
            wide = jnp.dot(
                link_ref[at].astype(jnp.float32), spread, preferred_element_type=jnp.float32
            )
            wide = jnp.sum(jnp.where(own_tile, wide, 0.0), axis=0, keepdims=True)
            links = jnp.where(row == at, wide, links)
        return links

    def turned(part):
        return part.T.astype(jnp.float32).reshape(parts, rows_of, part.shape[0])

    out_copies, links = [], None
    for first in range(0, slots, joined):
        main, rest = [], []
        for tile in range(first, first + joined):
            data_copies[tile].wait()
            at = slice(tile * tile_cells, (tile + 1) * tile_cells)
            main.append(turned(data_ref[:whole, at]))
            links = wide_links() if links is None else links
            end = data_ref[whole:genes_here, at].astype(jnp.float32)
            end = jnp.concatenate([end, links[:, at]], axis=0)
            rest.append(turned(end.astype(jnp.bfloat16)))
        keep = slice(first * rows_of, first * rows_of + share)
        out_ref[:, keep, :whole] = jnp.concatenate(main, axis=1).astype(jnp.bfloat16)
        out_ref[:, keep, whole:] = jnp.concatenate(rest, axis=1).astype(jnp.bfloat16)
        keep = pl.ds(first * rows_of, share)
        out_copies.append(
            pltpu.make_async_copy(
                out_ref.at[:, keep], out_any.at[:, keep], out_sem.at[first // joined]
            )
        )
        out_copies[-1].start()
    for copy in out_copies:
        copy.wait()


def share_second(core, to, second, out_ref, chunk, groups):
    width, cells = second.shape
    blocks, tall = out_ref.shape[:2]
    cores = 2
    rows = cells * groups // (cores * blocks)
    tall = tall - chunk
    slabs = width // groups // tall
    lane = lax.broadcasted_iota(jnp.int32, (tall, LANES), 1) // rows
    chips = LANES // rows // cores
    for at in range(cells // LANES):
        wide = second[:, at * LANES : (at + 1) * LANES].astype(jnp.float32)
        for chip in range(chips):
            for group in range(groups):
                share = jnp.zeros((tall, LANES), jnp.float32)
                for slab in range(slabs):
                    first_row = (group * slabs + slab) * tall
                    place = core * slabs + slab
                    shift = (place - chip * cores - to) * rows
                    turned = pltpu.roll(
                        wide[first_row : first_row + tall],
                        lax.rem(shift + LANES, LANES),
                        1,
                    )
                    share = jnp.where(lane == place, turned, share)
                out_ref[(at * chips + chip) * groups + group, chunk:] = share.astype(
                    out_ref.dtype
                )


def order_shares(arrived_ref, chunk, out_ref, groups, cores, slots):
    part_width, cells = out_ref.shape
    blocks, tall = arrived_ref.shape[:2]
    tall = tall - chunk
    parts = blocks * cores
    rows_of = cells // (slots * parts)
    rows = slots * rows_of
    slabs = part_width // tall
    together = LANES // rows_of
    lane = lax.broadcasted_iota(jnp.int32, (tall, LANES), 1) // rows_of
    for slab in range(slabs):
        for slot in range(slots):
            for first in range(0, parts, together):
                whole = jnp.zeros((tall, LANES), jnp.float32)
                for at in range(together):
                    chip, rest = divmod(first + at, cores * groups)
                    core, group = divmod(rest, groups)
                    source = (core * slabs + slab) * rows + slot * rows_of
                    share = arrived_ref[chip * groups + group, chunk:].astype(jnp.float32)
                    turned = pltpu.roll(share, (at * rows_of - source) % LANES, 1)
                    whole = jnp.where(lane == at, turned, whole)
                to = (slot * parts + first) * rows_of
                out_ref[slab * tall : (slab + 1) * tall, to : to + LANES] = whole.astype(
                    jnp.bfloat16
                )


def first_kernel(
    genes_here,
    slots,
    place_ref,
    data_ref,
    start_ref,
    other_ref,
    second_ref,
    links_ref,
    degree_ref,
):
    devices, groups, rows, padded = data_ref.shape
    tiles = devices * slots
    core, own = place_ref[0], place_ref[1]
    packed = block(data_ref, 0)[:, padded - LANES :].astype(jnp.float32)
    offset = genes_here - (padded - LANES)
    links, degree = link_matrix(
        packed[:, offset : offset + 3], tiles, rows // slots, slots, rows // slots
    )
    links_ref[...] = links
    degree_ref[...] = degree
    order = [lax.rem(own + groups - shift, groups) for shift in range(groups)]
    scores = score(lambda shift: start_ref[shift], data_ref, order)
    scores = scores / math.sqrt(genes_here * groups)
    second = diffuse(scores, links, degree[:1])
    second_ref[...] = second
    push_update(genes_here, data_ref, 1 - core, second, other_ref, other_ref.shape[1])


def half_kernel(place_ref, half_ref, data_ref, scores_ref, gram_ref, update_ref):
    pull_update(half_ref, update_ref)
    gram_ref[...] = gram_of(update_ref[...])
    scores_ref[...] = score(lambda _: update_ref[...], data_ref, [place_ref[0]])


def next_kernel(
    genes_here,
    chunk,
    place_ref,
    scores_ref,
    gram_ref,
    rest_ref,
    data_ref,
    links_ref,
    degree_ref,
    other_ref,
    second_ref,
    worst_ref,
    update_ref,
    spread_ref,
):
    core = place_ref[0]
    groups = data_ref.shape[1]
    genes_total = genes_here * groups
    pull_update(rest_ref, update_ref)
    gram = (gram_ref[...] + gram_of(update_ref[...])) / genes_total
    inverse, amplified = inverse_factor(gram, spread_ref)
    worst_ref[...] = jnp.broadcast_to(amplified, worst_ref.shape)
    scores = scores_ref[...] + score(lambda _: update_ref[...], data_ref, [1 - core])
    scores = apply(inverse, scores) / math.sqrt(genes_total)
    second = diffuse(scores, links_ref[...], degree_ref[:1])
    second_ref[...] = second
    push_update(genes_here, data_ref, 1 - core, second, other_ref, chunk)
    if other_ref.shape[1] > chunk:
        share_second(core, 1 - core, second, other_ref, chunk, groups)


def exact_kernel(
    genes_here,
    chunk,
    place_ref,
    half_ref,
    rest_ref,
    data_ref,
    links_ref,
    degree_ref,
    other_ref,
    second_ref,
    worst_ref,
    update_ref,
    spread_ref,
):
    core = place_ref[0]
    groups = data_ref.shape[1]
    genes_total = genes_here * groups
    pull_both(core, half_ref, rest_ref, update_ref)
    inverse, amplified = normaliser(update_ref, genes_total, spread_ref)
    worst_ref[...] = jnp.broadcast_to(amplified, worst_ref.shape)
    scores = score(
        lambda group: apply(inverse, update_ref[group]).astype(jnp.bfloat16),
        data_ref,
        range(groups),
    ) / math.sqrt(genes_total)
    second = diffuse(scores, links_ref[...], degree_ref[:1])
    second_ref[...] = second
    push_update(genes_here, data_ref, 1 - core, second, other_ref, chunk)
    if other_ref.shape[1] > chunk:
        share_second(core, 1 - core, second, other_ref, chunk, groups)


def mine_kernel(genes_here, chunk, place_ref, data_ref, second_ref, mine_ref):
    core, second = place_ref[0], second_ref[...]
    push_update(genes_here, data_ref, core, second, mine_ref, chunk)
    if mine_ref.shape[1] > chunk:
        share_second(core, core, second, mine_ref, chunk, data_ref.shape[1])


def own_kernel(slots, place_ref, half_ref, arrived_ref, smoothed_ref, gram_ref, update_ref):
    pull_update(half_ref, update_ref)
    gram_ref[...] = gram_of(update_ref[...])
    order_shares(arrived_ref, half_ref.shape[1], smoothed_ref, 2, 2, slots)


def last_kernel(genes_here, place_ref, half_ref, rest_ref, gram_ref, *refs):
    *earlier, out_ref, good_ref, update_ref, spread_ref = refs
    core, own = place_ref[0], place_ref[1]
    groups = update_ref.shape[0]
    pull_both(core, half_ref, rest_ref, update_ref)
    gram = gram_ref[...] + gram_of(update_ref[1 - core])
    inverse, amplified = inverse_factor(gram / (genes_here * groups), spread_ref)
    good = amplified <= AMPLIFIED
    for worst_ref in earlier:
        good = good & (worst_ref[:, :1] <= AMPLIFIED)
    good_ref[0] = jnp.min(good.astype(jnp.int32))
    loadings = apply(inverse, update_ref[own].astype(jnp.float32))
    out_ref[...] = loadings[:, :genes_here]


def add_kernel(mine_ref, arrived_ref, out_ref):
    total = mine_ref[...].astype(jnp.float32) + arrived_ref[...].astype(jnp.float32)
    out_ref[...] = total.astype(out_ref.dtype)


def sum_kernel(chunks_ref, out_ref):
    parts = chunks_ref[:, : out_ref.shape[1]].astype(jnp.float32)
    total = jnp.sum(parts, axis=0).astype(out_ref.dtype)
    out_ref[...] = jnp.broadcast_to(total[None], out_ref.shape)


def like(array):
    return jax.ShapeDtypeStruct(array.shape, array.dtype)


def call(kernel, out_shape, scratch=(), scalars=0, arrays=0):
    in_specs = [pl.BlockSpec(memory_space=pltpu.SMEM)] * scalars
    in_specs += [pl.BlockSpec(memory_space=pltpu.VMEM)] * arrays
    return pl.pallas_call(
        kernel,
        out_shape=out_shape,
        in_specs=in_specs,
        out_specs=jax.tree.map(
            lambda leaf: pl.BlockSpec(memory_space=pltpu.VMEM if leaf.ndim > 1 else pltpu.SMEM),
            out_shape,
        ),
        scratch_shapes=list(scratch),
        compiler_params=pltpu.CompilerParams(vmem_limit_bytes=32 * 1024 * 1024),
    )


def by_cell(kept, data, start, link_dev, link_slot, link_weight):
    cores, groups = lax.axis_size("core"), lax.axis_size("genes")
    devices = lax.axis_size("chips") * cores
    parts = devices * groups
    blocks = parts // cores
    slots, neighbours = link_dev.shape
    genes_here, width = data.shape[1], start.shape[1]
    tile_cells = data.shape[0] // slots
    rows_of = tile_cells // parts
    rows = slots * rows_of
    padded = -(-genes_here // LANES) * LANES
    cells = devices * rows
    chunk = width // cores
    place = jnp.stack([lax.axis_index("core"), lax.axis_index("genes")]).astype(jnp.int32)

    def exchange(array):
        return lax.all_to_all(array, ("chips", "genes"), 0, 0, tiled=True)

    def swap(array):
        return lax.ppermute(array, "core", [(0, 1), (1, 0)])

    narrow = jnp.pad(start.astype(jnp.bfloat16).T, ((0, 0), (0, padded - genes_here)))
    starts = [narrow]
    for shift in range(1, groups):
        pairs = [(at, (at + shift) % groups) for at in range(groups)]
        starts.append(lax.ppermute(narrow, "genes", pairs))
    starts = jnp.stack(starts)
    moved = pl.pallas_call(
        functools.partial(regroup_kernel, rows_of),
        out_shape=jax.ShapeDtypeStruct((parts, rows, padded), jnp.bfloat16),
        in_specs=[pl.BlockSpec(memory_space=pl.ANY)] * 4,
        out_specs=pl.BlockSpec(memory_space=pl.ANY),
        scratch_shapes=[
            pltpu.VMEM((genes_here, slots * tile_cells), jnp.bfloat16),
            pltpu.VMEM((3, slots, neighbours), jnp.int32),
            pltpu.VMEM((parts, rows, padded), jnp.bfloat16),
            pltpu.SemaphoreType.DMA((slots,)),
            pltpu.SemaphoreType.DMA((3,)),
            pltpu.SemaphoreType.DMA((rows // max(16, rows_of),)),
        ],
        compiler_params=pltpu.CompilerParams(vmem_limit_bytes=60 * 1024 * 1024),
    )(data.T, link_dev, link_slot, link_weight)
    moved = lax.all_to_all(moved, ("chips", "core", "genes"), 0, 0, tiled=True)
    moved = moved.reshape(devices, groups, rows, padded)

    def cut(tall):
        return jax.ShapeDtypeStruct((blocks, tall, LANES), kept)

    def shape(*sizes, dtype=jnp.float32):
        return jax.ShapeDtypeStruct(sizes, dtype)

    part = pltpu.VMEM((width, padded), kept)
    update = pltpu.VMEM((groups, width, padded), kept)
    spread = pltpu.VMEM((2, 17, 8, 2 * width), jnp.float32)
    second_shape = shape(width, cells, dtype=jnp.bfloat16)
    worst = shape(width, LANES)
    earlier = []

    def reduce(other, second):
        swapped = swap(other)
        mine = call(
            functools.partial(mine_kernel, genes_here, chunk), like(other), scalars=1, arrays=2
        )(place, moved, second)
        return exchange(call(add_kernel, like(other), arrays=2)(mine, swapped))

    def gather(arrived):
        half = exchange(call(sum_kernel, cut(chunk), arrays=1)(arrived))
        return half, swap(half)

    other, second, links, degree = call(
        functools.partial(first_kernel, genes_here, slots),
        (cut(chunk), second_shape, shape(cells, cells, dtype=jnp.bfloat16), shape(8, cells)),
        scalars=1,
        arrays=2,
    )(place, moved, starts)
    arrived = reduce(other, second)
    for step in range(1, ITERS):
        share = cut(chunk + 16 if step == ITERS - 1 else chunk)
        half, rest = gather(arrived)
        if kept == jnp.float32:
            kernel, known, scratch = exact_kernel, (half, rest), update
        else:
            scores, gram = call(
                half_kernel,
                (shape(width, cells), shape(width, width)),
                (part,),
                scalars=1,
                arrays=2,
            )(place, half, moved)
            kernel, known, scratch = next_kernel, (scores, gram, rest), part
        other, second, amplified = call(
            functools.partial(kernel, genes_here, chunk),
            (share, second_shape, worst),
            (scratch, spread),
            scalars=1,
            arrays=3 + len(known),
        )(place, *known, moved, links, degree)
        earlier.append(amplified)
        arrived = reduce(other, second)
    half, rest = gather(arrived)
    smoothed, gram = call(
        functools.partial(own_kernel, slots),
        (
            shape(width // groups, slots * tile_cells, dtype=jnp.bfloat16),
            shape(width, width),
        ),
        (part,),
        scalars=1,
        arrays=2,
    )(place, half, arrived)
    loadings, good = call(
        functools.partial(last_kernel, genes_here),
        (shape(width, genes_here), shape(1, dtype=jnp.int32)),
        (update, spread),
        scalars=1,
        arrays=3 + len(earlier),
    )(place, half, rest, gram, *earlier)
    return loadings.T, smoothed, good[0] == 1


def by_condition(*arguments):
    loadings, smoothed, good = by_cell(jnp.bfloat16, *arguments)
    return lax.while_loop(
        lambda state: jnp.logical_not(state[2]),
        lambda _: by_cell(jnp.float32, *arguments)[:2] + (jnp.array(True),),
        (loadings, smoothed, good),
    )[:2]


def by_tile(data, start, link_dev, link_slot, link_weight):
    devices = lax.axis_size("cells")
    groups = lax.axis_size("genes")
    tiles_here, neighbours = link_dev.shape
    tile_cells = data.shape[0] // tiles_here
    genes_total = data.shape[1] * groups
    width = start.shape[1]
    part_width = width // groups
    capacity = max(2, 2 * tiles_here * neighbours // devices)
    slot_count = devices * capacity
    links = tiles_here * neighbours
    columns = part_width * tile_cells
    flat_dev = link_dev.reshape(links)
    flat_slot = link_slot.reshape(links)
    flat_weight = link_weight.reshape(links)
    dev_hits = (flat_dev[:, None] == jnp.arange(devices, dtype=jnp.int32)[None, :]).astype(
        jnp.int32
    )
    earlier = jnp.cumsum(dev_hits, axis=0) - dev_hits
    ranking = jnp.sum(earlier * dev_hits, axis=1)
    position = flat_dev * capacity + ranking
    placed = (position[:, None] == jnp.arange(slot_count, dtype=jnp.int32)[None, :]).astype(
        jnp.int32
    )
    wanted = jnp.sum(placed * (flat_slot + 1)[:, None], axis=0).reshape(devices, capacity)
    wanted_weight = jnp.sum(placed * flat_weight[:, None], axis=0).reshape(devices, capacity)
    asked_pair = (
        lax.all_to_all(wanted, "cells", split_axis=0, concat_axis=0, tiled=True),
        lax.all_to_all(wanted_weight, "cells", split_axis=0, concat_axis=0, tiled=True),
    )
    asked = asked_pair[0].reshape(slot_count)
    asked_weight = asked_pair[1].reshape(slot_count)
    tile_ids = jnp.arange(tiles_here, dtype=jnp.int32)
    serve_match = ((asked - 1)[:, None] == tile_ids[None, :]).astype(jnp.int32)
    serve = serve_match.astype(jnp.bfloat16)
    collect = (serve_match * asked_weight[:, None]).T.astype(jnp.bfloat16)
    placed_tiles = placed.reshape(tiles_here, neighbours, slot_count)
    link_matrix = jnp.sum(placed_tiles * link_weight[:, :, None], axis=1).astype(jnp.bfloat16)
    sender = jnp.sum(placed_tiles, axis=1).astype(jnp.bfloat16)
    degree = (self_weight + jnp.sum(link_weight, axis=1).astype(jnp.float32))[:, None]
    loadings = start
    smoothed = jnp.zeros((part_width, tiles_here * tile_cells), jnp.bfloat16)
    for step in range(ITERS):
        narrow = loadings.astype(jnp.bfloat16)
        partial_scores = lax.dot_general(
            narrow, data, (((0,), (1,)), ((), ())), preferred_element_type=jnp.float32
        )
        summed = lax.psum(partial_scores.astype(jnp.bfloat16), "genes").astype(jnp.float32)
        mine = lax.dynamic_slice_in_dim(summed, lax.axis_index("genes") * part_width, part_width, 0)
        scores = (mine / math.sqrt(genes_total)).astype(jnp.bfloat16)
        tiles = (
            scores.reshape(part_width, tiles_here, tile_cells)
            .transpose(1, 0, 2)
            .reshape(tiles_here, columns)
        )
        outgoing = jnp.dot(serve, tiles, preferred_element_type=jnp.float32).astype(jnp.bfloat16)
        linked = jnp.dot(
            link_matrix,
            lax.all_to_all(
                outgoing.reshape(devices, capacity, columns),
                "cells",
                split_axis=0,
                concat_axis=0,
                tiled=True,
            ).reshape(slot_count, -1),
            preferred_element_type=jnp.float32,
        )
        first = lax.optimization_barrier(
            ((self_weight * tiles.astype(jnp.float32) + linked) / degree).astype(jnp.bfloat16)
        )
        spread = lax.optimization_barrier(
            (self_weight * first.astype(jnp.float32) / degree).astype(jnp.bfloat16)
        )
        returning = lax.dot_general(
            sender, spread, (((0,), (0,)), ((), ())), preferred_element_type=jnp.float32
        ).astype(jnp.bfloat16)
        pushed = jnp.dot(
            collect,
            lax.all_to_all(
                returning.reshape(devices, capacity, columns),
                "cells",
                split_axis=0,
                concat_axis=0,
                tiled=True,
            ).reshape(slot_count, -1),
            preferred_element_type=jnp.float32,
        )
        second = (self_weight * spread.astype(jnp.float32) + pushed).astype(jnp.bfloat16)
        smoothed = (
            second.reshape(tiles_here, part_width, tile_cells)
            .transpose(1, 0, 2)
            .reshape(part_width, tiles_here * tile_cells)
        )
        update = lax.dot_general(
            data,
            lax.all_gather(smoothed, "genes", axis=0, tiled=True),
            (((0,), (1,)), ((), ())),
            preferred_element_type=jnp.float32,
        )
        update = lax.psum(update, "cells")
        gram_part = jnp.dot(
            update.T, update, precision=lax.Precision.HIGHEST, preferred_element_type=jnp.float32
        )
        gram = lax.psum(gram_part, "genes") / genes_total
        factor = jnp.linalg.cholesky(gram)
        loadings = lax.linalg.triangular_solve(
            factor, update, left_side=False, lower=True, transpose_a=True
        )
    return (loadings, smoothed)


def fits_by_cell(mesh, data, start, link_dev):
    groups, parts = mesh.shape["genes"], mesh.size
    slots, neighbours = link_dev.shape[0] * groups // parts, link_dev.shape[1]
    tile_cells = data.shape[0] // link_dev.shape[0]
    genes_here, width = data.shape[1] // groups, start.shape[1]
    padded = -(-genes_here // LANES) * LANES
    rows_of = tile_cells // parts
    rows = slots * rows_of
    return (
        mesh.shape["cells"] % 2 == 0
        and groups == 2
        and tile_cells % (8 * parts) == 0
        and neighbours <= rows_of
        and rows % 16 == 0
        and rows % max(16, rows_of) == 0
        and LANES % rows == 0
        and genes_here % 8 == 0
        and padded - genes_here >= 3
        and groups * padded // LANES == parts // 2
        and width % (32 * groups) == 0
        and width // groups // 16 * rows * 2 <= LANES
    )


def solution(mesh):
    chips = Mesh(
        mesh.devices.reshape(mesh.shape["cells"] // 2, 2, mesh.shape["genes"]),
        ("chips", "core", "genes"),
    )

    def program(data, start, link_dev, link_slot, link_weight):
        if fits_by_cell(mesh, data, start, link_dev):
            way, over, cells = by_condition, chips, ("chips", "core")
        else:
            way, over, cells = by_tile, mesh, "cells"
        return jax.shard_map(
            way,
            mesh=over,
            in_specs=(P(cells, "genes"), P("genes", None)) + (P(cells, None),) * 3,
            out_specs=(P("genes", None), P("genes", cells)),
            check_vma=False,
        )(data, start, link_dev, link_slot, link_weight)

    return program
```

```python
import functools
import math

import jax
import jax.numpy as jnp
from jax import lax
from jax.experimental import pallas as pl
from jax.experimental.pallas import tpu as pltpu
from jax.sharding import Mesh
from jax.sharding import PartitionSpec as P

ITERS = 3
LANES = 128
AMPLIFIED = 4.0

self_weight = 8.0
HIGHEST = lax.Precision.HIGHEST


def inverse_factor(gram, spread_ref):
    width = gram.shape[0]
    rows = lax.broadcasted_iota(jnp.int32, (width, width), 0)
    cols = lax.broadcasted_iota(jnp.int32, (width, width), 1)
    diagonal = jnp.where(rows == cols, gram, 0.0)
    down = lax.rsqrt(jnp.sum(diagonal, axis=1, keepdims=True))
    along = lax.rsqrt(jnp.sum(diagonal, axis=0, keepdims=True))
    scaled = gram * down * along
    state = jnp.concatenate([(rows == cols).astype(jnp.float32), scaled], axis=1)
    strips = [state[at : at + 8] for at in range(0, width, 8)]
    shape = strips[0].shape
    place = lax.broadcasted_iota(jnp.int32, shape, 0)
    done = []

    def column(of, lane):
        return jnp.broadcast_to(of[:, lane : lane + 1], shape)

    ahead = [column(strips[0], width + j) for j in range(8)]
    for panel in range(len(strips)):
        base = width + 8 * panel
        slot = spread_ref.at[panel % 2]
        for j in range(8):
            slot[j] = ahead[j]
        slot[16] = strips[panel]

        def row(of, i):
            return slot[of, pl.ds(i, 8, stride=0)]

        core = {(i, j): row(j, i) for j in range(8) for i in range(j, 8)}
        lines = [row(16, j) for j in range(8)]
        below = range(panel + 1, len(strips))
        rest = {(at, j): column(strips[at], base + j) for at in below for j in range(8)}
        if below:
            ahead = [column(strips[panel + 1], base + 8 + j) for j in range(8)]
        for j in range(0, 8, 2):
            a, b, c = core[j, j], core[j + 1, j], core[j + 1, j + 1]
            area = a * c - b * b
            over = 1.0 / a
            step = b * over
            later = a * (1.0 / area)
            left = {i: core[i, j + 1] - step * core[i, j] for i in range(j + 2, 8)}
            lines[j + 1] -= step * lines[j]
            core[j + 1, j + 1] = area * over
            for i in range(j + 2, 8):
                first, second = core[i, j] * over, left[i] * later
                for m in range(j + 2, i + 1):
                    core[i, m] -= first * core[m, j] + second * left[m]
                lines[i] -= first * lines[j] + second * lines[j + 1]
            for at in below:
                rest[at, j + 1] -= step * rest[at, j]
                first, second = rest[at, j] * over, rest[at, j + 1] * later
                for m in range(j + 2, 8):
                    rest[at, m] -= first * core[m, j] + second * left[m]
                if at == panel + 1:
                    slot[8 + j], slot[9 + j] = rest[at, j], rest[at, j + 1]
                    for i in range(8):
                        ahead[i] -= first * row(8 + j, i) + second * row(9 + j, i)
                strips[at] -= first * lines[j] + second * lines[j + 1]
        final = lines[0] * lax.rsqrt(core[0, 0])
        for j in range(1, 8):
            final = jnp.where(place == j, lines[j] * lax.rsqrt(core[j, j]), final)
        done.append(final)
    inverse = jnp.concatenate(done, axis=0)[:, :width]
    return inverse * along, jnp.sum(inverse * inverse, axis=1, keepdims=True)


def link_matrix(packed, tiles, neighbours, slots, rows_of):
    own_dev, own_slot, own_weight = packed[:, 0:1], packed[:, 1:2], packed[:, 2:3]
    target = own_dev * slots + own_slot
    lane = lax.broadcasted_iota(jnp.int32, (tiles * neighbours, tiles), 1).astype(jnp.float32)
    hits = jnp.where(lane == target, own_weight, 0.0)
    weights = jnp.sum(hits.reshape(tiles, neighbours, tiles), axis=1, keepdims=True)
    cells = tiles * rows_of
    tall = jnp.broadcast_to(weights, (tiles, rows_of, tiles)).reshape(cells, tiles)
    tile_of = lax.broadcasted_iota(jnp.int32, (cells, tiles), 0) // rows_of
    own = tile_of == lax.broadcasted_iota(jnp.int32, (cells, tiles), 1)
    tall = tall + jnp.where(own, self_weight, 0.0)
    expand = own.astype(jnp.bfloat16)
    full = lax.dot_general(
        tall.astype(jnp.bfloat16),
        expand,
        (((1,), (1,)), ((), ())),
        preferred_element_type=jnp.float32,
    )
    same = (
        lax.broadcasted_iota(jnp.int32, (cells, cells), 0) % rows_of
        == lax.broadcasted_iota(jnp.int32, (cells, cells), 1) % rows_of
    )
    full = jnp.where(same, full, 0.0).astype(jnp.bfloat16)
    ones = jnp.ones((8, cells), jnp.bfloat16)
    degree = lax.dot_general(
        ones, full, (((1,), (1,)), ((), ())), preferred_element_type=jnp.float32
    )
    return full, degree


def diffuse(scores, links, degree):
    scores = scores.astype(jnp.bfloat16)
    total = lax.dot_general(
        scores, links, (((1,), (1,)), ((), ())), preferred_element_type=jnp.float32
    )
    first = (total / degree).astype(jnp.bfloat16).astype(jnp.float32)
    spread = (self_weight * first / degree).astype(jnp.bfloat16)
    return jnp.dot(spread, links, preferred_element_type=jnp.float32).astype(jnp.bfloat16)


def block(data_ref, group):
    part = data_ref[:, group]
    return part.reshape(part.shape[0] * part.shape[1], part.shape[2])


def push_update(genes_here, data_ref, group, second, out_ref, chunk):
    update = jnp.dot(second, block(data_ref, group), preferred_element_type=jnp.float32)
    lane = lax.broadcasted_iota(jnp.int32, update.shape, 1)
    update = jnp.where(lane < genes_here, update, 0.0).astype(out_ref.dtype)
    halves = update.shape[0] // chunk
    for at in range(update.shape[1] // LANES):
        for half in range(halves):
            out_ref[at * halves + half, :chunk] = update[
                half * chunk : (half + 1) * chunk, at * LANES : (at + 1) * LANES
            ]


def pull_update(chunks_ref, update_ref):
    width, padded = update_ref.shape
    chunk = chunks_ref.shape[1]
    halves = width // chunk
    for at in range(padded // LANES):
        for half in range(halves):
            update_ref[
                half * chunk : (half + 1) * chunk, at * LANES : (at + 1) * LANES
            ] = chunks_ref[at * halves + half]


def pull_both(core, half_ref, rest_ref, update_ref):
    pull_update(half_ref, update_ref.at[core])
    pull_update(rest_ref, update_ref.at[1 - core])


def gram_of(update):
    return lax.dot_general(
        update,
        update,
        (((1,), (1,)), ((), ())),
        precision=HIGHEST if update.dtype == jnp.float32 else None,
        preferred_element_type=jnp.float32,
    )


def normaliser(update_ref, genes_total, spread_ref):
    gram = gram_of(update_ref[0])
    for group in range(1, update_ref.shape[0]):
        gram = gram + gram_of(update_ref[group])
    return inverse_factor(gram / genes_total, spread_ref)


def apply(inverse, array):
    return jnp.dot(inverse, array, precision=HIGHEST, preferred_element_type=jnp.float32)


def score(left, data_ref, groups):
    total = None
    for at, group in enumerate(groups):
        part = lax.dot_general(
            left(at),
            block(data_ref, group),
            (((1,), (1,)), ((), ())),
            preferred_element_type=jnp.float32,
        )
        total = part if total is None else total + part
    return total


def regroup_kernel(
    rows_of,
    data_any,
    dev_any,
    slot_any,
    weight_any,
    out_any,
    data_ref,
    link_ref,
    out_ref,
    data_sem,
    link_sem,
    out_sem,
):
    genes_here, cells = data_ref.shape
    parts, rows, padded = out_ref.shape
    slots, neighbours = link_ref.shape[1:]
    tile_cells = cells // slots
    share = max(16, rows_of)
    joined = share // rows_of
    whole = padded - LANES
    link_copies = [
        pltpu.make_async_copy(source, link_ref.at[at], link_sem.at[at])
        for at, source in enumerate((dev_any, slot_any, weight_any))
    ]
    tile_at = [pl.ds(tile * tile_cells, tile_cells) for tile in range(slots)]
    data_copies = [
        pltpu.make_async_copy(data_any.at[:, at], data_ref.at[:, at], data_sem.at[tile])
        for tile, at in enumerate(tile_at)
    ]
    for copy in data_copies[:1] + link_copies + data_copies[1:]:
        copy.start()

    def wide_links():
        spread = (
            lax.broadcasted_iota(jnp.int32, (neighbours, cells), 0)
            == lax.broadcasted_iota(jnp.int32, (neighbours, cells), 1) % rows_of
        ).astype(jnp.float32)
        tile = lax.broadcasted_iota(jnp.int32, (slots, cells), 0)
        own_tile = tile == lax.broadcasted_iota(jnp.int32, (slots, cells), 1) // tile_cells
        row = lax.broadcasted_iota(jnp.int32, (padded - genes_here, cells), 0)
        links = jnp.zeros((padded - genes_here, cells), jnp.float32)
        for copy in link_copies:
            copy.wait()
        known = jnp.concatenate([link_ref[at] for at in range(3)], axis=0).astype(jnp.float32)
        wide = jnp.dot(known, spread, preferred_element_type=jnp.float32)
        for at in range(3):
            one = jnp.where(own_tile, wide[at * slots : (at + 1) * slots], 0.0)
            links = jnp.where(row == at, jnp.sum(one, axis=0, keepdims=True), links)
        return links

    def turned(part):
        return part.T.astype(jnp.float32).reshape(parts, rows_of, part.shape[0])

    out_copies, links = [], None
    for first in range(0, slots, joined):
        main, rest = [], []
        for tile in range(first, first + joined):
            data_copies[tile].wait()
            at = slice(tile * tile_cells, (tile + 1) * tile_cells)
            main.append(turned(data_ref[:whole, at]))
            links = wide_links() if links is None else links
            end = data_ref[whole:genes_here, at].astype(jnp.float32)
            end = jnp.concatenate([end, links[:, at]], axis=0)
            rest.append(turned(end.astype(jnp.bfloat16)))
        keep = slice(first * rows_of, first * rows_of + share)
        out_ref[:, keep, :whole] = jnp.concatenate(main, axis=1).astype(jnp.bfloat16)
        out_ref[:, keep, whole:] = jnp.concatenate(rest, axis=1).astype(jnp.bfloat16)
        keep = pl.ds(first * rows_of, share)
        out_copies.append(
            pltpu.make_async_copy(
                out_ref.at[:, keep], out_any.at[:, keep], out_sem.at[first // joined]
            )
        )
        out_copies[-1].start()
    for copy in out_copies:
        copy.wait()


def share_second(core, to, second, out_ref, chunk, groups):
    width, cells = second.shape
    blocks, tall = out_ref.shape[:2]
    cores = 2
    rows = cells * groups // (cores * blocks)
    tall = tall - chunk
    slabs = width // groups // tall
    lane = lax.broadcasted_iota(jnp.int32, (tall, LANES), 1) // rows
    chips = LANES // rows // cores
    for at in range(cells // LANES):
        wide = second[:, at * LANES : (at + 1) * LANES].astype(jnp.float32)
        for chip in range(chips):
            for group in range(groups):
                share = jnp.zeros((tall, LANES), jnp.float32)
                for slab in range(slabs):
                    first_row = (group * slabs + slab) * tall
                    place = core * slabs + slab
                    shift = (place - chip * cores - to) * rows
                    turned = pltpu.roll(
                        wide[first_row : first_row + tall],
                        lax.rem(shift + LANES, LANES),
                        1,
                    )
                    share = jnp.where(lane == place, turned, share)
                out_ref[(at * chips + chip) * groups + group, chunk:] = share.astype(
                    out_ref.dtype
                )


def order_shares(arrived_ref, chunk, out_ref, groups, cores, slots):
    part_width, cells = out_ref.shape
    blocks, tall = arrived_ref.shape[:2]
    tall = tall - chunk
    parts = blocks * cores
    rows_of = cells // (slots * parts)
    rows = slots * rows_of
    slabs = part_width // tall
    together = LANES // rows_of
    lane = lax.broadcasted_iota(jnp.int32, (tall, LANES), 1) // rows_of
    for slab in range(slabs):
        for slot in range(slots):
            for first in range(0, parts, together):
                whole = jnp.zeros((tall, LANES), jnp.float32)
                for at in range(together):
                    chip, rest = divmod(first + at, cores * groups)
                    core, group = divmod(rest, groups)
                    source = (core * slabs + slab) * rows + slot * rows_of
                    share = arrived_ref[chip * groups + group, chunk:].astype(jnp.float32)
                    turned = pltpu.roll(share, (at * rows_of - source) % LANES, 1)
                    whole = jnp.where(lane == at, turned, whole)
                to = (slot * parts + first) * rows_of
                out_ref[slab * tall : (slab + 1) * tall, to : to + LANES] = whole.astype(
                    jnp.bfloat16
                )


def first_kernel(
    genes_here,
    slots,
    place_ref,
    data_ref,
    start_ref,
    other_ref,
    second_ref,
    links_ref,
    degree_ref,
):
    devices, groups, rows, padded = data_ref.shape
    tiles = devices * slots
    core, own = place_ref[0], place_ref[1]
    packed = block(data_ref, 0)[:, padded - LANES :].astype(jnp.float32)
    offset = genes_here - (padded - LANES)
    links, degree = link_matrix(
        packed[:, offset : offset + 3], tiles, rows // slots, slots, rows // slots
    )
    links_ref[...] = links
    degree_ref[...] = degree
    order = [lax.rem(own + groups - shift, groups) for shift in range(groups)]
    scores = score(lambda shift: start_ref[shift], data_ref, order)
    scores = scores / math.sqrt(genes_here * groups)
    second = diffuse(scores, links, degree[:1])
    second_ref[...] = second
    push_update(genes_here, data_ref, 1 - core, second, other_ref, other_ref.shape[1])


def half_kernel(place_ref, half_ref, data_ref, scores_ref, gram_ref, update_ref):
    pull_update(half_ref, update_ref)
    gram_ref[...] = gram_of(update_ref[...])
    scores_ref[...] = score(lambda _: update_ref[...], data_ref, [place_ref[0]])


def next_kernel(
    genes_here,
    chunk,
    place_ref,
    scores_ref,
    gram_ref,
    rest_ref,
    data_ref,
    links_ref,
    degree_ref,
    other_ref,
    second_ref,
    worst_ref,
    update_ref,
    spread_ref,
):
    core = place_ref[0]
    groups = data_ref.shape[1]
    genes_total = genes_here * groups
    pull_update(rest_ref, update_ref)
    gram = (gram_ref[...] + gram_of(update_ref[...])) / genes_total
    inverse, amplified = inverse_factor(gram, spread_ref)
    worst_ref[...] = jnp.broadcast_to(amplified, worst_ref.shape)
    scores = scores_ref[...] + score(lambda _: update_ref[...], data_ref, [1 - core])
    scores = apply(inverse, scores) / math.sqrt(genes_total)
    second = diffuse(scores, links_ref[...], degree_ref[:1])
    second_ref[...] = second
    push_update(genes_here, data_ref, 1 - core, second, other_ref, chunk)
    if other_ref.shape[1] > chunk:
        share_second(core, 1 - core, second, other_ref, chunk, groups)


def exact_kernel(
    genes_here,
    chunk,
    place_ref,
    half_ref,
    rest_ref,
    data_ref,
    links_ref,
    degree_ref,
    other_ref,
    second_ref,
    worst_ref,
    update_ref,
    spread_ref,
):
    core = place_ref[0]
    groups = data_ref.shape[1]
    genes_total = genes_here * groups
    pull_both(core, half_ref, rest_ref, update_ref)
    inverse, amplified = normaliser(update_ref, genes_total, spread_ref)
    worst_ref[...] = jnp.broadcast_to(amplified, worst_ref.shape)
    scores = score(
        lambda group: apply(inverse, update_ref[group]).astype(jnp.bfloat16),
        data_ref,
        range(groups),
    ) / math.sqrt(genes_total)
    second = diffuse(scores, links_ref[...], degree_ref[:1])
    second_ref[...] = second
    push_update(genes_here, data_ref, 1 - core, second, other_ref, chunk)
    if other_ref.shape[1] > chunk:
        share_second(core, 1 - core, second, other_ref, chunk, groups)


def mine_kernel(genes_here, chunk, place_ref, data_ref, second_ref, mine_ref):
    core, second = place_ref[0], second_ref[...]
    push_update(genes_here, data_ref, core, second, mine_ref, chunk)
    if mine_ref.shape[1] > chunk:
        share_second(core, core, second, mine_ref, chunk, data_ref.shape[1])


def own_kernel(slots, place_ref, half_ref, arrived_ref, smoothed_ref, gram_ref, update_ref):
    pull_update(half_ref, update_ref)
    gram_ref[...] = gram_of(update_ref[...])
    order_shares(arrived_ref, half_ref.shape[1], smoothed_ref, 2, 2, slots)


def last_kernel(genes_here, place_ref, half_ref, rest_ref, gram_ref, *refs):
    *earlier, out_ref, good_ref, update_ref, spread_ref = refs
    core, own = place_ref[0], place_ref[1]
    groups = update_ref.shape[0]
    pull_both(core, half_ref, rest_ref, update_ref)
    gram = gram_ref[...] + gram_of(update_ref[1 - core])
    inverse, amplified = inverse_factor(gram / (genes_here * groups), spread_ref)
    good = amplified <= AMPLIFIED
    for worst_ref in earlier:
        good = good & (worst_ref[:, :1] <= AMPLIFIED)
    good_ref[0] = jnp.min(good.astype(jnp.int32))
    mine = update_ref[own]
    if mine.dtype == jnp.float32:
        loadings = apply(inverse, mine)
    else:
        loadings = None
        for _ in range(3):
            piece = inverse.astype(jnp.bfloat16)
            inverse = inverse - piece.astype(jnp.float32)
            part = jnp.dot(piece, mine, preferred_element_type=jnp.float32)
            loadings = part if loadings is None else loadings + part
    out_ref[...] = loadings[:, :genes_here]


def add_kernel(mine_ref, arrived_ref, out_ref):
    total = mine_ref[...].astype(jnp.float32) + arrived_ref[...].astype(jnp.float32)
    out_ref[...] = total.astype(out_ref.dtype)


def sum_kernel(chunks_ref, out_ref):
    parts = chunks_ref[:, : out_ref.shape[1]].astype(jnp.float32)
    total = jnp.sum(parts, axis=0).astype(out_ref.dtype)
    out_ref[...] = jnp.broadcast_to(total[None], out_ref.shape)


def like(array):
    return jax.ShapeDtypeStruct(array.shape, array.dtype)


def call(kernel, out_shape, scratch=(), scalars=0, arrays=0):
    in_specs = [pl.BlockSpec(memory_space=pltpu.SMEM)] * scalars
    in_specs += [pl.BlockSpec(memory_space=pltpu.VMEM)] * arrays
    return pl.pallas_call(
        kernel,
        out_shape=out_shape,
        in_specs=in_specs,
        out_specs=jax.tree.map(
            lambda leaf: pl.BlockSpec(memory_space=pltpu.VMEM if leaf.ndim > 1 else pltpu.SMEM),
            out_shape,
        ),
        scratch_shapes=list(scratch),
        compiler_params=pltpu.CompilerParams(vmem_limit_bytes=32 * 1024 * 1024),
    )


def by_cell(kept, data, start, link_dev, link_slot, link_weight):
    cores, groups = lax.axis_size("core"), lax.axis_size("genes")
    devices = lax.axis_size("chips") * cores
    parts = devices * groups
    blocks = parts // cores
    slots, neighbours = link_dev.shape
    genes_here, width = data.shape[1], start.shape[1]
    tile_cells = data.shape[0] // slots
    rows_of = tile_cells // parts
    rows = slots * rows_of
    padded = -(-genes_here // LANES) * LANES
    cells = devices * rows
    chunk = width // cores
    place = jnp.stack([lax.axis_index("core"), lax.axis_index("genes")]).astype(jnp.int32)

    def exchange(array):
        return lax.all_to_all(array, ("chips", "genes"), 0, 0, tiled=True)

    def swap(array):
        return lax.ppermute(array, "core", [(0, 1), (1, 0)])

    narrow = jnp.pad(start.astype(jnp.bfloat16).T, ((0, 0), (0, padded - genes_here)))
    starts = [narrow]
    for shift in range(1, groups):
        pairs = [(at, (at + shift) % groups) for at in range(groups)]
        starts.append(lax.ppermute(narrow, "genes", pairs))
    starts = jnp.stack(starts)
    moved = pl.pallas_call(
        functools.partial(regroup_kernel, rows_of),
        out_shape=jax.ShapeDtypeStruct((parts, rows, padded), jnp.bfloat16),
        in_specs=[pl.BlockSpec(memory_space=pl.ANY)] * 4,
        out_specs=pl.BlockSpec(memory_space=pl.ANY),
        scratch_shapes=[
            pltpu.VMEM((genes_here, slots * tile_cells), jnp.bfloat16),
            pltpu.VMEM((3, slots, neighbours), jnp.int32),
            pltpu.VMEM((parts, rows, padded), jnp.bfloat16),
            pltpu.SemaphoreType.DMA((slots,)),
            pltpu.SemaphoreType.DMA((3,)),
            pltpu.SemaphoreType.DMA((rows // max(16, rows_of),)),
        ],
        compiler_params=pltpu.CompilerParams(vmem_limit_bytes=60 * 1024 * 1024),
    )(data.T, link_dev, link_slot, link_weight)
    moved = lax.all_to_all(moved, ("chips", "core", "genes"), 0, 0, tiled=True)
    moved = moved.reshape(devices, groups, rows, padded)

    def cut(tall):
        return jax.ShapeDtypeStruct((blocks, tall, LANES), kept)

    def shape(*sizes, dtype=jnp.float32):
        return jax.ShapeDtypeStruct(sizes, dtype)

    part = pltpu.VMEM((width, padded), kept)
    update = pltpu.VMEM((groups, width, padded), kept)
    spread = pltpu.VMEM((2, 17, 8, 2 * width), jnp.float32)
    second_shape = shape(width, cells, dtype=jnp.bfloat16)
    worst = shape(width, LANES)
    earlier = []

    def reduce(other, second):
        swapped = swap(other)
        mine = call(
            functools.partial(mine_kernel, genes_here, chunk), like(other), scalars=1, arrays=2
        )(place, moved, second)
        return exchange(call(add_kernel, like(other), arrays=2)(mine, swapped))

    def gather(arrived):
        half = exchange(call(sum_kernel, cut(chunk), arrays=1)(arrived))
        return half, swap(half)

    other, second, links, degree = call(
        functools.partial(first_kernel, genes_here, slots),
        (cut(chunk), second_shape, shape(cells, cells, dtype=jnp.bfloat16), shape(8, cells)),
        scalars=1,
        arrays=2,
    )(place, moved, starts)
    arrived = reduce(other, second)
    for step in range(1, ITERS):
        share = cut(chunk + 16 if step == ITERS - 1 else chunk)
        half, rest = gather(arrived)
        if kept == jnp.float32:
            kernel, known, scratch = exact_kernel, (half, rest), update
        else:
            scores, gram = call(
                half_kernel,
                (shape(width, cells), shape(width, width)),
                (part,),
                scalars=1,
                arrays=2,
            )(place, half, moved)
            kernel, known, scratch = next_kernel, (scores, gram, rest), part
        other, second, amplified = call(
            functools.partial(kernel, genes_here, chunk),
            (share, second_shape, worst),
            (scratch, spread),
            scalars=1,
            arrays=3 + len(known),
        )(place, *known, moved, links, degree)
        earlier.append(amplified)
        arrived = reduce(other, second)
    half, rest = gather(arrived)
    smoothed, gram = call(
        functools.partial(own_kernel, slots),
        (
            shape(width // groups, slots * tile_cells, dtype=jnp.bfloat16),
            shape(width, width),
        ),
        (part,),
        scalars=1,
        arrays=2,
    )(place, half, arrived)
    loadings, good = call(
        functools.partial(last_kernel, genes_here),
        (shape(width, genes_here), shape(1, dtype=jnp.int32)),
        (update, spread),
        scalars=1,
        arrays=3 + len(earlier),
    )(place, half, rest, gram, *earlier)
    return loadings.T, smoothed, good[0] == 1


def by_condition(*arguments):
    loadings, smoothed, good = by_cell(jnp.bfloat16, *arguments)
    return lax.while_loop(
        lambda state: jnp.logical_not(state[2]),
        lambda _: by_cell(jnp.float32, *arguments)[:2] + (jnp.array(True),),
        (loadings, smoothed, good),
    )[:2]


def by_tile(data, start, link_dev, link_slot, link_weight):
    devices = lax.axis_size("cells")
    groups = lax.axis_size("genes")
    tiles_here, neighbours = link_dev.shape
    tile_cells = data.shape[0] // tiles_here
    genes_total = data.shape[1] * groups
    width = start.shape[1]
    part_width = width // groups
    capacity = max(2, 2 * tiles_here * neighbours // devices)
    slot_count = devices * capacity
    links = tiles_here * neighbours
    columns = part_width * tile_cells
    flat_dev = link_dev.reshape(links)
    flat_slot = link_slot.reshape(links)
    flat_weight = link_weight.reshape(links)
    dev_hits = (flat_dev[:, None] == jnp.arange(devices, dtype=jnp.int32)[None, :]).astype(
        jnp.int32
    )
    earlier = jnp.cumsum(dev_hits, axis=0) - dev_hits
    ranking = jnp.sum(earlier * dev_hits, axis=1)
    position = flat_dev * capacity + ranking
    placed = (position[:, None] == jnp.arange(slot_count, dtype=jnp.int32)[None, :]).astype(
        jnp.int32
    )
    wanted = jnp.sum(placed * (flat_slot + 1)[:, None], axis=0).reshape(devices, capacity)
    wanted_weight = jnp.sum(placed * flat_weight[:, None], axis=0).reshape(devices, capacity)
    asked_pair = (
        lax.all_to_all(wanted, "cells", split_axis=0, concat_axis=0, tiled=True),
        lax.all_to_all(wanted_weight, "cells", split_axis=0, concat_axis=0, tiled=True),
    )
    asked = asked_pair[0].reshape(slot_count)
    asked_weight = asked_pair[1].reshape(slot_count)
    tile_ids = jnp.arange(tiles_here, dtype=jnp.int32)
    serve_match = ((asked - 1)[:, None] == tile_ids[None, :]).astype(jnp.int32)
    serve = serve_match.astype(jnp.bfloat16)
    collect = (serve_match * asked_weight[:, None]).T.astype(jnp.bfloat16)
    placed_tiles = placed.reshape(tiles_here, neighbours, slot_count)
    link_matrix = jnp.sum(placed_tiles * link_weight[:, :, None], axis=1).astype(jnp.bfloat16)
    sender = jnp.sum(placed_tiles, axis=1).astype(jnp.bfloat16)
    degree = (self_weight + jnp.sum(link_weight, axis=1).astype(jnp.float32))[:, None]
    loadings = start
    smoothed = jnp.zeros((part_width, tiles_here * tile_cells), jnp.bfloat16)
    for step in range(ITERS):
        narrow = loadings.astype(jnp.bfloat16)
        partial_scores = lax.dot_general(
            narrow, data, (((0,), (1,)), ((), ())), preferred_element_type=jnp.float32
        )
        summed = lax.psum(partial_scores.astype(jnp.bfloat16), "genes").astype(jnp.float32)
        mine = lax.dynamic_slice_in_dim(summed, lax.axis_index("genes") * part_width, part_width, 0)
        scores = (mine / math.sqrt(genes_total)).astype(jnp.bfloat16)
        tiles = (
            scores.reshape(part_width, tiles_here, tile_cells)
            .transpose(1, 0, 2)
            .reshape(tiles_here, columns)
        )
        outgoing = jnp.dot(serve, tiles, preferred_element_type=jnp.float32).astype(jnp.bfloat16)
        linked = jnp.dot(
            link_matrix,
            lax.all_to_all(
                outgoing.reshape(devices, capacity, columns),
                "cells",
                split_axis=0,
                concat_axis=0,
                tiled=True,
            ).reshape(slot_count, -1),
            preferred_element_type=jnp.float32,
        )
        first = lax.optimization_barrier(
            ((self_weight * tiles.astype(jnp.float32) + linked) / degree).astype(jnp.bfloat16)
        )
        spread = lax.optimization_barrier(
            (self_weight * first.astype(jnp.float32) / degree).astype(jnp.bfloat16)
        )
        returning = lax.dot_general(
            sender, spread, (((0,), (0,)), ((), ())), preferred_element_type=jnp.float32
        ).astype(jnp.bfloat16)
        pushed = jnp.dot(
            collect,
            lax.all_to_all(
                returning.reshape(devices, capacity, columns),
                "cells",
                split_axis=0,
                concat_axis=0,
                tiled=True,
            ).reshape(slot_count, -1),
            preferred_element_type=jnp.float32,
        )
        second = (self_weight * spread.astype(jnp.float32) + pushed).astype(jnp.bfloat16)
        smoothed = (
            second.reshape(tiles_here, part_width, tile_cells)
            .transpose(1, 0, 2)
            .reshape(part_width, tiles_here * tile_cells)
        )
        update = lax.dot_general(
            data,
            lax.all_gather(smoothed, "genes", axis=0, tiled=True),
            (((0,), (1,)), ((), ())),
            preferred_element_type=jnp.float32,
        )
        update = lax.psum(update, "cells")
        gram_part = jnp.dot(
            update.T, update, precision=lax.Precision.HIGHEST, preferred_element_type=jnp.float32
        )
        gram = lax.psum(gram_part, "genes") / genes_total
        factor = jnp.linalg.cholesky(gram)
        loadings = lax.linalg.triangular_solve(
            factor, update, left_side=False, lower=True, transpose_a=True
        )
    return (loadings, smoothed)


def fits_by_cell(mesh, data, start, link_dev):
    groups, parts = mesh.shape["genes"], mesh.size
    slots, neighbours = link_dev.shape[0] * groups // parts, link_dev.shape[1]
    tile_cells = data.shape[0] // link_dev.shape[0]
    genes_here, width = data.shape[1] // groups, start.shape[1]
    padded = -(-genes_here // LANES) * LANES
    rows_of = tile_cells // parts
    rows = slots * rows_of
    return (
        mesh.shape["cells"] % 2 == 0
        and groups == 2
        and tile_cells % (8 * parts) == 0
        and neighbours <= rows_of
        and rows % 16 == 0
        and rows % max(16, rows_of) == 0
        and LANES % rows == 0
        and genes_here % 8 == 0
        and padded - genes_here >= 3
        and groups * padded // LANES == parts // 2
        and width % (32 * groups) == 0
        and width // groups // 16 * rows * 2 <= LANES
    )


def solution(mesh):
    chips = Mesh(
        mesh.devices.reshape(mesh.shape["cells"] // 2, 2, mesh.shape["genes"]),
        ("chips", "core", "genes"),
    )

    def program(data, start, link_dev, link_slot, link_weight):
        if fits_by_cell(mesh, data, start, link_dev):
            way, over, cells = by_condition, chips, ("chips", "core")
        else:
            way, over, cells = by_tile, mesh, "cells"
        return jax.shard_map(
            way,
            mesh=over,
            in_specs=(P(cells, "genes"), P("genes", None)) + (P(cells, None),) * 3,
            out_specs=(P("genes", None), P("genes", cells)),
            check_vma=False,
        )(data, start, link_dev, link_slot, link_weight)

    return program
```
